32 devices in a mesh: rows: 16 (over z, x, core), feat: 2 (over y).
Axes of the slice: x: 2, y: 2, z: 4, core: 2. Of those that a mesh axis runs over, the one named last changes fastest.
Arguments:
- features: bfloat16 [256, 32768], P('feat', 'rows'), may hold values from -8 to 8
- adjacency: bfloat16 [256, 12, 128, 128], P('rows'), may hold values from 0 to 1, as said below
- tile_cols: int32 [256, 12], P('rows'), may hold values from 0 to 255, as said below
- self_weight: bfloat16 [256, 256], P('feat'), may hold values from -0.375 to 0.375
- neigh_weight: bfloat16 [256, 256], P('feat'), may hold values from -0.375 to 0.375
- bias_vector: float32 [256], P('feat'), may hold values from -3 to 3
- grad_output: bfloat16 [256, 32768], P('feat', 'rows'), may hold values from -8 to 8
Outputs:
- activation: bfloat16 [256, 32768], P('feat', 'rows')
- grad_features: bfloat16 [256, 32768], P('feat', 'rows')
- grad_self: float32 [256, 256], P('feat')
- grad_neigh: float32 [256, 256], P('feat')
- grad_bias: float32 [256], P('feat')
The draws below stay inside these ranges and needn't reach their ends.
Inputs may be any that keep to these rules, and one draw needn't show every extreme that they name: `tile_cols`: row blocks b with the same b // 16 form one group; among the 192 tiles of one group, at most 12 have source blocks c with the same c // 16, and in every group some c // 16 is reached by exactly 12 tiles. `adjacency`: the first tile of every row block has all its diagonal entries at 0.5 or more.
All inputs are finite; a program needn't handle non-finite values.
Results may differ from the reference program's by a relative error of at most 0.0034.
Values may be sent and summed in bfloat16 or wider, within the bound.
No kernel may reach another device: no remote copies, remote signals or barrier semaphores. Data moves between devices by JAX's collectives and lax.ppermute only.
A program may use at most 128 MiB of HBM per device.

```python
import jax
import jax.numpy as jnp
from jax import lax

HID = 256
TILE = 128
TPB = 12
CAP = 12
NB = 16
BLOCKS = 256
NODES = 32768


def block_field(key):
    first, second = jax.random.split(key)
    noise = jax.random.normal(first, (HID, NODES), jnp.float32)
    shared = jax.random.normal(second, (HID, BLOCKS), jnp.float32)
    shared = jnp.repeat(shared, TILE, axis=1)
    return jnp.clip(noise + shared, -8.0, 8.0)


def draw_features(key, part):
    key = jax.random.fold_in(key, 11)
    return block_field(key).astype(jnp.bfloat16)


def draw_grad_output(key, part):
    key = jax.random.fold_in(key, 23)
    return block_field(key).astype(jnp.bfloat16)


def draw_adjacency(key, part):
    key = jax.random.fold_in(key, 37)
    first, second, third = jax.random.split(key, 3)
    shape = (BLOCKS, TPB, TILE, TILE)
    present = jax.random.uniform(first, shape, jnp.float32) < 0.04
    weights = jnp.exp(jax.random.uniform(second, shape, jnp.float32, jnp.log(0.05), 0.0))
    tiles = jnp.where(present, weights, 0.0)
    diagonal = 0.5 + 0.5 * jax.random.uniform(third, (BLOCKS, TILE), jnp.float32)
    eye_mask = jnp.eye(TILE, dtype=jnp.float32)
    first_tile = tiles[:, 0] * (1.0 - eye_mask)[None] + diagonal[:, :, None] * eye_mask[None]
    return tiles.at[:, 0].set(first_tile).astype(jnp.bfloat16)


def draw_tile_cols(key, part):
    key = jax.random.fold_in(key, 53)
    groups = BLOCKS // NB
    count = NB * TPB

    def one_group(group_key):
        keys = jax.random.split(group_key, 4)
        busiest = jax.random.randint(keys[0], (), 0, groups)
        slots = jax.random.permutation(keys[1], (groups - 1) * CAP)[:count - CAP]
        others = (busiest + 1 + slots // CAP) % groups
        owners = jnp.concatenate([jnp.full((CAP,), busiest, jnp.int32), others.astype(jnp.int32)])
        order = jax.random.permutation(keys[2], count)
        owners = owners[order]
        local = jax.random.randint(keys[3], (count,), 0, NB)
        return (owners * NB + local).astype(jnp.int32)
    group_keys = jax.random.split(key, groups)
    return jax.vmap(one_group)(group_keys).reshape(BLOCKS, TPB).astype(jnp.int32)


def level_of(stream_key, extent, pieces, low, top_value):
    def one(position, blocks):
        draws = jax.random.uniform(jax.random.fold_in(jax.random.fold_in(stream_key, 6), position), (blocks,), jnp.float32, low / len(pieces), top_value / len(pieces))
        return jnp.repeat(jnp.exp(draws), extent[position] // blocks).reshape((-1,) + (1,) * (len(extent) - position - 1))

    gain = one(*pieces[0])
    for cut in pieces[1:]:
        gain = gain * one(*cut)
    return gain


def gaussian(own_key, shape, width, limit, cuts=(), held_as=jnp.bfloat16):
    values = width * jax.random.normal(own_key, shape, jnp.float32)
    if cuts:
        values = values * level_of(own_key, shape, cuts, -0.22, 0.18)
    return jnp.clip(values, -limit, limit).astype(held_as)


def setup_inputs(seed: int = 0) -> dict:
    key_list = jax.random.split(jax.random.key(seed), 8)
    features = draw_features(jax.random.fold_in(key_list[7], 71), 0)
    adjacency = draw_adjacency(jax.random.fold_in(key_list[7], 71), 0)
    tile_cols = draw_tile_cols(jax.random.fold_in(key_list[7], 71), 0)
    self_weight = gaussian(key_list[3], (HID, HID), HID ** -0.5, 0.375, ((0, 2),))
    neigh_weight = gaussian(key_list[4], (HID, HID), HID ** -0.5, 0.375, ((0, 2),))
    bias_vector = gaussian(key_list[5], (HID,), 0.5, 3.0, ((0, 2),), jnp.float32)
    grad_output = draw_grad_output(jax.random.fold_in(key_list[7], 71), 0)
    return {"features": features, "adjacency": adjacency, "tile_cols": tile_cols, "self_weight": self_weight, "neigh_weight": neigh_weight, "bias_vector": bias_vector, "grad_output": grad_output}


def reference(features, adjacency, tile_cols, self_weight, neigh_weight, bias_vector, grad_output):
    degree = jnp.sum(adjacency.astype(jnp.float32), axis=(1, 3))
    inverse = 1.0 / degree
    blocked = features.reshape(HID, BLOCKS, TILE)

    def aggregate_block(pair):
        block_tiles, columns = pair
        picked = jnp.take(blocked, columns, axis=1).astype(jnp.float32)
        return jnp.einsum("htj,tij->hi", picked, block_tiles.astype(jnp.float32))

    summed = lax.map(aggregate_block, (adjacency, tile_cols))
    summed = summed * inverse[:, None, :]
    aggregate = jnp.transpose(summed, (1, 0, 2)).reshape(HID, NODES).astype(jnp.bfloat16)
    preact = jnp.dot(self_weight.T, features, preferred_element_type=jnp.float32)
    preact = preact + jnp.dot(neigh_weight.T, aggregate, preferred_element_type=jnp.float32)
    preact = preact + bias_vector[:, None]
    activation = jnp.where(preact > 0, preact, jnp.expm1(jnp.minimum(preact, 0.0))).astype(jnp.bfloat16)
    slopes = jnp.where(preact > 0, 1.0, jnp.exp(jnp.minimum(preact, 0.0)))
    grad_pre = (grad_output.astype(jnp.float32) * slopes).astype(jnp.bfloat16)
    grad_self = jnp.dot(features, grad_pre.T, preferred_element_type=jnp.float32)
    grad_neigh = jnp.dot(aggregate, grad_pre.T, preferred_element_type=jnp.float32)
    grad_bias = jnp.sum(grad_pre.astype(jnp.float32), axis=1)
    inverse_flat = inverse.reshape(NODES)
    scaled = (jnp.dot(neigh_weight, grad_pre, preferred_element_type=jnp.float32) * inverse_flat[None, :]).astype(jnp.bfloat16)
    scaled_blocks = jnp.transpose(scaled.reshape(HID, BLOCKS, TILE), (1, 0, 2))

    def spread(total, item):
        block_tiles, columns, rows_part = item
        terms = jnp.einsum("hi,tij->htj", rows_part.astype(jnp.float32), block_tiles.astype(jnp.float32))
        return total.at[:, columns, :].add(terms), None

    start_sum = jnp.zeros((HID, BLOCKS, TILE), jnp.float32)
    backward_sum, unused = lax.scan(spread, start_sum, (adjacency, tile_cols, scaled_blocks))
    self_term = jnp.dot(self_weight, grad_pre, preferred_element_type=jnp.float32)
    grad_features = (self_term + backward_sum.reshape(HID, NODES)).astype(jnp.bfloat16)
    return activation, grad_features, grad_self, grad_neigh, grad_bias
```

```python
import functools

import jax
import jax.numpy as jnp
from jax import lax
from jax.experimental import pallas as pl
from jax.experimental.pallas import tpu as pltpu
from jax.sharding import PartitionSpec as P

CAP = 12
VMEM_BYTES = 40 * 1024 * 1024
HBM = pl.BlockSpec(memory_space=pl.ANY)
VMEM = pl.BlockSpec(memory_space=pltpu.VMEM)
SMEM = pl.BlockSpec(memory_space=pltpu.SMEM)


def params():
    return pltpu.CompilerParams(vmem_limit_bytes=VMEM_BYTES)


def cost(flops, moved):
    return pl.CostEstimate(flops=flops, bytes_accessed=moved, transcendentals=0)


def ring_pairs(rows, step):
    levels, chips = rows // 4, rows // 2
    order = [2 * z for z in range(levels)] + [2 * z + 1 for z in reversed(range(levels))]
    return [
        (2 * order[p] + core, 2 * order[(p + step) % chips] + core)
        for p in range(chips)
        for core in range(2)
    ]


def ring_row(row, offset, rows):
    levels, chips = rows // 4, rows // 2
    z, x, core = row // 4, (row // 2) % 2, row % 2
    target = ((z if x == 0 else chips - 1 - z) + offset) % chips
    chip = 2 * target if target < levels else 2 * (chips - 1 - target) + 1
    return 2 * chip + core


def places(spot, row, wanted, rows):
    table = [[ring_row(r, offset, rows) ^ flip for offset, flip in wanted] for r in range(rows)]
    mine = lax.dynamic_index_in_dim(jnp.array(table, jnp.int32), row, 0, keepdims=False)
    return jnp.concatenate([jnp.reshape(spot, (1,)).astype(jnp.int32), mine])


def swap_cores(value, rows):
    return lax.ppermute(value, "rows", [(r, r ^ 1) for r in range(rows)])


def exchange(pieces, feats):
    got = [pieces[0]]
    for k in range(1, feats):
        got.append(lax.ppermute(pieces[k], "feat", [(i, (i + k) % feats) for i in range(feats)]))
    return got


def aggregate_kernel(plan, here, cols, adj, *refs):
    feats, count, hid, half, width, per_block, tile = plan
    blocks = width // tile
    part = blocks // feats
    sources, refs = refs[:count], refs[count:]
    aggs, inverse, held, tiles, sems, tile_sems = refs[:feats], *refs[feats:]
    spot = here[0]
    copies = []
    for n in range(count):
        row = here[1 + n]
        if sources[n].shape[0] == hid:
            target = held.at[row]
        else:
            target = held.at[row, pl.ds((n % 2) * half, half)]
        copies.append(pltpu.make_async_copy(sources[n], target, sems.at[n]))
    for copy in copies:
        copy.start()

    def fetch(block):
        return pltpu.make_async_copy(adj.at[block], tiles.at[block], tile_sems.at[block])

    for block in range(blocks):
        fetch(block).start()
    for copy in copies:
        copy.wait()
    ones = jnp.ones((16, 2 * tile), jnp.bfloat16)
    for k in range(feats):
        where = lax.rem(spot + k, feats)

        def step(local, carry):
            block = where * part + local
            fetch(block).wait()
            total = None
            for t in range(0, per_block, 2):
                left, right = [], []
                for u in (t, t + 1):
                    col = cols[block, u]
                    row = col // blocks
                    lane = pl.multiple_of((col - row * blocks) * tile, tile)
                    left.append(held[row, :, pl.ds(lane, tile)])
                    right.append(tiles[block, u])
                term = lax.dot_general(
                    jnp.concatenate([jnp.concatenate(left, axis=1), ones], axis=0),
                    jnp.concatenate(right, axis=1),
                    (((1,), (1,)), ((), ())),
                    preferred_element_type=jnp.float32,
                )
                total = term if total is None else total + term
            factor = 1.0 / total[hid : hid + 1]
            lane = pl.ds(pl.multiple_of(local * tile, tile), tile)
            aggs[k][:, lane] = (total[:hid] * factor).astype(jnp.bfloat16)
            inverse[where, :, lane] = factor
            return carry

        lax.fori_loop(0, part, step, 0, unroll=2 if part % 2 == 0 else 1)


def middle_kernel(plan, here, wt, wn, bias, inverse, *refs):
    feats, hid, span, chunk = plan
    xs, gos, aggs = refs[:feats], refs[feats : 2 * feats], refs[2 * feats : 3 * feats]
    refs = refs[3 * feats :]
    scaled, acts, grad = refs[:feats], refs[feats : 2 * feats], refs[2 * feats]
    both, cot = refs[2 * feats + 1 :]
    spot = here[0]
    for k in range(feats):
        at = pl.multiple_of(lax.rem(spot - k + feats, feats) * hid, hid)
        both[pl.ds(at, hid)] = xs[k][...]
        both[pl.ds(feats * hid + at, hid)] = aggs[k][...]
        cot[pl.ds(at, hid)] = gos[k][...]
    for c in range(0, span, chunk):
        lane = pl.ds(c, chunk)
        values = both[:, lane]
        for k in range(feats):
            at = pl.ds(pl.multiple_of(lax.rem(spot + k, feats) * hid, hid), hid)
            pre = jnp.dot(wt[at], values, preferred_element_type=jnp.float32) + bias[at]
            slope = jnp.exp(jnp.minimum(pre, 0.0))
            acts[k][:, lane] = jnp.where(pre > 0, pre, slope - 1.0).astype(jnp.bfloat16)
            grad[at, lane] = (cot[at, lane].astype(jnp.float32) * slope).astype(jnp.bfloat16)
        for k in range(feats):
            at = pl.ds(pl.multiple_of(lax.rem(spot + k, feats) * hid, hid), hid)
            back = jnp.dot(wn[at], grad[:, lane], preferred_element_type=jnp.float32)
            scaled[k][:, lane] = (back * inverse[spot, :, lane]).astype(jnp.bfloat16)


def weights_kernel(plan, here, ws, grad, *refs):
    feats, hid, span = plan
    xs, aggs, refs = refs[:feats], refs[feats : 2 * feats], refs[2 * feats :]
    selfs, grads = refs[:feats], refs[feats:]
    spot = here[0]
    every = feats * hid
    g = grad[...]
    contract = (((1,), (1,)), ((), ()))
    sums = lax.dot_general(
        jnp.ones((8, span), jnp.bfloat16), g, contract, preferred_element_type=jnp.float32
    )
    for k in range(feats):
        at = pl.ds(pl.multiple_of(lax.rem(spot + k, feats) * hid, hid), hid)
        selfs[k][...] = jnp.dot(ws[at], g, preferred_element_type=jnp.float32)
        back = (feats - k) % feats
        grads[k][:hid, :every] = lax.dot_general(
            xs[back][...], g, contract, preferred_element_type=jnp.float32
        )
        grads[k][:hid, every:] = lax.dot_general(
            aggs[back][...], g, contract, preferred_element_type=jnp.float32
        )
        grads[k][hid:, :every] = sums
        grads[k][hid:, every:] = sums


def spread_kernel(plan, here, slots, lanes, adj, pair, *refs):
    feats, hid, span, tile, blocks, per_block, outs, with_self = plan
    own, other, refs = refs[:feats], refs[feats : 2 * feats], refs[2 * feats :]
    if with_self:
        selfs, refs = refs[:feats], refs[feats:]
    results, (held, tiles, total, sems) = refs[: 2 * len(outs)], refs[2 * len(outs) :]
    spot = here[0]
    half = hid // 2
    copies = []
    for d in range(len(outs)):
        first = here[1 + d] * CAP
        for side, source in enumerate((adj, pair)):
            for s in range(CAP):
                found = jnp.maximum(slots[side, first + s], 0)
                block = found // per_block
                n = (d * 2 + side) * CAP + s
                copy = pltpu.make_async_copy(
                    source.at[block, found - block * per_block], tiles.at[n], sems.at[n]
                )
                copy.start()
                copies.append(copy)
    for side, pieces in enumerate((own, other)):
        held[side, blocks] = jnp.zeros((hid, tile), jnp.bfloat16)
        for k in range(feats):
            base = lax.rem(spot - k + feats, feats) * (span // tile)
            for local in range(span // tile):
                held[side, base + local] = pieces[k][:, local * tile : (local + 1) * tile]
    for d, kinds in enumerate(outs):
        if with_self:
            for k in range(feats):
                at = pl.multiple_of(lax.rem(spot - k + feats, feats) * span, span)
                total[:, pl.ds(at, span)] = selfs[k][...]
        else:
            total[...] = jnp.zeros_like(total)
        first = here[1 + d] * CAP
        for side in range(2):
            for s0 in range(0, CAP, 6):
                terms = []
                for s in range(s0, s0 + 6):
                    n = (d * 2 + side) * CAP + s
                    copies[n].wait()
                    found = slots[side, first + s]
                    block = jnp.where(found < 0, blocks, found // per_block)
                    term = jnp.dot(
                        held[side, block], tiles[n], preferred_element_type=jnp.float32
                    )
                    terms.append(term)
                for i, term in enumerate(terms):
                    lane = pl.multiple_of(lanes[side, first + s0 + i] * tile, tile)
                    total[:, pl.ds(lane, tile)] += term
        for part, kind in enumerate(kinds):
            value = total[part * half : (part + 1) * half]
            results[2 * d + part][...] = value.astype(kind)


def finish_kernel(base_low, base_high, a_low, b_low, a_high, b_high, out):
    half = a_low.shape[0]
    out[:half] = (
        base_low[...] + a_low[...].astype(jnp.float32) + b_low[...].astype(jnp.float32)
    ).astype(jnp.bfloat16)
    out[half:] = (
        base_high[...] + a_high[...].astype(jnp.float32) + b_high[...].astype(jnp.float32)
    ).astype(jnp.bfloat16)


def place_kernel(feats, here, *refs):
    out = refs[-1]
    span = refs[0].shape[1]
    for k in range(feats):
        at = pl.multiple_of(lax.rem(here[0] - k + feats, feats) * span, span)
        out[:, pl.ds(at, span)] = refs[k][...]


def slot_table(cols, rows, blocks):
    flat = cols.reshape(-1)
    group = flat // blocks
    ids = lax.iota(jnp.int32, flat.shape[0])
    earlier = (group[None, :] == group[:, None]) & (ids[None, :] < ids[:, None])
    spot = group * CAP + jnp.sum(earlier.astype(jnp.int32), axis=1)
    hit = spot[None, :] == lax.iota(jnp.int32, rows * CAP)[:, None]
    slots = jnp.max(jnp.where(hit, ids[None, :], -1), axis=1)
    lanes = jnp.sum(jnp.where(hit, (flat % blocks)[None, :], 0), axis=1)
    return slots, lanes


def shards(rows, feats, features, adjacency, tile_cols, self_weight, neigh_weight, bias_vector, grad_output):
    hid, width = features.shape
    blocks, per_block, tile, unused = adjacency.shape
    half, span = hid // 2, width // feats
    every = hid * feats
    top = rows // 4
    row, spot = lax.axis_index("rows"), lax.axis_index("feat")
    spot_only = jnp.reshape(spot, (1,)).astype(jnp.int32)
    forward, backward = ring_pairs(rows, 1), ring_pairs(rows, -1)

    sources, wanted = [features, swap_cores(features, rows)], [(0, 0), (0, 1)]
    up = [features[:half], features[half:]]
    down = list(up)
    for step in range(1, top + 1):
        arrived = {}
        for part in range(2):
            if step < top or part == 0:
                up[part] = lax.ppermute(up[part], "rows", forward)
                arrived[-step, part] = up[part]
            if step < top or part == 1:
                down[part] = lax.ppermute(down[part], "rows", backward)
                arrived[step, part] = down[part]
        if step == top:
            arrived = {(step, 0): up[0], (step, 1): down[1]}
        for offset in sorted({key[0] for key in arrived}):
            for flip in range(2):
                for part in range(2):
                    piece = arrived[offset, part]
                    sources.append(swap_cores(piece, rows) if flip else piece)
                    wanted.append((offset, flip))

    def sections(value):
        return [
            lax.dynamic_slice_in_dim(value, ((spot + k) % feats) * span, span, axis=1)
            for k in range(feats)
        ]

    xs = exchange(sections(features), feats)
    gos = exchange(sections(grad_output), feats)
    weights = lax.all_gather(jnp.stack([self_weight, neigh_weight]), "feat", axis=1, tiled=True)
    bias = lax.all_gather(bias_vector, "feat", axis=0, tiled=True).reshape(every, 1)
    turned = weights.reshape(2 * every, every).T
    pair_adjacency = swap_cores(adjacency, rows)
    tables = [slot_table(c, rows, blocks) for c in (tile_cols, swap_cores(tile_cols, rows))]
    slots = jnp.stack([t[0] for t in tables])
    lanes = jnp.stack([t[1] for t in tables])

    count = len(sources)
    here = places(spot, row, wanted, rows)
    shape = jax.ShapeDtypeStruct
    *aggs, inverse = pl.pallas_call(
        functools.partial(aggregate_kernel, (feats, count, hid, half, width, per_block, tile)),
        out_shape=[shape((hid, span), jnp.bfloat16)] * feats
        + [shape((feats, 1, span), jnp.float32)],
        in_specs=[SMEM, SMEM, HBM] + [HBM] * count,
        out_specs=[VMEM] * (feats + 1),
        scratch_shapes=[
            pltpu.VMEM((rows, hid, width), jnp.bfloat16),
            pltpu.VMEM(adjacency.shape, jnp.bfloat16),
            pltpu.SemaphoreType.DMA((count,)),
            pltpu.SemaphoreType.DMA((blocks,)),
        ],
        compiler_params=params(),
        cost_estimate=cost(2 * hid * adjacency.size, 2 * adjacency.size + 2 * rows * hid * width),
        name="aggregate",
    )(here, tile_cols, adjacency, *sources)
    aggs = exchange(aggs, feats)

    chunk = min(span, 256)
    outs = pl.pallas_call(
        functools.partial(middle_kernel, (feats, hid, span, chunk)),
        out_shape=[shape((hid, span), jnp.bfloat16)] * (2 * feats)
        + [shape((every, span), jnp.bfloat16)],
        in_specs=[SMEM] + [VMEM] * (4 + 3 * feats),
        out_specs=[VMEM] * (2 * feats + 1),
        scratch_shapes=[
            pltpu.VMEM((2 * every, span), jnp.bfloat16),
            pltpu.VMEM((every, span), jnp.bfloat16),
        ],
        compiler_params=params(),
        cost_estimate=cost(6 * every * every * span, 14 * every * span),
        name="middle",
    )(spot_only, turned, weights[1], bias, inverse, *xs, *gos, *aggs)
    scaled, acts, grad = outs[:feats], outs[feats : 2 * feats], outs[2 * feats]
    scaled = exchange(scaled, feats)
    scaled_pair = [swap_cores(piece, rows) for piece in scaled]

    outs = pl.pallas_call(
        functools.partial(weights_kernel, (feats, hid, span)),
        out_shape=[shape((hid, span), jnp.float32)] * feats
        + [shape((hid + 8, 2 * every), jnp.float32)] * feats,
        in_specs=[SMEM] + [VMEM] * (2 + 2 * feats),
        out_specs=[VMEM] * (2 * feats),
        compiler_params=params(),
        cost_estimate=cost(6 * every * every * span, 10 * every * span),
        name="weights",
    )(spot_only, weights[0], grad, *xs, *aggs)
    selfs, grads = exchange(outs[:feats], feats), exchange(outs[feats:], feats)
    acts = exchange(acts, feats)
    activation = pl.pallas_call(
        functools.partial(place_kernel, feats),
        out_shape=shape((hid, width), jnp.bfloat16),
        in_specs=[SMEM] + [VMEM] * feats,
        out_specs=VMEM,
        compiler_params=params(),
        cost_estimate=cost(0, 4 * hid * width),
        name="place",
    )(spot_only, *acts)
    grads = lax.psum(sum(grads[1:], grads[0]), "rows")
    grad_self, grad_neigh = grads[:hid, :every], grads[:hid, every:]
    grad_bias = lax.dynamic_slice_in_dim(grads[hid, :every], spot * hid, hid)

    def spread(offsets, kinds, extra=()):
        dests = places(spot, row, [(offset, 0) for offset in offsets], rows)
        n = len(offsets) * 2 * CAP
        return pl.pallas_call(
            functools.partial(
                spread_kernel,
                (feats, hid, span, tile, blocks, per_block, kinds, bool(extra)),
            ),
            out_shape=[shape((half, width), kind) for pair in kinds for kind in pair],
            in_specs=[SMEM] * 3 + [HBM] * 2 + [VMEM] * (2 * feats + len(extra)),
            out_specs=[VMEM] * (2 * len(offsets)),
            scratch_shapes=[
                pltpu.VMEM((2, blocks + 1, hid, tile), jnp.bfloat16),
                pltpu.VMEM((n, tile, tile), jnp.bfloat16),
                pltpu.VMEM((hid, width), jnp.float32),
                pltpu.SemaphoreType.DMA((n,)),
            ],
            compiler_params=params(),
            cost_estimate=cost(2 * n * hid * tile * tile, 2 * n * tile * tile + 8 * hid * width),
            name="spread",
        )(dests, slots, lanes, adjacency, pair_adjacency, *scaled, *scaled_pair, *extra)

    narrow, wide = jnp.bfloat16, jnp.float32
    up, down = [None, None], [None, None]

    def joined(arrived, mine):
        if arrived is None:
            return mine
        return (arrived.astype(jnp.float32) + mine).astype(jnp.bfloat16)

    for level in range(top, 0, -1):
        if level == top:
            low, high = spread([top], [(narrow, narrow)])
            up[0] = lax.ppermute(low, "rows", forward)
            down[1] = lax.ppermute(high, "rows", backward)
            continue
        kinds = [
            tuple(narrow if arrived is None else wide for arrived in way) for way in (up, down)
        ]
        mine = spread([level, -level], kinds)
        up = [lax.ppermute(joined(up[i], mine[i]), "rows", forward) for i in range(2)]
        down = [lax.ppermute(joined(down[i], mine[2 + i]), "rows", backward) for i in range(2)]
    low, high = spread([0], [(wide, wide)], extra=tuple(selfs))
    grad_features = pl.pallas_call(
        finish_kernel,
        out_shape=shape((hid, width), jnp.bfloat16),
        in_specs=[VMEM] * 6,
        out_specs=VMEM,
        compiler_params=params(),
        cost_estimate=cost(0, 8 * hid * width),
        name="finish",
    )(low, high, up[0], down[0], up[1], down[1])
    return (activation, grad_features, grad_self, grad_neigh, grad_bias)


def solution(mesh):
    in_specs = (
        P("feat", "rows"),
        P("rows", None, None, None),
        P("rows", None),
        P("feat", None),
        P("feat", None),
        P("feat"),
        P("feat", "rows"),
    )
    out_specs = (P("feat", "rows"), P("feat", "rows"), P("feat", None), P("feat", None), P("feat"))
    body = functools.partial(shards, mesh.shape["rows"], mesh.shape["feat"])
    return jax.shard_map(body, mesh=mesh, in_specs=in_specs, out_specs=out_specs, check_vma=False)
```

```python
import functools

import jax
import jax.numpy as jnp
from jax import lax
from jax.experimental import pallas as pl
from jax.experimental.pallas import tpu as pltpu
from jax.sharding import PartitionSpec as P

CAP = 12
MIB = 1024 * 1024
HBM = pl.BlockSpec(memory_space=pltpu.HBM)
VMEM = pl.BlockSpec(memory_space=pltpu.VMEM)
SMEM = pl.BlockSpec(memory_space=pltpu.SMEM)
LAST = (((1,), (1,)), ((), ()))


def params(mib):
    return pltpu.CompilerParams(vmem_limit_bytes=mib * MIB)


def cost(flops, moved):
    return pl.CostEstimate(flops=flops, bytes_accessed=moved, transcendentals=0)


def product(left, right, dims=(((1,), (0,)), ((), ()))):
    return lax.dot_general(left, right, dims, preferred_element_type=jnp.float32)


def ring_pairs(rows, step):
    levels, chips = rows // 4, rows // 2
    order = [2 * z for z in range(levels)] + [2 * z + 1 for z in reversed(range(levels))]
    return [
        (2 * order[p] + core, 2 * order[(p + step) % chips] + core)
        for p in range(chips)
        for core in range(2)
    ]


def ring_row(row, offset, rows):
    levels, chips = rows // 4, rows // 2
    z, x, core = row // 4, lax.rem(row // 2, 2), lax.rem(row, 2)
    target = lax.rem(jnp.where(x == 0, z, chips - 1 - z) + (offset + chips), chips)
    low = target < levels
    return 2 * jnp.where(low, 2 * target, 2 * (chips - 1 - target) + 1) + core


def swap(value, rows, bit=1):
    return lax.ppermute(value, "rows", [(r, r ^ bit) for r in range(rows)])


def exchange(pieces, feats):
    got = [pieces[0]]
    for k in range(1, feats):
        got.append(lax.ppermute(pieces[k], "feat", [(i, (i + k) % feats) for i in range(feats)]))
    return got


def ahead(k, feats, size):
    return pl.multiple_of(lax.rem(lax.axis_index("feat") + k, feats) * size, size)


def behind(k, feats, size):
    return pl.multiple_of(lax.rem(lax.axis_index("feat") - k + feats, feats) * size, size)


def pack_kernel(feats, feature, grad_output, ws, wn, bias, *outs):
    hid, every = ws.shape
    span = feature.shape[1] // feats
    line = lax.broadcasted_iota(jnp.int32, (hid, hid), 0)
    lane = lax.broadcasted_iota(jnp.int32, (hid, hid), 1)
    column = jnp.sum(jnp.where(line == lane, bias[...], 0.0), axis=1, keepdims=True)
    high = column.astype(jnp.bfloat16).astype(jnp.float32)
    middle = (column - high).astype(jnp.bfloat16).astype(jnp.float32)
    spread = lax.broadcasted_iota(jnp.int32, (hid, 128), 1)
    parts = jnp.where(
        spread == 0, high, jnp.where(spread == 1, middle, jnp.where(spread == 2, column - high - middle, 0.0))
    )
    for k in range(feats):
        at = pl.ds(ahead(k, feats, span), span)
        outs[k][:, :span] = feature[:, at]
        outs[k][:, span : 2 * span] = grad_output[:, at]
        outs[k][:, 2 * span : 2 * span + every] = ws[...]
        outs[k][:, 2 * span + every : 2 * span + 2 * every] = wn[...]
        outs[k][:, 2 * span + 2 * every :] = parts.astype(jnp.bfloat16)


def unpack_kernel(feats, *refs):
    packs, (turned, ws_all, wn_all, bias_all, x_all, cot_all, both) = refs[:feats], refs[feats:]
    hid, span = packs[0].shape[0], x_all.shape[1]
    every = feats * hid
    for k in range(feats):
        at = pl.ds(behind(k, feats, hid), hid)
        pack = packs[k]
        x_all[at] = pack[:, :span]
        cot_all[at] = pack[:, span : 2 * span]
        ws_all[at] = pack[:, 2 * span : 2 * span + every]
        wn_all[at] = pack[:, 2 * span + every : 2 * span + 2 * every]
        parts = pack[:, 2 * span + 2 * every :].astype(jnp.float32)
        bias_all[at] = jnp.sum(parts, axis=1, keepdims=True)
    both[:every] = ws_all[...].astype(jnp.float32)
    both[every:] = wn_all[...].astype(jnp.float32)
    turned[...] = both[...].T.astype(jnp.bfloat16)


def table_kernel(cols, table, counts):
    blocks, per_block = cols.shape
    size = table.shape[0]

    def clear(i, carry):
        table[i] = -1
        return carry

    def reset(i, carry):
        counts[i] = 0
        return carry

    lax.fori_loop(0, size, clear, 0)
    lax.fori_loop(0, size // CAP, reset, 0)

    def step(block, carry):
        for t in range(per_block):
            col = cols[block, t]
            group = col // blocks
            seen = counts[group]
            table[group * CAP + seen] = (block * per_block + t) * 256 + (col - group * blocks)
            counts[group] = seen + 1
        return carry

    lax.fori_loop(0, blocks, step, 0)


def aggregate_kernel(plan, cols, adj, *refs):
    feats, wanted, rows, hid, half, width, per_block, tile = plan
    count = len(wanted)
    blocks = width // tile
    part = blocks // feats
    sources, refs = refs[:count], refs[count:]
    aggs, inverse, held, sems = refs[:feats], *refs[feats:]
    row = lax.axis_index("rows")
    copies = []
    for n, (offset, flip, side) in enumerate(wanted):
        place = ring_row(row, offset, rows)
        if flip:
            place = place + 1 - 2 * lax.rem(place, 2)
        target = held.at[place]
        if side is not None:
            target = held.at[place, pl.ds(side * half, half)]
        copies.append(pltpu.make_async_copy(sources[n], target, sems.at[n]))
    for copy in copies:
        copy.start()
    for copy in copies:
        copy.wait()
    ones = jnp.ones((16, 2 * tile), jnp.bfloat16)
    for k in range(feats):
        where = lax.rem(lax.axis_index("feat") + k, feats)

        def step(local, carry):
            block = where * part + local
            total = None
            for t in range(0, per_block, 2):
                left, right = [], []
                for u in (t, t + 1):
                    col = cols[block, u]
                    source = col // blocks
                    lane = pl.multiple_of((col - source * blocks) * tile, tile)
                    left.append(held[source, :, pl.ds(lane, tile)])
                    right.append(adj[block, u])
                term = product(
                    jnp.concatenate([jnp.concatenate(left, axis=1), ones], axis=0),
                    jnp.concatenate(right, axis=1),
                    LAST,
                )
                total = term if total is None else total + term
            factor = 1.0 / total[hid : hid + 1]
            lane = pl.ds(pl.multiple_of(local * tile, tile), tile)
            aggs[k][:, lane] = (total[:hid] * factor).astype(jnp.bfloat16)
            inverse[where, :, lane] = factor
            return carry

        lax.fori_loop(0, part, step, 0, unroll=2 if part % 2 == 0 else 1)


def middle_kernel(plan, turned, wn, bias, inverse, x_all, cot, *refs):
    feats, hid, span, chunk = plan
    aggs, refs = refs[:feats], refs[feats:]
    scaled, acts, grad, both = refs[:feats], refs[feats : 2 * feats], *refs[2 * feats :]
    every = feats * hid
    both[:every] = x_all[...]
    for k in range(feats):
        both[pl.ds(every + behind(k, feats, hid), hid)] = aggs[k][...]
    for c in range(0, span, chunk):
        lane = pl.ds(c, chunk)
        for k in range(feats):
            at = pl.ds(ahead(k, feats, hid), hid)
            pre = product(turned[at], both[:, lane]) + bias[at]
            slope = jnp.exp(jnp.minimum(pre, 0.0))
            acts[k][:, lane] = jnp.where(pre > 0, pre, slope - 1.0).astype(jnp.bfloat16)
            grad[at, lane] = (cot[at, lane].astype(jnp.float32) * slope).astype(jnp.bfloat16)
        for k in range(feats):
            at = pl.ds(ahead(k, feats, hid), hid)
            back = product(wn[at], grad[:, lane])
            factor = inverse[lax.axis_index("feat"), :, lane]
            scaled[k][:, lane] = (back * factor).astype(jnp.bfloat16)


def own_quarter():
    row = lax.axis_index("rows")
    return 2 * lax.rem(row, 2) + lax.rem(row // 2, 2)


def turned_quarter(mine, index):
    both = (index // 2, index % 2)
    core = both[0] + mine // 2 - 2 * both[0] * (mine // 2)
    x = both[1] + lax.rem(mine, 2) - 2 * both[1] * lax.rem(mine, 2)
    return 2 * core + x


def weights_kernel(feats, ws, x_all, grad, *refs):
    aggs, refs = refs[:feats], refs[feats:]
    selfs, grads = refs[:feats], refs[feats:]
    every, span = grad.shape
    hid = every // feats
    wide = every // 2
    mine = own_quarter()
    g = grad[...]
    sums = product(jnp.ones((8, span), jnp.bfloat16), g, LAST)
    for k in range(feats):
        at = pl.ds(ahead(k, feats, hid), hid)
        selfs[k][...] = product(ws[at], g)
        values = [product(x_all[at], g, LAST), product(aggs[(feats - k) % feats][...], g, LAST)]
        for quarter in range(4):
            slot = turned_quarter(mine, quarter)
            lane = slice(quarter % 2 * wide, (quarter % 2 + 1) * wide)
            grads[k][slot, :hid] = values[quarter // 2][:, lane]
            grads[k][slot, hid:] = sums[:, lane]


def collect_kernel(pair, pair_far, grad_self, grad_neigh, sums):
    hid, every = grad_self.shape
    wide = every // 2
    mine = own_quarter()
    for slot in range(4):
        value = (pair, pair_far)[slot // 2][slot % 2]
        quarter = turned_quarter(mine, slot)
        for q, out in enumerate((grad_self, grad_self, grad_neigh, grad_neigh)):

            @pl.when(quarter == q)
            def _():
                lane = slice(q % 2 * wide, (q % 2 + 1) * wide)
                out[:, lane] = value[:hid]
                if q < 2:
                    sums[:, lane] = value[hid:]


def arrange_kernel(feats, tile, *refs):
    pieces, held = refs[:-1], refs[-1]
    hid, span = pieces[0].shape
    part = span // tile
    for side in range(2):
        held[side, feats * part] = jnp.zeros((hid, tile), jnp.bfloat16)
        for k in range(feats):
            base = lax.rem(lax.axis_index("feat") - k + feats, feats) * part
            for local in range(part):
                held[side, base + local] = pieces[side * feats + k][:, local * tile : (local + 1) * tile]


def spread_kernel(plan, table, table_pair, adj, pair, held, *refs):
    feats, rows, offsets, kinds = plan
    selfs = refs[:feats] if offsets == (0,) else ()
    refs = refs[len(selfs) :]
    results, total = refs[:-1], refs[-1]
    blocks, per_block, tile, unused = adj.shape
    half = total.shape[0] // 2
    for d, offset in enumerate(offsets):
        if selfs:
            span = selfs[0].shape[1]
            for k in range(feats):
                total[:, pl.ds(behind(k, feats, span), span)] = selfs[k][...]
        else:
            total[...] = jnp.zeros_like(total)
        first = ring_row(lax.axis_index("rows"), offset, rows) * CAP
        for side, (slots, tiles) in enumerate(((table, adj), (table_pair, pair))):
            for s0 in range(0, CAP, 4):
                terms = []
                for s in range(s0, s0 + 4):
                    entry = slots[first + s]
                    index = jnp.maximum(entry, 0) // 256
                    block = index // per_block
                    place = jnp.where(entry < 0, blocks, block)
                    lane = lax.rem(jnp.maximum(entry, 0), 256) * tile
                    term = product(held[side, place], tiles[block, index - block * per_block])
                    terms.append((pl.multiple_of(lane, tile), term))
                for lane, term in terms:
                    total[:, pl.ds(lane, tile)] += term
        for part in range(2):
            value = total[part * half : (part + 1) * half]
            results[2 * d + part][...] = value.astype(kinds[2 * d + part])


def finish_kernel(base_low, base_high, a_low, b_low, a_high, b_high, out):
    half = a_low.shape[0]
    low = base_low[...] + a_low[...].astype(jnp.float32) + b_low[...].astype(jnp.float32)
    out[:half] = low.astype(jnp.bfloat16)
    high = base_high[...] + a_high[...].astype(jnp.float32) + b_high[...].astype(jnp.float32)
    out[half:] = high.astype(jnp.bfloat16)


def place_kernel(feats, *refs):
    out = refs[-1]
    span = refs[0].shape[1]
    for k in range(feats):
        out[:, pl.ds(behind(k, feats, span), span)] = refs[k][...]


def call(kernel, name, outs, ins, out_specs, scratch, mib, flops, moved, *args):
    return pl.pallas_call(
        kernel,
        out_shape=[jax.ShapeDtypeStruct(shape, kind) for shape, kind in outs],
        in_specs=ins,
        out_specs=out_specs,
        scratch_shapes=scratch,
        compiler_params=params(mib),
        cost_estimate=cost(flops, moved),
        name=name,
    )(*args)


def shards(rows, feats, features, adjacency, tile_cols, self_weight, neigh_weight, bias_vector, grad_output):
    hid, width = features.shape
    blocks, per_block, tile, unused = adjacency.shape
    half, span = hid // 2, width // feats
    every = hid * feats
    top = rows // 4
    narrow, wide = jnp.bfloat16, jnp.float32
    forward, backward = ring_pairs(rows, 1), ring_pairs(rows, -1)
    bind = functools.partial

    sources, wanted = [features, swap(features, rows)], [(0, 0, None), (0, 1, None)]
    up = [features[:half], features[half:]]
    down = list(up)
    for step in range(1, top + 1):
        for side in range(2):
            arrived = []
            if step < top or side == 0:
                up[side] = lax.ppermute(up[side], "rows", forward)
                arrived.append((-step, up[side]))
            if step < top or side == 1:
                down[side] = lax.ppermute(down[side], "rows", backward)
                arrived.append((step, down[side]))
            for offset, piece in arrived:
                sources += [piece, swap(piece, rows)]
                wanted += [(offset, 0, side), (offset, 1, side)]

    packed = 2 * span + 2 * every + 128
    packs = call(
        bind(pack_kernel, feats), "pack", [((hid, packed), narrow)] * feats, [VMEM] * 5,
        [VMEM] * feats, [], 8, 0, 4 * hid * packed * feats,
        features, grad_output, self_weight, neigh_weight, bias_vector.reshape(1, hid),
    )
    packs = exchange(packs, feats)
    turned, ws_all, wn_all, bias_all, x_all, cot_all = call(
        bind(unpack_kernel, feats), "unpack",
        [((every, 2 * every), narrow), ((every, every), narrow), ((every, every), narrow),
         ((every, 1), wide), ((every, span), narrow), ((every, span), narrow)],
        [VMEM] * feats, [VMEM] * 6, [pltpu.VMEM((2 * every, every), wide)], 8, 0,
        4 * every * packed, *packs,
    )
    (table,) = call(
        table_kernel, "table", [((rows * CAP,), jnp.int32)], [SMEM], [SMEM],
        [pltpu.SMEM((rows,), jnp.int32)], 4, 0, 8 * rows * CAP, tile_cols,
    )
    table_pair = swap(table, rows)
    pair = swap(adjacency, rows)

    count = len(sources)
    *aggs, inverse = call(
        bind(aggregate_kernel, (feats, tuple(wanted), rows, hid, half, width, per_block, tile)),
        "aggregate", [((hid, span), narrow)] * feats + [((feats, 1, span), wide)],
        [SMEM, VMEM] + [HBM] * count, [VMEM] * (feats + 1),
        [pltpu.VMEM((rows, hid, width), narrow), pltpu.SemaphoreType.DMA((count,))], 20,
        2 * hid * adjacency.size, 2 * adjacency.size + 2 * rows * hid * width,
        tile_cols, adjacency, *sources,
    )
    aggs = exchange(aggs, feats)

    outs = call(
        bind(middle_kernel, (feats, hid, span, min(span, 256))), "middle",
        [((hid, span), narrow)] * (2 * feats) + [((every, span), narrow)],
        [VMEM] * (6 + feats), [VMEM] * (2 * feats + 1),
        [pltpu.VMEM((2 * every, span), narrow)], 12,
        6 * every * every * span, 14 * every * span,
        turned, wn_all, bias_all, inverse, x_all, cot_all, *aggs,
    )
    scaled, acts, grad = outs[:feats], outs[feats : 2 * feats], outs[2 * feats]
    scaled = exchange(scaled, feats)
    scaled_pair = [swap(piece, rows) for piece in scaled]

    outs = call(
        bind(weights_kernel, feats), "weights",
        [((hid, span), wide)] * feats + [((4, hid + 8, every // 2), wide)] * feats,
        [VMEM] * (3 + feats), [VMEM] * (2 * feats), [], 12,
        6 * every * every * span, 10 * every * span,
        ws_all, x_all, grad, *aggs,
    )
    selfs, grads = exchange(outs[:feats], feats), exchange(outs[feats:], feats)
    acts = exchange(acts, feats)
    (activation,) = call(
        bind(place_kernel, feats), "place", [((hid, width), narrow)], [VMEM] * feats, [VMEM], [], 8,
        0, 4 * hid * width, *acts,
    )

    grads = sum(grads[1:], grads[0])
    grads = grads[:2] + swap(grads[2:], rows, 1)
    grads = grads[0] + swap(grads[1], rows, 2)
    bit = 4
    while bit < rows:
        grads = grads + swap(grads, rows, bit)
        bit *= 2
    near = jnp.stack([grads, swap(grads, rows, 2)])
    far = swap(near, rows, 1)
    grad_self, grad_neigh, sums = call(
        collect_kernel, "collect",
        [((hid, every), wide), ((hid, every), wide), ((8, every), wide)],
        [VMEM] * 2, [VMEM] * 3, [], 8, 0, 16 * hid * every, near, far,
    )
    grad_bias = lax.dynamic_slice_in_dim(sums[0], lax.axis_index("feat") * hid, hid)

    (held,) = call(
        bind(arrange_kernel, feats, tile), "arrange", [((2, blocks + 1, hid, tile), narrow)],
        [VMEM] * (2 * feats), [VMEM], [], 8, 0, 8 * hid * width, *scaled, *scaled_pair,
    )

    def spread(offsets, kinds, extra=()):
        return call(
            bind(spread_kernel, (feats, rows, offsets, kinds)), "spread",
            [((half, width), kind) for kind in kinds],
            [SMEM] * 2 + [VMEM] * (3 + len(extra)), [VMEM] * len(kinds),
            [pltpu.VMEM((hid, width), wide)], 8,
            4 * CAP * len(offsets) * hid * tile * tile, 8 * hid * width * len(offsets),
            table, table_pair, adjacency, pair, held, *extra,
        )

    up, down = [None, None], [None, None]

    def joined(arrived, mine):
        if arrived is None:
            return mine
        return (arrived.astype(jnp.float32) + mine).astype(jnp.bfloat16)

    for level in range(top, 0, -1):
        if level == top:
            low, high = spread((top,), (narrow, narrow))
            up[0] = lax.ppermute(low, "rows", forward)
            down[1] = lax.ppermute(high, "rows", backward)
            continue
        kinds = tuple(narrow if arrived is None else wide for arrived in up + down)
        mine = spread((level, -level), kinds)
        up = [lax.ppermute(joined(up[i], mine[i]), "rows", forward) for i in range(2)]
        down = [lax.ppermute(joined(down[i], mine[2 + i]), "rows", backward) for i in range(2)]
    low, high = spread((0,), (wide, wide), extra=tuple(selfs))
    (grad_features,) = call(
        finish_kernel, "finish", [((hid, width), narrow)], [VMEM] * 6, [VMEM], [], 8, 0,
        8 * hid * width, low, high, up[0], down[0], up[1], down[1],
    )
    return (activation, grad_features, grad_self, grad_neigh, grad_bias)


def solution(mesh):
    in_specs = (
        P("feat", "rows"),
        P("rows", None, None, None),
        P("rows", None),
        P("feat", None),
        P("feat", None),
        P("feat"),
        P("feat", "rows"),
    )
    out_specs = (P("feat", "rows"), P("feat", "rows"), P("feat", None), P("feat", None), P("feat"))
    body = functools.partial(shards, mesh.shape["rows"], mesh.shape["feat"])
    return jax.shard_map(body, mesh=mesh, in_specs=in_specs, out_specs=out_specs, check_vma=False)
```

```python
import functools

import jax
import jax.numpy as jnp
from jax import lax
from jax.experimental import pallas as pl
from jax.experimental.pallas import tpu as pltpu
from jax.sharding import PartitionSpec as P

CAP = 12
MIB = 1024 * 1024
WHOLE = 60
HBM = pl.BlockSpec(memory_space=pltpu.HBM)
VMEM = pl.BlockSpec(memory_space=pltpu.VMEM)
SMEM = pl.BlockSpec(memory_space=pltpu.SMEM)
LAST = (((1,), (1,)), ((), ()))


def params(mib):
    return pltpu.CompilerParams(vmem_limit_bytes=mib * MIB)


def cost(flops, moved):
    return pl.CostEstimate(flops=flops, bytes_accessed=moved, transcendentals=0)


def product(left, right, dims=(((1,), (0,)), ((), ()))):
    return lax.dot_general(left, right, dims, preferred_element_type=jnp.float32)


def ring_pairs(rows, step, flip=0):
    levels, chips = rows // 4, rows // 2
    order = [2 * z for z in range(levels)] + [2 * z + 1 for z in reversed(range(levels))]
    return [
        (2 * order[p] + core, 2 * order[(p + step) % chips] + (core ^ flip))
        for p in range(chips)
        for core in range(2)
    ]


def ring_row(row, offset, rows):
    levels, chips = rows // 4, rows // 2
    z, x, core = row // 4, lax.rem(row // 2, 2), lax.rem(row, 2)
    target = lax.rem(jnp.where(x == 0, z, chips - 1 - z) + (offset + chips), chips)
    low = target < levels
    return 2 * jnp.where(low, 2 * target, 2 * (chips - 1 - target) + 1) + core


def swap(value, rows, bit=1):
    return lax.ppermute(value, "rows", [(r, r ^ bit) for r in range(rows)])


def exchange(pieces, feats):
    got = [pieces[0]]
    for k in range(1, feats):
        got.append(lax.ppermute(pieces[k], "feat", [(i, (i + k) % feats) for i in range(feats)]))
    return got


def after(value, *others):
    return lax.optimization_barrier((value, *others))[0]


def ahead(k, feats, size):
    return pl.multiple_of(lax.rem(lax.axis_index("feat") + k, feats) * size, size)


def behind(k, feats, size):
    return pl.multiple_of(lax.rem(lax.axis_index("feat") - k + feats, feats) * size, size)


def pack_kernel(feats, feature, grad_output, ws, wn, bias, *refs):
    outs, (parts, sems) = refs[:feats], refs[feats:]
    hid, every = ws.shape
    span = feature.shape[1] // feats
    copies = []
    for k in range(feats):
        at = pl.ds(ahead(k, feats, span), span)
        for source, low, size in (
            (feature.at[:, at], 0, span),
            (grad_output.at[:, at], span, span),
            (ws, 2 * span, every),
            (wn, 2 * span + every, every),
            (parts, 2 * span + 2 * every, 128),
        ):
            place = outs[k].at[:, pl.ds(low, size)]
            copies.append(pltpu.make_async_copy(source, place, sems.at[len(copies)]))
    line = lax.broadcasted_iota(jnp.int32, (hid, hid), 0)
    lane = lax.broadcasted_iota(jnp.int32, (hid, hid), 1)
    column = jnp.sum(jnp.where(line == lane, bias[...], 0.0), axis=1, keepdims=True)
    high = column.astype(jnp.bfloat16).astype(jnp.float32)
    middle = (column - high).astype(jnp.bfloat16).astype(jnp.float32)
    low = column - high - middle
    at = lax.broadcasted_iota(jnp.int32, (hid, 128), 1)
    value = jnp.where(at == 0, high, jnp.where(at == 1, middle, jnp.where(at == 2, low, 0.0)))
    parts[...] = value.astype(jnp.bfloat16)
    for copy in copies:
        copy.start()
    for copy in copies:
        copy.wait()


def unpack_kernel(feats, *refs):
    packs, (turned, ws_all, wn_all, bias_all, x_all, cot_all, both) = refs[:feats], refs[feats:]
    hid, span = packs[0].shape[0], x_all.shape[1]
    every = feats * hid
    for k in range(feats):
        at = pl.ds(behind(k, feats, hid), hid)
        pack = packs[k]
        x_all[at] = pack[:, :span]
        cot_all[at] = pack[:, span : 2 * span]
        ws_all[at] = pack[:, 2 * span : 2 * span + every]
        wn_all[at] = pack[:, 2 * span + every : 2 * span + 2 * every]
        parts = pack[:, 2 * span + 2 * every :].astype(jnp.float32)
        bias_all[at] = jnp.sum(parts, axis=1, keepdims=True)
    both[:every] = ws_all[...].astype(jnp.float32)
    both[every:] = wn_all[...].astype(jnp.float32)
    turned[...] = both[...].T.astype(jnp.bfloat16)


def table_kernel(cols, table, counts):
    blocks, per_block = cols.shape
    base = blocks * per_block
    groups = counts.shape[0]

    def clear(i, carry):
        counts[i] = 0
        for s in range(CAP):
            table[base + i * CAP + s] = -1
        return carry

    lax.fori_loop(0, groups, clear, 0)

    def step(block, carry):
        for t in range(per_block):
            col = cols[block, t]
            group = col // blocks
            seen = counts[group]
            counts[group] = seen + 1
            index = block * per_block + t
            table[index] = col
            table[base + group * CAP + seen] = index * 256 + (col - group * blocks)
        return carry

    lax.fori_loop(0, blocks, step, 0)


def aggregate_kernel(plan, table, table_pair, adj, pair, *refs):
    feats, parts, wanted, rows = plan
    count, taken = len(wanted), len(parts)
    blocks, per_block, tile, unused = adj.shape
    part = blocks // feats
    half = refs[0].shape[0]
    sources, refs = refs[:count], refs[count:]
    near, far, inverse, (held, tiles, sems, tile_sems) = (
        refs[:taken],
        refs[taken : 2 * taken],
        refs[2 * taken],
        refs[2 * taken + 1 :],
    )
    row = lax.axis_index("rows")
    copies = []
    for n, (offset, side) in enumerate(wanted):
        place = ring_row(row, offset, rows)
        if side:
            place = place + 1 - 2 * lax.rem(place, 2)
        copies.append(pltpu.make_async_copy(sources[n], held.at[place], sems.at[n]))

    def fetch(slot, local, side):
        where = lax.rem(lax.axis_index("feat") + parts[slot], feats)
        return pltpu.make_async_copy(
            (adj, pair)[side].at[where * part + local],
            tiles.at[slot, local, side],
            tile_sems.at[slot, local, side],
        )

    for copy in copies:
        copy.start()
    for slot in range(taken):
        for local in range(part):
            for side in range(2):
                fetch(slot, local, side).start()
    for copy in copies:
        copy.wait()
    ones = jnp.ones((16, 2 * tile), jnp.bfloat16)
    for slot in range(taken):
        where = lax.rem(lax.axis_index("feat") + parts[slot], feats)

        def step(local, carry):
            lane = pl.ds(pl.multiple_of(local * tile, tile), tile)
            for side in range(2):
                fetch(slot, local, side).wait()
            for side in range(2):
                first = (where * part + local) * per_block
                total = None
                for t in range(0, per_block, 2):
                    left, right = [], []
                    for u in (t, t + 1):
                        col = (table, table_pair)[side][first + u]
                        source = col // blocks
                        at = pl.multiple_of((col - source * blocks) * tile, tile)
                        left.append(held[source, :, pl.ds(at, tile)])
                        right.append(tiles[slot, local, side, u])
                    term = product(
                        jnp.concatenate([jnp.concatenate(left, axis=1), ones], axis=0),
                        jnp.concatenate(right, axis=1),
                        LAST,
                    )
                    total = term if total is None else total + term
                factor = 1.0 / total[half : half + 1]
                value = (total[:half] * factor).astype(jnp.bfloat16)
                (near, far)[side][slot][:, lane] = value
                if side == 0:
                    inverse[slot, :, lane] = factor
            return carry

        lax.fori_loop(0, part, step, 0)


def middle_kernel(plan, turned, wn, bias, inverse, x_all, cot, *refs):
    feats, hid, span, chunk = plan
    near, far, refs = refs[:feats], refs[feats : 2 * feats], refs[2 * feats :]
    scaled, acts, grad, agg = refs[:feats], refs[feats : 2 * feats], refs[2 * feats], refs[2 * feats + 1]
    half = hid // 2
    core = lax.rem(lax.axis_index("rows"), 2)
    for k in range(feats):
        base = behind(k, feats, hid)
        agg[pl.ds(pl.multiple_of(base + core * half, half), half)] = near[k][...]
        agg[pl.ds(pl.multiple_of(base + (1 - core) * half, half), half)] = far[k][...]
    every = feats * hid
    for c in range(0, span, chunk):
        lane = pl.ds(c, chunk)
        for k in range(feats):
            at = pl.ds(ahead(k, feats, hid), hid)
            pre = product(turned[at, :every], x_all[:, lane])
            pre = pre + product(turned[at, every:], agg[:, lane]) + bias[at]
            slope = jnp.exp(jnp.minimum(pre, 0.0))
            acts[k][:, lane] = jnp.where(pre > 0, pre, slope - 1.0).astype(jnp.bfloat16)
            grad[at, lane] = (cot[at, lane].astype(jnp.float32) * slope).astype(jnp.bfloat16)
        for k in range(feats):
            at = pl.ds(ahead(k, feats, hid), hid)
            back = product(wn[at], grad[:, lane])
            scaled[k][:, lane] = (back * inverse[0, :, lane]).astype(jnp.bfloat16)


def own_quarter():
    row = lax.axis_index("rows")
    return 2 * lax.rem(row, 2) + lax.rem(row // 2, 2)


def turned_quarter(mine, index):
    both = (index // 2, index % 2)
    core = both[0] + mine // 2 - 2 * both[0] * (mine // 2)
    x = both[1] + lax.rem(mine, 2) - 2 * both[1] * lax.rem(mine, 2)
    return 2 * core + x


def weights_kernel(feats, ws, x_all, agg, grad, *refs):
    acts, (first, *sent), grads = refs[:feats], refs[feats : 2 * feats], refs[2 * feats :]
    every, span = grad.shape
    hid = every // feats
    wide = every // 2
    mine = own_quarter()
    g = grad[...]
    sums = product(jnp.ones((8, span), jnp.bfloat16), g, LAST)
    for k in range(feats):
        at = pl.ds(ahead(k, feats, hid), hid)
        own = product(ws[at], g)
        if k == 0:
            first[...] = own
        else:
            high = own.astype(jnp.bfloat16)
            sent[k - 1][:, :span] = acts[k][...]
            sent[k - 1][:, span : 2 * span] = high
            sent[k - 1][:, 2 * span :] = (own - high.astype(jnp.float32)).astype(jnp.bfloat16)
        values = [product(x_all[at], g, LAST), product(agg[at], g, LAST)]
        for quarter in range(4):
            slot = turned_quarter(mine, quarter)
            lane = slice(quarter % 2 * wide, (quarter % 2 + 1) * wide)
            grads[k][slot, :hid] = values[quarter // 2][:, lane]
            grads[k][slot, hid:] = sums[:, lane]


def collect_kernel(pair, pair_far, grad_self, grad_neigh, sums):
    hid, every = grad_self.shape
    wide = every // 2
    mine = own_quarter()
    for slot in range(4):
        value = (pair, pair_far)[slot // 2][slot % 2]
        quarter = turned_quarter(mine, slot)
        for q, out in enumerate((grad_self, grad_self, grad_neigh, grad_neigh)):

            @pl.when(quarter == q)
            def _():
                lane = slice(q % 2 * wide, (q % 2 + 1) * wide)
                out[:, lane] = value[:hid]
                if q < 2:
                    sums[:, lane] = value[hid:]


def arrange_kernel(feats, tile, *refs):
    pieces, held = refs[:-1], refs[-1]
    hid, span = pieces[0].shape
    part = span // tile
    for side in range(2):
        held[side, feats * part] = jnp.zeros((hid, tile), jnp.bfloat16)
        for k in range(feats):
            base = lax.rem(lax.axis_index("feat") - k + feats, feats) * part
            for local in range(part):
                held[side, base + local] = pieces[side * feats + k][:, local * tile : (local + 1) * tile]


def spread_kernel(plan, table, table_pair, adj, pair, held, *refs):
    rows, offsets, kinds = plan
    results, (total, tiles, sems) = refs[: len(kinds)], refs[len(kinds) :]
    blocks, per_block, tile, unused = adj.shape
    half = total.shape[0] // 2
    row = lax.axis_index("rows")
    firsts = [blocks * per_block + ring_row(row, offset, rows) * CAP for offset in offsets]
    sides = ((table, adj), (table_pair, pair))
    copies = []
    for d in range(len(offsets)):
        for side, (slots, source) in enumerate(sides):
            for s in range(CAP):
                index = jnp.maximum(slots[firsts[d] + s], 0) // 256
                block = index // per_block
                n = (2 * d + side) * CAP + s
                tiled = source.at[block, index - block * per_block]
                copies.append(pltpu.make_async_copy(tiled, tiles.at[n], sems.at[n]))
                copies[-1].start()
    for d in range(len(offsets)):
        total[...] = jnp.zeros_like(total)
        for copy in copies[2 * d * CAP : 2 * (d + 1) * CAP]:
            copy.wait()
        for side, (slots, source) in enumerate(sides):
            for s0 in range(0, CAP, 4):
                terms = []
                for s in range(s0, s0 + 4):
                    entry = slots[firsts[d] + s]
                    index = jnp.maximum(entry, 0) // 256
                    place = jnp.where(entry < 0, blocks, index // per_block)
                    lane = lax.rem(jnp.maximum(entry, 0), 256) * tile
                    term = product(held[side, place], tiles[(2 * d + side) * CAP + s])
                    terms.append((pl.multiple_of(lane, tile), term))
                for lane, term in terms:
                    total[:, pl.ds(lane, tile)] += term
        for part in range(2):
            value = total[part * half : (part + 1) * half]
            results[2 * d + part][...] = value.astype(kinds[2 * d + part])


def finish_kernel(feats, base_low, base_high, a_low, b_low, a_high, b_high, *refs):
    (own, *sent), out = refs[:feats], refs[feats]
    half, span = a_low.shape[0], own.shape[1]
    for k in range(feats):
        at = behind(k, feats, span)
        nodes = pl.ds(at, span)
        for part, (base, a, b) in enumerate(((base_low, a_low, b_low), (base_high, a_high, b_high))):
            lines = slice(part * half, (part + 1) * half)
            if k == 0:
                value = own[lines]
            else:
                value = sent[k - 1][lines, span : 2 * span].astype(jnp.float32)
                value = value + sent[k - 1][lines, 2 * span :].astype(jnp.float32)
            value = value + base[:, nodes] + a[:, nodes].astype(jnp.float32)
            out[lines, nodes] = (value + b[:, nodes].astype(jnp.float32)).astype(jnp.bfloat16)


def place_kernel(feats, *refs):
    (own, *sent), out = refs[:feats], refs[feats]
    span = own.shape[1]
    out[:, pl.ds(behind(0, feats, span), span)] = own[...]
    for k in range(1, feats):
        out[:, pl.ds(behind(k, feats, span), span)] = sent[k - 1][:, :span]


def call(kernel, name, outs, ins, out_specs, scratch, mib, flops, moved, *args):
    return pl.pallas_call(
        kernel,
        out_shape=[jax.ShapeDtypeStruct(shape, kind) for shape, kind in outs],
        in_specs=ins,
        out_specs=out_specs,
        scratch_shapes=scratch,
        compiler_params=params(mib),
        cost_estimate=cost(flops, moved),
        name=name,
    )(*args)


def shards(rows, feats, features, adjacency, tile_cols, self_weight, neigh_weight, bias_vector, grad_output):
    hid, width = features.shape
    blocks, per_block, tile, unused = adjacency.shape
    half, span = hid // 2, width // feats
    every = hid * feats
    top = rows // 4
    narrow, wide = jnp.bfloat16, jnp.float32
    forward, backward = ring_pairs(rows, 1), ring_pairs(rows, -1)
    bind = functools.partial

    core = lax.rem(lax.axis_index("rows"), 2)
    mine = lax.dynamic_slice_in_dim(features, core * half, half)
    away = lax.dynamic_slice_in_dim(features, (1 - core) * half, half)
    sources, wanted = [mine], [(0, 0)]
    up, down = [mine, away], [mine, away]
    (table,) = call(
        table_kernel, "table", [((tile_cols.size + rows * CAP,), jnp.int32)], [SMEM], [SMEM],
        [pltpu.SMEM((rows,), jnp.int32)], 4, 0, 8 * rows * CAP, tile_cols,
    )
    packed = 2 * span + 2 * every + 128
    packs = call(
        bind(pack_kernel, feats), "pack", [((hid, packed), narrow)] * feats, [HBM] * 4 + [VMEM],
        [HBM] * feats,
        [pltpu.VMEM((hid, 128), narrow), pltpu.SemaphoreType.DMA((5 * feats,))], WHOLE, 0,
        4 * hid * packed * feats,
        features, grad_output, self_weight, neigh_weight, bias_vector.reshape(1, hid),
    )
    for step in range(1, top + 1):
        if step == 2:
            pair = swap(after(adjacency, up[0], down[0]), rows)
        if step == top - 1:
            up[0], pair, table, packs = lax.optimization_barrier((up[0], pair, table, packs))
            table_pair = swap(table, rows)
            packs = exchange(packs, feats)
        if step == top:
            sources.append(swap(after(away, up[0], down[0]), rows))
            wanted.append((0, 1))
        for side in range(2):
            flip = side if step == 1 else 0
            forward, backward = ring_pairs(rows, 1, flip), ring_pairs(rows, -1, flip)
            if step < top or side == 0:
                up[side] = lax.ppermute(up[side], "rows", forward)
                sources.append(up[side])
                wanted.append((-step, side))
            if step < top or side == 1:
                down[side] = lax.ppermute(down[side], "rows", backward)
                sources.append(down[side])
                wanted.append((step, side))

    turned, ws_all, wn_all, bias_all, x_all, cot_all = call(
        bind(unpack_kernel, feats), "unpack",
        [((every, 2 * every), narrow), ((every, every), narrow), ((every, every), narrow),
         ((every, 1), wide), ((every, span), narrow), ((every, span), narrow)],
        [VMEM] * feats, [VMEM] * 6, [pltpu.VMEM((2 * every, every), wide)], 8, 0,
        4 * every * packed, *packs,
    )

    count = len(sources)

    def aggregate(parts):
        n = len(parts)
        outs = call(
            bind(aggregate_kernel, (feats, parts, tuple(wanted), rows)), "aggregate",
            [((half, span), narrow)] * (2 * n) + [((n, 1, span), wide)],
            [SMEM] * 2 + [HBM] * (2 + count), [VMEM] * (2 * n + 1),
            [
                pltpu.VMEM((rows, half, width), narrow),
                pltpu.VMEM((n, blocks // feats, 2, per_block, tile, tile), narrow),
                pltpu.SemaphoreType.DMA((count,)),
                pltpu.SemaphoreType.DMA((n, blocks // feats, 2)),
            ],
            WHOLE, 2 * hid * adjacency.size, 2 * adjacency.size + rows * hid * width,
            table, table_pair, adjacency, pair, *sources,
        )
        return outs[:n], outs[n : 2 * n], outs[2 * n]

    def send(value, k, flip):
        pairs = [
            (r * feats + i, (r ^ flip) * feats + (i + k) % feats)
            for r in range(rows)
            for i in range(feats)
        ]
        return lax.ppermute(value, ("rows", "feat"), pairs)

    there, there_far, unused_inverse = aggregate(tuple(range(1, feats)))
    near = [send(there[k - 1], k, 0) for k in range(1, feats)]
    far = [send(there_far[k - 1], k, 1) for k in range(1, feats)]
    here, here_far, inverse = aggregate((0,))
    near, far = [here[0]] + near, [send(here_far[0], 0, 1)] + far

    outs = call(
        bind(middle_kernel, (feats, hid, span, min(span, 256))), "middle",
        [((hid, span), narrow)] * (2 * feats) + [((every, span), narrow)] * 2,
        [VMEM] * (6 + 2 * feats), [VMEM] * (2 * feats + 2), [], 12,
        6 * every * every * span, 14 * every * span,
        turned, wn_all, bias_all, inverse, x_all, cot_all, *near, *far,
    )
    scaled, acts, grad, agg = outs[:feats], outs[feats : 2 * feats], outs[-2], outs[-1]
    scaled = exchange(scaled, feats)
    scaled_pair = [swap(piece, rows) for piece in scaled]

    outs = call(
        bind(weights_kernel, feats), "weights",
        [((hid, span), wide)] + [((hid, 3 * span), narrow)] * (feats - 1)
        + [((4, hid + 8, every // 2), wide)] * feats,
        [VMEM] * (4 + feats), [VMEM] * (2 * feats), [], 12,
        6 * every * every * span, 10 * every * span,
        ws_all, x_all, agg, grad, *acts,
    )
    parcels, grads = outs[:feats], outs[feats:]

    (held,) = call(
        bind(arrange_kernel, feats, tile), "arrange", [((2, blocks + 1, hid, tile), narrow)],
        [VMEM] * (2 * feats), [VMEM], [], 8, 0, 8 * hid * width, *scaled, *scaled_pair,
    )

    def spread(offsets, kinds):
        n = 2 * CAP * len(offsets)
        return call(
            bind(spread_kernel, (rows, offsets, kinds)), "spread",
            [((half, width), kind) for kind in kinds],
            [SMEM] * 2 + [HBM] * 2 + [VMEM], [VMEM] * len(kinds),
            [
                pltpu.VMEM((hid, width), wide),
                pltpu.VMEM((n, tile, tile), narrow),
                pltpu.SemaphoreType.DMA((n,)),
            ],
            12, 2 * n * hid * tile * tile, 8 * hid * width * len(offsets),
            table, table_pair, adjacency, pair, held,
        )

    up, down = [None, None], [None, None]

    def joined(arrived, mine):
        if arrived is None:
            return mine
        return (arrived.astype(jnp.float32) + mine).astype(jnp.bfloat16)

    for level in range(top, 0, -1):
        if level == top:
            low, high = spread((top,), (narrow, narrow))
            grads, low = lax.optimization_barrier((grads, low))
            up[0] = lax.ppermute(low, "rows", forward)
            down[1] = lax.ppermute(high, "rows", backward)
            continue
        kinds = tuple(narrow if arrived is None else wide for arrived in up + down)
        offsets = (level, -level)
        if level == 1:
            offsets, kinds = (1, -1, 0), kinds + (wide, wide)
        mine = spread(offsets, kinds)
        up = [lax.ppermute(joined(up[i], mine[i]), "rows", forward) for i in range(2)]
        down = [lax.ppermute(joined(down[i], mine[2 + i]), "rows", backward) for i in range(2)]

    grads = exchange(grads, feats)
    grads = sum(grads[1:], grads[0])
    grads = grads[:2] + swap(grads[2:], rows, 1)
    grads = grads[0] + swap(grads[1], rows, 2)
    bit = 4
    while bit < rows:
        grads = grads + swap(grads, rows, bit)
        bit *= 2
    near = jnp.stack([grads, swap(grads, rows, 2)])
    far = swap(near, rows, 1)
    far, parcels = lax.optimization_barrier((far, parcels))
    parcels = exchange(parcels, feats)
    grad_self, grad_neigh, sums = call(
        collect_kernel, "collect",
        [((hid, every), wide), ((hid, every), wide), ((8, every), wide)],
        [VMEM] * 2, [VMEM] * 3, [], 8, 0, 16 * hid * every, near, far,
    )
    grad_bias = lax.dynamic_slice_in_dim(sums[0], lax.axis_index("feat") * hid, hid)
    (activation,) = call(
        bind(place_kernel, feats), "place", [((hid, width), narrow)], [VMEM] * feats, [VMEM], [], 8,
        0, 4 * hid * width, acts[0], *parcels[1:],
    )
    (grad_features,) = call(
        bind(finish_kernel, feats), "finish", [((hid, width), narrow)], [VMEM] * (6 + feats),
        [VMEM], [], 8, 0, 8 * hid * width,
        mine[4], mine[5], up[0], down[0], up[1], down[1], *parcels,
    )
    return (activation, grad_features, grad_self, grad_neigh, grad_bias)


def solution(mesh):
    in_specs = (
        P("feat", "rows"),
        P("rows", None, None, None),
        P("rows", None),
        P("feat", None),
        P("feat", None),
        P("feat"),
        P("feat", "rows"),
    )
    out_specs = (P("feat", "rows"), P("feat", "rows"), P("feat", None), P("feat", None), P("feat"))
    body = functools.partial(shards, mesh.shape["rows"], mesh.shape["feat"])
    return jax.shard_map(body, mesh=mesh, in_specs=in_specs, out_specs=out_specs, check_vma=False)
```

```python
import functools

import jax
import jax.numpy as jnp
from jax import lax
from jax.experimental import pallas as pl
from jax.experimental.pallas import tpu as pltpu
from jax.sharding import PartitionSpec as P

CAP = 12
MIB = 1024 * 1024
HBM = pl.BlockSpec(memory_space=pltpu.HBM)
VMEM = pl.BlockSpec(memory_space=pltpu.VMEM)
SMEM = pl.BlockSpec(memory_space=pltpu.SMEM)
LAST = (((1,), (1,)), ((), ()))


def params(mib):
    return pltpu.CompilerParams(vmem_limit_bytes=mib * MIB)


def cost(flops, moved):
    return pl.CostEstimate(flops=flops, bytes_accessed=moved, transcendentals=0)


def product(left, right, dims=(((1,), (0,)), ((), ()))):
    return lax.dot_general(left, right, dims, preferred_element_type=jnp.float32)


def ring_pairs(rows, step, flip=0):
    levels, chips = rows // 4, rows // 2
    order = [2 * z for z in range(levels)] + [2 * z + 1 for z in reversed(range(levels))]
    return [
        (2 * order[p] + core, 2 * order[(p + step) % chips] + (core ^ flip))
        for p in range(chips)
        for core in range(2)
    ]


def ring_row(row, offset, rows):
    levels, chips = rows // 4, rows // 2
    z, x, core = row // 4, lax.rem(row // 2, 2), lax.rem(row, 2)
    target = lax.rem(jnp.where(x == 0, z, chips - 1 - z) + (offset + chips), chips)
    low = target < levels
    return 2 * jnp.where(low, 2 * target, 2 * (chips - 1 - target) + 1) + core


def swap(value, rows, bit=1):
    return lax.ppermute(value, "rows", [(r, r ^ bit) for r in range(rows)])


def exchange(pieces, feats):
    got = [pieces[0]]
    for k in range(1, feats):
        got.append(lax.ppermute(pieces[k], "feat", [(i, (i + k) % feats) for i in range(feats)]))
    return got


def after(value, *others):
    return lax.optimization_barrier((value, *others))[0]


def ahead(k, feats, size):
    return pl.multiple_of(lax.rem(lax.axis_index("feat") + k, feats) * size, size)


def behind(k, feats, size):
    return pl.multiple_of(lax.rem(lax.axis_index("feat") - k + feats, feats) * size, size)


def pack_kernel(feats, feature, grad_output, ws, wn, bias, *refs):
    outs, (parts, sems) = refs[:feats], refs[feats:]
    hid, every = ws.shape
    span = feature.shape[1] // feats
    copies = []
    for k in range(feats):
        at = pl.ds(ahead(k, feats, span), span)
        for source, low, size in (
            (feature.at[:, at], 0, span),
            (grad_output.at[:, at], span, span),
            (ws, 2 * span, every),
            (wn, 2 * span + every, every),
            (parts, 2 * span + 2 * every, 128),
        ):
            place = outs[k].at[:, pl.ds(low, size)]
            copies.append(pltpu.make_async_copy(source, place, sems.at[len(copies)]))
    line = lax.broadcasted_iota(jnp.int32, (hid, hid), 0)
    lane = lax.broadcasted_iota(jnp.int32, (hid, hid), 1)
    column = jnp.sum(jnp.where(line == lane, bias[...], 0.0), axis=1, keepdims=True)
    high = column.astype(jnp.bfloat16).astype(jnp.float32)
    middle = (column - high).astype(jnp.bfloat16).astype(jnp.float32)
    low = column - high - middle
    at = lax.broadcasted_iota(jnp.int32, (hid, 128), 1)
    value = jnp.where(at == 0, high, jnp.where(at == 1, middle, jnp.where(at == 2, low, 0.0)))
    parts[...] = value.astype(jnp.bfloat16)
    for copy in copies:
        copy.start()
    for copy in copies:
        copy.wait()


def unpack_kernel(feats, *refs):
    packs, (turned, ws_all, wn_all, bias_all, x_all, cot_all, both) = refs[:feats], refs[feats:]
    hid, span = packs[0].shape[0], x_all.shape[1]
    every = feats * hid
    for k in range(feats):
        at = pl.ds(behind(k, feats, hid), hid)
        pack = packs[k]
        x_all[at] = pack[:, :span]
        cot_all[at] = pack[:, span : 2 * span]
        ws_all[at] = pack[:, 2 * span : 2 * span + every]
        wn_all[at] = pack[:, 2 * span + every : 2 * span + 2 * every]
        parts = pack[:, 2 * span + 2 * every :].astype(jnp.float32)
        bias_all[at] = jnp.sum(parts, axis=1, keepdims=True)
    both[:every] = ws_all[...].astype(jnp.float32)
    both[every:] = wn_all[...].astype(jnp.float32)
    turned[...] = both[...].T.astype(jnp.bfloat16)


def table_kernel(cols, table, counts):
    blocks, per_block = cols.shape
    base = blocks * per_block
    groups = counts.shape[0]

    def clear(i, carry):
        counts[i] = 0
        for s in range(CAP):
            table[base + i * CAP + s] = -1
        return carry

    lax.fori_loop(0, groups, clear, 0)

    def step(block, carry):
        for t in range(per_block):
            col = cols[block, t]
            group = col // blocks
            seen = counts[group]
            counts[group] = seen + 1
            index = block * per_block + t
            table[index] = col
            table[base + group * CAP + seen] = index * 256 + (col - group * blocks)
        return carry

    lax.fori_loop(0, blocks, step, 0)


def load_kernel(source, out, sem):
    copy = pltpu.make_async_copy(source, out, sem)
    copy.start()
    copy.wait()


def aggregate_kernel(plan, table, table_pair, adj, pair, *refs):
    feats, parts, wanted, rows = plan
    count, taken = len(wanted), len(parts)
    blocks, per_block, tile, unused = adj.shape
    part = blocks // feats
    half = refs[0].shape[0]
    sources, refs = refs[:count], refs[count:]
    near, far, inverse, (held, sems) = (
        refs[:taken],
        refs[taken : 2 * taken],
        refs[2 * taken],
        refs[2 * taken + 1 :],
    )
    row = lax.axis_index("rows")
    copies = []
    for n, (offset, side) in enumerate(wanted):
        place = ring_row(row, offset, rows)
        if side:
            place = place + 1 - 2 * lax.rem(place, 2)
        copies.append(pltpu.make_async_copy(sources[n], held.at[place], sems.at[n]))

    for copy in copies:
        copy.start()
    for copy in copies:
        copy.wait()
    ones = jnp.ones((16, 2 * tile), jnp.bfloat16)
    for slot in range(taken):
        where = lax.rem(lax.axis_index("feat") + parts[slot], feats)

        def step(local, carry):
            lane = pl.ds(pl.multiple_of(local * tile, tile), tile)
            for side in range(2):
                block = where * part + local
                first = block * per_block
                total = None
                for t in range(0, per_block, 2):
                    left, right = [], []
                    for u in (t, t + 1):
                        col = (table, table_pair)[side][first + u]
                        source = col // blocks
                        at = pl.multiple_of((col - source * blocks) * tile, tile)
                        left.append(held[source, :, pl.ds(at, tile)])
                        right.append((adj, pair)[side][block, u])
                    term = product(
                        jnp.concatenate([jnp.concatenate(left, axis=1), ones], axis=0),
                        jnp.concatenate(right, axis=1),
                        LAST,
                    )
                    total = term if total is None else total + term
                factor = 1.0 / total[half : half + 1]
                value = (total[:half] * factor).astype(jnp.bfloat16)
                (near, far)[side][slot][:, lane] = value
                if side == 0:
                    inverse[slot, :, lane] = factor
            return carry

        lax.fori_loop(0, part, step, 0, unroll=2 if part % 2 == 0 else 1)


def middle_kernel(plan, turned, wn, bias, inverse, x_all, cot, *refs):
    feats, hid, span, chunk = plan
    near, far, refs = refs[:feats], refs[feats : 2 * feats], refs[2 * feats :]
    scaled, acts, grad, agg = refs[:feats], refs[feats : 2 * feats], refs[2 * feats], refs[2 * feats + 1]
    half = hid // 2
    core = lax.rem(lax.axis_index("rows"), 2)
    for k in range(feats):
        base = behind(k, feats, hid)
        agg[pl.ds(pl.multiple_of(base + core * half, half), half)] = near[k][...]
        agg[pl.ds(pl.multiple_of(base + (1 - core) * half, half), half)] = far[k][...]
    every = feats * hid
    for c in range(0, span, chunk):
        lane = pl.ds(c, chunk)
        for k in range(feats):
            at = pl.ds(ahead(k, feats, hid), hid)
            pre = product(turned[at, :every], x_all[:, lane])
            pre = pre + product(turned[at, every:], agg[:, lane]) + bias[at]
            slope = jnp.exp(jnp.minimum(pre, 0.0))
            acts[k][:, lane] = jnp.where(pre > 0, pre, slope - 1.0).astype(jnp.bfloat16)
            grad[at, lane] = (cot[at, lane].astype(jnp.float32) * slope).astype(jnp.bfloat16)
        for k in range(feats):
            at = pl.ds(ahead(k, feats, hid), hid)
            back = product(wn[at], grad[:, lane])
            scaled[k][:, lane] = (back * inverse[0, :, lane]).astype(jnp.bfloat16)


def own_quarter():
    row = lax.axis_index("rows")
    return 2 * lax.rem(row, 2) + lax.rem(row // 2, 2)


def turned_quarter(mine, index):
    both = (index // 2, index % 2)
    core = both[0] + mine // 2 - 2 * both[0] * (mine // 2)
    x = both[1] + lax.rem(mine, 2) - 2 * both[1] * lax.rem(mine, 2)
    return 2 * core + x


def weights_kernel(feats, ws, x_all, agg, grad, *refs):
    acts, (first, *sent), grads = refs[:feats], refs[feats : 2 * feats], refs[2 * feats :]
    every, span = grad.shape
    hid = every // feats
    wide = every // 2
    mine = own_quarter()
    g = grad[...]
    sums = product(jnp.ones((8, span), jnp.bfloat16), g, LAST)
    for k in range(feats):
        at = pl.ds(ahead(k, feats, hid), hid)
        own = product(ws[at], g)
        if k == 0:
            first[...] = own
        else:
            high = own.astype(jnp.bfloat16)
            sent[k - 1][:, :span] = acts[k][...]
            sent[k - 1][:, span : 2 * span] = high
            sent[k - 1][:, 2 * span :] = (own - high.astype(jnp.float32)).astype(jnp.bfloat16)
        values = [product(x_all[at], g, LAST), product(agg[at], g, LAST)]
        for quarter in range(4):
            slot = turned_quarter(mine, quarter)
            lane = slice(quarter % 2 * wide, (quarter % 2 + 1) * wide)
            grads[k][slot, :hid] = values[quarter // 2][:, lane]
            grads[k][slot, hid:] = sums[:, lane]


def collect_kernel(pair, pair_far, grad_self, grad_neigh, sums):
    hid, every = grad_self.shape
    wide = every // 2
    mine = own_quarter()
    for slot in range(4):
        value = (pair, pair_far)[slot // 2][slot % 2]
        quarter = turned_quarter(mine, slot)
        for q, out in enumerate((grad_self, grad_self, grad_neigh, grad_neigh)):

            @pl.when(quarter == q)
            def _():
                lane = slice(q % 2 * wide, (q % 2 + 1) * wide)
                out[:, lane] = value[:hid]
                if q < 2:
                    sums[:, lane] = value[hid:]


def arrange_kernel(feats, tile, *refs):
    pieces, held = refs[:-1], refs[-1]
    hid, span = pieces[0].shape
    part = span // tile
    for side in range(2):
        held[side, feats * part] = jnp.zeros((hid, tile), jnp.bfloat16)
        for k in range(feats):
            base = lax.rem(lax.axis_index("feat") - k + feats, feats) * part
            for local in range(part):
                held[side, base + local] = pieces[side * feats + k][:, local * tile : (local + 1) * tile]


def spread_kernel(plan, table, table_pair, adj, pair, held, *refs):
    rows, offsets, kinds = plan
    results, total = refs[:-1], refs[-1]
    blocks, per_block, tile, unused = adj.shape
    half = total.shape[0] // 2
    row = lax.axis_index("rows")
    firsts = [blocks * per_block + ring_row(row, offset, rows) * CAP for offset in offsets]
    for d in range(len(offsets)):
        total[...] = jnp.zeros_like(total)
        for side, (slots, tiles) in enumerate(((table, adj), (table_pair, pair))):
            for s0 in range(0, CAP, 4):
                terms = []
                for s in range(s0, s0 + 4):
                    entry = slots[firsts[d] + s]
                    index = jnp.maximum(entry, 0) // 256
                    block = index // per_block
                    place = jnp.where(entry < 0, blocks, block)
                    lane = lax.rem(jnp.maximum(entry, 0), 256) * tile
                    term = product(held[side, place], tiles[block, index - block * per_block])
                    terms.append((pl.multiple_of(lane, tile), term))
                for lane, term in terms:
                    total[:, pl.ds(lane, tile)] += term
        if len(kinds) == 2 * len(offsets):
            for part in range(2):
                value = total[part * half : (part + 1) * half]
                results[2 * d + part][...] = value.astype(kinds[2 * d + part])
        else:
            results[d][...] = total[...]


def join_kernel(name, arrived, mine, out):
    half = mine.shape[0] // 2
    if arrived.shape[0] == half:
        lines = slice(0, half) if name == "low" else slice(half, 2 * half)
        rest = slice(half, 2 * half) if name == "low" else slice(0, half)
        out[rest] = mine[rest].astype(jnp.bfloat16)
    else:
        lines = slice(0, 2 * half)
    out[lines] = (arrived[...].astype(jnp.float32) + mine[lines]).astype(jnp.bfloat16)


def finish_kernel(feats, base, a, b, *refs):
    (own, *sent), out = refs[:feats], refs[feats]
    span = own.shape[1]
    for k in range(feats):
        nodes = pl.ds(behind(k, feats, span), span)
        if k == 0:
            value = own[...]
        else:
            value = sent[k - 1][:, span : 2 * span].astype(jnp.float32)
            value = value + sent[k - 1][:, 2 * span :].astype(jnp.float32)
        value = value + base[:, nodes] + a[:, nodes].astype(jnp.float32)
        out[:, nodes] = (value + b[:, nodes].astype(jnp.float32)).astype(jnp.bfloat16)


def place_kernel(feats, *refs):
    (own, *sent), out = refs[:feats], refs[feats]
    span = own.shape[1]
    out[:, pl.ds(behind(0, feats, span), span)] = own[...]
    for k in range(1, feats):
        out[:, pl.ds(behind(k, feats, span), span)] = sent[k - 1][:, :span]


def call(kernel, name, outs, ins, out_specs, scratch, mib, flops, moved, *args):
    return pl.pallas_call(
        kernel,
        out_shape=[jax.ShapeDtypeStruct(shape, kind) for shape, kind in outs],
        in_specs=ins,
        out_specs=out_specs,
        scratch_shapes=scratch,
        compiler_params=params(mib),
        cost_estimate=cost(flops, moved),
        name=name,
    )(*args)


def shards(rows, feats, features, adjacency, tile_cols, self_weight, neigh_weight, bias_vector, grad_output):
    hid, width = features.shape
    blocks, per_block, tile, unused = adjacency.shape
    half, span = hid // 2, width // feats
    every = hid * feats
    top = rows // 4
    narrow, wide = jnp.bfloat16, jnp.float32
    forward, backward = ring_pairs(rows, 1), ring_pairs(rows, -1)
    bind = functools.partial

    core = lax.rem(lax.axis_index("rows"), 2)
    mine = lax.dynamic_slice_in_dim(features, core * half, half)
    away = lax.dynamic_slice_in_dim(features, (1 - core) * half, half)
    sources, wanted = [mine], [(0, 0)]
    up, down = [mine, away], [mine, away]
    (table,) = call(
        table_kernel, "table", [((tile_cols.size + rows * CAP,), jnp.int32)], [SMEM], [SMEM],
        [pltpu.SMEM((rows,), jnp.int32)], 4, 0, 8 * rows * CAP, tile_cols,
    )
    packed = 2 * span + 2 * every + 128
    packs = call(
        bind(pack_kernel, feats), "pack", [((hid, packed), narrow)] * feats, [HBM] * 4 + [VMEM],
        [VMEM] * feats,
        [pltpu.VMEM((hid, 128), narrow), pltpu.SemaphoreType.DMA((5 * feats,))], 6, 0,
        4 * hid * packed * feats,
        features, grad_output, self_weight, neigh_weight, bias_vector.reshape(1, hid),
    )
    (tiles,) = call(
        load_kernel, "load", [(adjacency.shape, narrow)], [HBM], [VMEM],
        [pltpu.SemaphoreType.DMA], 4, 0, 4 * adjacency.size, adjacency,
    )
    for step in range(1, top + 1):
        if step == 2:
            down[1], tiles = lax.optimization_barrier((down[1], tiles))
            pair = swap(after(adjacency, up[0], down[0]), rows)
        if step == top - 1:
            up[0], pair, table, packs = lax.optimization_barrier((up[0], pair, table, packs))
            table_pair = swap(table, rows)
            packs = exchange(packs, feats)
        if step == top:
            sources.append(swap(after(away, up[0], down[0]), rows))
            wanted.append((0, 1))
        for side in range(2):
            flip = side if step == 1 else 0
            forward, backward = ring_pairs(rows, 1, flip), ring_pairs(rows, -1, flip)
            if step < top or side == 0:
                up[side] = lax.ppermute(up[side], "rows", forward)
                sources.append(up[side])
                wanted.append((-step, side))
            if step < top or side == 1:
                down[side] = lax.ppermute(down[side], "rows", backward)
                sources.append(down[side])
                wanted.append((step, side))

    turned, ws_all, wn_all, bias_all, x_all, cot_all = call(
        bind(unpack_kernel, feats), "unpack",
        [((every, 2 * every), narrow), ((every, every), narrow), ((every, every), narrow),
         ((every, 1), wide), ((every, span), narrow), ((every, span), narrow)],
        [VMEM] * feats, [VMEM] * 6, [pltpu.VMEM((2 * every, every), wide)], 8, 0,
        4 * every * packed, *packs,
    )

    count = len(sources)

    def aggregate(parts):
        n = len(parts)
        outs = call(
            bind(aggregate_kernel, (feats, parts, tuple(wanted), rows)), "aggregate",
            [((half, span), narrow)] * (2 * n) + [((n, 1, span), wide)],
            [SMEM] * 2 + [VMEM] * 2 + [HBM] * count, [VMEM] * (2 * n + 1),
            [pltpu.VMEM((rows, half, width), narrow), pltpu.SemaphoreType.DMA((count,))],
            12, 2 * hid * adjacency.size, 2 * adjacency.size + rows * hid * width,
            table, table_pair, tiles, pair, *sources,
        )
        return outs[:n], outs[n : 2 * n], outs[2 * n]

    def send(value, k, flip):
        pairs = [
            (r * feats + i, (r ^ flip) * feats + (i + k) % feats)
            for r in range(rows)
            for i in range(feats)
        ]
        return lax.ppermute(value, ("rows", "feat"), pairs)

    there, there_far, unused_inverse = aggregate(tuple(range(1, feats)))
    near = [send(there[k - 1], k, 0) for k in range(1, feats)]
    far = [send(there_far[k - 1], k, 1) for k in range(1, feats)]
    here, here_far, inverse = aggregate((0,))
    near, far = [here[0]] + near, [send(here_far[0], 0, 1)] + far

    outs = call(
        bind(middle_kernel, (feats, hid, span, min(span, 256))), "middle",
        [((hid, span), narrow)] * (2 * feats) + [((every, span), narrow)] * 2,
        [VMEM] * (6 + 2 * feats), [VMEM] * (2 * feats + 2), [], 12,
        6 * every * every * span, 14 * every * span,
        turned, wn_all, bias_all, inverse, x_all, cot_all, *near, *far,
    )
    scaled, acts, grad, agg = outs[:feats], outs[feats : 2 * feats], outs[-2], outs[-1]
    scaled = exchange(scaled, feats)
    scaled_pair = [swap(piece, rows) for piece in scaled]

    outs = call(
        bind(weights_kernel, feats), "weights",
        [((hid, span), wide)] + [((hid, 3 * span), narrow)] * (feats - 1)
        + [((4, hid + 8, every // 2), wide)] * feats,
        [VMEM] * (4 + feats), [VMEM] * (2 * feats), [], 12,
        6 * every * every * span, 10 * every * span,
        ws_all, x_all, agg, grad, *acts,
    )
    parcels, grads = outs[:feats], outs[feats:]

    (held,) = call(
        bind(arrange_kernel, feats, tile), "arrange", [((2, blocks + 1, hid, tile), narrow)],
        [VMEM] * (2 * feats), [VMEM], [], 8, 0, 8 * hid * width, *scaled, *scaled_pair,
    )

    def spread(offsets, halves=False):
        n = 2 * CAP * len(offsets)
        outs = [((half, width), narrow)] * 2 if halves else [((hid, width), wide)] * len(offsets)
        return call(
            bind(spread_kernel, (rows, offsets, tuple(kind for shape, kind in outs))), "spread", outs,
            [SMEM] * 2 + [VMEM] * 3, [VMEM] * len(outs), [pltpu.VMEM((hid, width), wide)],
            8, 2 * n * hid * tile * tile, 8 * hid * width * len(offsets),
            table, table_pair, tiles, pair, held,
        )

    forward, backward = ring_pairs(rows, 1), ring_pairs(rows, -1)
    low, high = spread((top,), True)
    grads, low = lax.optimization_barrier((grads, low))
    up, down = lax.ppermute(low, "rows", forward), lax.ppermute(high, "rows", backward)
    for level in range(top - 1, 0, -1):
        offsets = (level, -level, 0) if level == 1 else (level, -level)
        mine = spread(offsets)

        def joined(name, arrived, value):
            (out,) = call(
                bind(join_kernel, name), "join", [((hid, width), narrow)], [VMEM] * 2, [VMEM], [], 8,
                0, 8 * hid * width, arrived, value,
            )
            return out

        up = lax.ppermute(joined("low", up, mine[0]), "rows", forward)
        down = lax.ppermute(joined("high", down, mine[1]), "rows", backward)

    grads = exchange(grads, feats)
    first, parcels = lax.optimization_barrier((grads[-1], parcels))
    grads = grads[:-1] + [first]
    parcels = exchange(parcels, feats)
    grads = sum(grads[1:], grads[0])
    grads = grads[:2] + swap(grads[2:], rows, 1)
    grads = grads[0] + swap(grads[1], rows, 2)
    bit = 4
    while bit < rows:
        grads = grads + swap(grads, rows, bit)
        bit *= 2
    near = jnp.stack([grads, swap(grads, rows, 2)])
    far = swap(near, rows, 1)
    grad_self, grad_neigh, sums = call(
        collect_kernel, "collect",
        [((hid, every), wide), ((hid, every), wide), ((8, every), wide)],
        [VMEM] * 2, [VMEM] * 3, [], 8, 0, 16 * hid * every, near, far,
    )
    grad_bias = lax.dynamic_slice_in_dim(sums[0], lax.axis_index("feat") * hid, hid)
    (activation,) = call(
        bind(place_kernel, feats), "place", [((hid, width), narrow)], [VMEM] * feats, [VMEM], [], 8,
        0, 4 * hid * width, acts[0], *parcels[1:],
    )
    (grad_features,) = call(
        bind(finish_kernel, feats), "finish", [((hid, width), narrow)], [VMEM] * (3 + feats),
        [VMEM], [], 8, 0, 8 * hid * width, mine[2], up, down, *parcels,
    )
    return (activation, grad_features, grad_self, grad_neigh, grad_bias)


def solution(mesh):
    in_specs = (
        P("feat", "rows"),
        P("rows", None, None, None),
        P("rows", None),
        P("feat", None),
        P("feat", None),
        P("feat"),
        P("feat", "rows"),
    )
    out_specs = (P("feat", "rows"), P("feat", "rows"), P("feat", None), P("feat", None), P("feat"))
    body = functools.partial(shards, mesh.shape["rows"], mesh.shape["feat"])
    return jax.shard_map(body, mesh=mesh, in_specs=in_specs, out_specs=out_specs, check_vma=False)
```

```python
import functools

import jax
import jax.numpy as jnp
from jax import lax
from jax.experimental import pallas as pl
from jax.experimental.pallas import tpu as pltpu
from jax.sharding import PartitionSpec as P

CAP = 12
MIB = 1024 * 1024
HBM = pl.BlockSpec(memory_space=pltpu.HBM)
VMEM = pl.BlockSpec(memory_space=pltpu.VMEM)
SMEM = pl.BlockSpec(memory_space=pltpu.SMEM)
LAST = (((1,), (1,)), ((), ()))


def params(mib):
    return pltpu.CompilerParams(vmem_limit_bytes=mib * MIB)


def cost(flops, moved):
    return pl.CostEstimate(flops=flops, bytes_accessed=moved, transcendentals=0)


def product(left, right, dims=(((1,), (0,)), ((), ()))):
    return lax.dot_general(left, right, dims, preferred_element_type=jnp.float32)


def ring_pairs(rows, step, flip=0):
    levels, chips = rows // 4, rows // 2
    order = [2 * z for z in range(levels)] + [2 * z + 1 for z in reversed(range(levels))]
    return [
        (2 * order[p] + core, 2 * order[(p + step) % chips] + (core ^ flip))
        for p in range(chips)
        for core in range(2)
    ]


def ring_row(row, offset, rows):
    levels, chips = rows // 4, rows // 2
    z, x, core = row // 4, lax.rem(row // 2, 2), lax.rem(row, 2)
    target = lax.rem(jnp.where(x == 0, z, chips - 1 - z) + (offset + chips), chips)
    low = target < levels
    return 2 * jnp.where(low, 2 * target, 2 * (chips - 1 - target) + 1) + core


def swap(value, rows, bit=1):
    return lax.ppermute(value, "rows", [(r, r ^ bit) for r in range(rows)])


def send(value, k, flip, rows, feats):
    pairs = [
        (r * feats + i, (r ^ flip) * feats + (i + k) % feats)
        for r in range(rows)
        for i in range(feats)
    ]
    return lax.ppermute(value, ("rows", "feat"), pairs)


def after(value, *others):
    return lax.optimization_barrier((value, *others))[0]


def behind(k, feats, size):
    return pl.multiple_of(lax.rem(lax.axis_index("feat") - k + feats, feats) * size, size)


def pack_kernel(feature, grad_output, ws, wn, bias, out, parts, sems):
    hid, every = ws.shape
    width = feature.shape[1]
    copies = []
    for source, low, size in (
        (feature, 0, width),
        (grad_output, width, width),
        (ws, 2 * width, every),
        (wn, 2 * width + every, every),
        (parts, 2 * width + 2 * every, 128),
    ):
        place = out.at[:, pl.ds(low, size)]
        copies.append(pltpu.make_async_copy(source, place, sems.at[len(copies)]))
    line = lax.broadcasted_iota(jnp.int32, (hid, hid), 0)
    lane = lax.broadcasted_iota(jnp.int32, (hid, hid), 1)
    column = jnp.sum(jnp.where(line == lane, bias[...], 0.0), axis=1, keepdims=True)
    high = column.astype(jnp.bfloat16).astype(jnp.float32)
    middle = (column - high).astype(jnp.bfloat16).astype(jnp.float32)
    low = column - high - middle
    at = lax.broadcasted_iota(jnp.int32, (hid, 128), 1)
    value = jnp.where(at == 0, high, jnp.where(at == 1, middle, jnp.where(at == 2, low, 0.0)))
    parts[...] = value.astype(jnp.bfloat16)
    for copy in copies:
        copy.start()
    for copy in copies:
        copy.wait()


def prepare_kernel(feats, *refs):
    packs, (turned, cot_all, base), (weights, bias, x_all) = refs[:feats], refs[feats:-3], refs[-3:]
    hid, width = packs[0].shape[0], x_all.shape[1]
    every = feats * hid
    for k in range(feats):
        at = pl.ds(behind(k, feats, hid), hid)
        pack = packs[k]
        x_all[at] = pack[:, :width]
        cot_all[at] = pack[:, width : 2 * width]
        weights[at] = pack[:, 2 * width : 2 * width + 2 * every].astype(jnp.float32)
        parts = pack[:, 2 * width + 2 * every :].astype(jnp.float32)
        bias[at] = jnp.sum(parts, axis=1, keepdims=True)
    own = weights[:, :every].T.astype(jnp.bfloat16)
    turned[...] = weights[:, every:].T.astype(jnp.bfloat16)
    chunk = min(width, 512)
    for c in range(0, width, chunk):
        lane = pl.ds(c, chunk)
        base[:, lane] = product(own, x_all[:, lane]) + bias[...]


def table_kernel(cols, table, counts):
    blocks, per_block = cols.shape
    base = blocks * per_block
    groups = counts.shape[0]

    def clear(i, carry):
        counts[i] = 0
        for s in range(CAP):
            table[base + i * CAP + s] = -1
        return carry

    lax.fori_loop(0, groups, clear, 0)

    def step(block, carry):
        for t in range(per_block):
            col = cols[block, t]
            group = col // blocks
            seen = counts[group]
            counts[group] = seen + 1
            index = block * per_block + t
            table[index] = col
            table[base + group * CAP + seen] = index * 256 + (col - group * blocks)
        return carry

    lax.fori_loop(0, blocks, step, 0)


def load_kernel(source, out, sem):
    copy = pltpu.make_async_copy(source, out, sem)
    copy.start()
    copy.wait()


def aggregate_kernel(wanted, rows, table, tiles, *refs):
    count = len(wanted)
    blocks, per_block, tile, unused = tiles.shape
    half = refs[0].shape[0]
    sources, (out, inverse, held, sems) = refs[:count], refs[count:]
    row = lax.axis_index("rows")
    copies = []
    for n, (offset, side) in enumerate(wanted):
        place = ring_row(row, offset, rows)
        if side:
            place = place + 1 - 2 * lax.rem(place, 2)
        copies.append(pltpu.make_async_copy(sources[n], held.at[place], sems.at[n]))
    for copy in copies:
        copy.start()
    for copy in copies:
        copy.wait()
    ones = jnp.ones((16, 2 * tile), jnp.bfloat16)

    def step(block, carry):
        total = None
        for t in range(0, per_block, 2):
            left, right = [], []
            for u in (t, t + 1):
                col = table[block * per_block + u]
                source = col // blocks
                at = pl.multiple_of((col - source * blocks) * tile, tile)
                left.append(held[source, :, pl.ds(at, tile)])
                right.append(tiles[block, u])
            term = product(
                jnp.concatenate([jnp.concatenate(left, axis=1), ones], axis=0),
                jnp.concatenate(right, axis=1),
                LAST,
            )
            total = term if total is None else total + term
        factor = 1.0 / total[half : half + 1]
        lane = pl.ds(pl.multiple_of(block * tile, tile), tile)
        out[:, lane] = (total[:half] * factor).astype(jnp.bfloat16)
        inverse[:, lane] = factor
        return carry

    lax.fori_loop(0, blocks, step, 0, unroll=4)


def middle_kernel(feats, turned, wn, inverse, base, cot, *refs):
    near, far, refs = refs[:feats], refs[feats : 2 * feats], refs[2 * feats :]
    act, grad, scaled, agg_own, agg, value = refs
    hid, width = act.shape
    half = hid // 2
    core = lax.rem(lax.axis_index("rows"), 2)
    for k in range(feats):
        first = behind(k, feats, hid)
        agg[pl.ds(pl.multiple_of(first + core * half, half), half)] = near[k][...]
        agg[pl.ds(pl.multiple_of(first + (1 - core) * half, half), half)] = far[k][...]
    own = pl.ds(behind(0, feats, hid), hid)
    agg_own[...] = agg[own]
    chunk = min(width, 256)
    for c in range(0, width, chunk):
        lane = pl.ds(c, chunk)
        pre = product(turned[...], agg[:, lane]) + base[:, lane]
        slope = jnp.exp(jnp.minimum(pre, 0.0))
        grad[:, lane] = (cot[:, lane].astype(jnp.float32) * slope).astype(jnp.bfloat16)
        value[...] = jnp.where(pre > 0, pre, slope - 1.0)
        back = product(wn[...], grad[:, lane])
        scaled[:, lane] = (back * inverse[:, lane]).astype(jnp.bfloat16)
        act[:, lane] = value[own].astype(jnp.bfloat16)


def weights_kernel(ws, x_own, agg_own, grad, self_own, sums):
    hid, every = ws.shape
    g = grad[...]
    self_own[...] = product(ws[...], g)
    sums[:hid, :every] = product(x_own[...], g, LAST)
    sums[:hid, every:] = product(agg_own[...], g, LAST)
    total = product(jnp.ones((8, g.shape[1]), jnp.bfloat16), g, LAST)
    sums[hid:, :every] = total
    sums[hid:, every:] = total


def arrange_kernel(own, other, held):
    hid, tile = held.shape[2:]
    blocks = held.shape[1] - 1
    for side, source in enumerate((own, other)):
        held[side, blocks] = jnp.zeros((hid, tile), jnp.bfloat16)
        for block in range(blocks):
            held[side, block] = source[:, block * tile : (block + 1) * tile]


def spread_kernel(plan, table, table_pair, adj, pair, held, *refs):
    rows, offsets, kinds = plan
    results, total = refs[:-1], refs[-1]
    blocks, per_block, tile, unused = adj.shape
    half = total.shape[0] // 2
    row = lax.axis_index("rows")
    firsts = [blocks * per_block + ring_row(row, offset, rows) * CAP for offset in offsets]
    for d in range(len(offsets)):
        total[...] = jnp.zeros_like(total)
        for side, (slots, tiles) in enumerate(((table, adj), (table_pair, pair))):
            for s0 in range(0, CAP, 4):
                terms = []
                for s in range(s0, s0 + 4):
                    entry = slots[firsts[d] + s]
                    index = jnp.maximum(entry, 0) // 256
                    block = index // per_block
                    place = jnp.where(entry < 0, blocks, block)
                    lane = lax.rem(jnp.maximum(entry, 0), 256) * tile
                    term = product(held[side, place], tiles[block, index - block * per_block])
                    terms.append((pl.multiple_of(lane, tile), term))
                for lane, term in terms:
                    total[:, pl.ds(lane, tile)] += term
        for part in range(2):
            value = total[part * half : (part + 1) * half]
            results[2 * d + part][...] = value.astype(kinds[2 * d + part])


def join_kernel(arrived, mine, out):
    out[...] = (arrived[...].astype(jnp.float32) + mine[...]).astype(jnp.bfloat16)


def finish_kernel(own, base_low, base_high, a_low, b_low, a_high, b_high, out):
    half = a_low.shape[0]
    for part, (base, a, b) in enumerate(((base_low, a_low, b_low), (base_high, a_high, b_high))):
        lines = slice(part * half, (part + 1) * half)
        value = own[lines] + base[...] + a[...].astype(jnp.float32)
        out[lines] = (value + b[...].astype(jnp.float32)).astype(jnp.bfloat16)


def call(kernel, name, outs, ins, out_specs, scratch, mib, flops, moved, *args):
    return pl.pallas_call(
        kernel,
        out_shape=[jax.ShapeDtypeStruct(shape, kind) for shape, kind in outs],
        in_specs=ins,
        out_specs=out_specs,
        scratch_shapes=scratch,
        compiler_params=params(mib),
        cost_estimate=cost(flops, moved),
        name=name,
    )(*args)


def shards(rows, feats, features, adjacency, tile_cols, self_weight, neigh_weight, bias_vector, grad_output):
    hid, width = features.shape
    blocks, per_block, tile, unused = adjacency.shape
    half = hid // 2
    every = hid * feats
    top = rows // 4
    narrow, wide = jnp.bfloat16, jnp.float32
    bind = functools.partial

    core = lax.rem(lax.axis_index("rows"), 2)
    mine = lax.dynamic_slice_in_dim(features, core * half, half)
    away = lax.dynamic_slice_in_dim(features, (1 - core) * half, half)
    sources, wanted = [mine], [(0, 0)]
    up, down = [mine, away], [mine, away]
    pair = swap(adjacency, rows)
    (table,) = call(
        table_kernel, "table", [((tile_cols.size + rows * CAP,), jnp.int32)], [SMEM], [SMEM],
        [pltpu.SMEM((rows,), jnp.int32)], 4, 0, 8 * rows * CAP, tile_cols,
    )
    packed = 2 * width + 2 * every + 128
    (pack,) = call(
        pack_kernel, "pack", [((hid, packed), narrow)], [HBM] * 4 + [VMEM], [VMEM],
        [pltpu.VMEM((hid, 128), narrow), pltpu.SemaphoreType.DMA((5,))], 6, 0,
        4 * hid * packed,
        features, grad_output, self_weight, neigh_weight, bias_vector.reshape(1, hid),
    )
    (tiles,) = call(
        load_kernel, "load", [(adjacency.shape, narrow)], [HBM], [VMEM],
        [pltpu.SemaphoreType.DMA], 4, 0, 4 * adjacency.size, adjacency,
    )
    for step in range(1, top + 1):
        if step == 2:
            up, down, pair, table, pack = lax.optimization_barrier((up, down, pair, table, pack))
            table_pair = swap(table, rows)
            packs = [pack] + [send(pack, k, 0, rows, feats) for k in range(1, feats)]
        if step == top:
            sources.append(swap(after(away, up[0], down[0], tiles), rows))
            wanted.append((0, 1))
        for side in range(2):
            flip = side if step == 1 else 0
            forward, backward = ring_pairs(rows, 1, flip), ring_pairs(rows, -1, flip)
            if step < top or side == 0:
                up[side] = lax.ppermute(up[side], "rows", forward)
                sources.append(up[side])
                wanted.append((-step, side))
            if step < top or side == 1:
                down[side] = lax.ppermute(down[side], "rows", backward)
                sources.append(down[side])
                wanted.append((step, side))

    def aggregate(columns, values):
        return call(
            bind(aggregate_kernel, tuple(wanted), rows), "aggregate",
            [((half, width), narrow), ((1, width), wide)],
            [SMEM, VMEM] + [HBM] * len(sources), [VMEM] * 2,
            [pltpu.VMEM((rows, half, width), narrow), pltpu.SemaphoreType.DMA((len(sources),))],
            12, hid * adjacency.size, 2 * adjacency.size + rows * hid * width,
            columns, values, *sources,
        )

    value, unused_inverse = aggregate(table_pair, pair)
    far = [send(value, k, 1, rows, feats) for k in reversed(range(feats))][::-1]
    value, inverse = aggregate(table, tiles)
    near = [value] + [send(value, k, 0, rows, feats) for k in range(1, feats)]

    turned, cot_all, base = call(
        bind(prepare_kernel, feats), "prepare",
        [((every, every), narrow), ((every, width), narrow), ((every, width), wide)],
        [VMEM] * feats, [VMEM] * 3,
        [
            pltpu.VMEM((every, 2 * every), wide),
            pltpu.VMEM((every, 1), wide),
            pltpu.VMEM((every, width), narrow),
        ],
        12, 2 * every * every * width, 4 * every * packed, *packs,
    )
    activation, grad, scaled, agg_own = call(
        bind(middle_kernel, feats), "middle",
        [((hid, width), narrow), ((every, width), narrow)] + [((hid, width), narrow)] * 2,
        [VMEM] * (5 + 2 * feats), [VMEM] * 4,
        [pltpu.VMEM((every, width), narrow), pltpu.VMEM((every, min(width, 256)), wide)], 12,
        3 * every * every * width, 14 * every * width,
        turned, neigh_weight, inverse, base, cot_all, *near, *far,
    )
    scaled_pair = swap(scaled, rows)
    self_own, sums = call(
        weights_kernel, "weights", [((hid, width), wide), ((hid + 8, 2 * every), wide)],
        [VMEM] * 4, [VMEM] * 2, [], 12, 6 * hid * every * width, 10 * every * width,
        self_weight, features, agg_own, grad,
    )
    (held,) = call(
        arrange_kernel, "arrange", [((2, blocks + 1, hid, tile), narrow)],
        [VMEM] * 2, [VMEM], [], 8, 0, 8 * hid * width, scaled, scaled_pair,
    )

    def spread(offsets, kinds):
        n = 2 * CAP * len(offsets)
        return call(
            bind(spread_kernel, (rows, offsets, kinds)), "spread",
            [((half, width), kind) for kind in kinds],
            [SMEM] * 2 + [VMEM] * 3, [VMEM] * len(kinds), [pltpu.VMEM((hid, width), wide)],
            8, 2 * n * hid * tile * tile, 8 * hid * width * len(offsets),
            table, table_pair, tiles, pair, held,
        )

    def joined(arrived, mine):
        if arrived is None:
            return mine
        (out,) = call(
            join_kernel, "join", [((half, width), narrow)], [VMEM] * 2, [VMEM], [], 8,
            0, 4 * hid * width, arrived, mine,
        )
        return out

    up, down = [None, None], [None, None]
    forward, backward = ring_pairs(rows, 1), ring_pairs(rows, -1)
    for level in range(top, 0, -1):
        if level == top:
            low, high = spread((top,), (narrow, narrow))
            up[0] = lax.ppermute(low, "rows", forward)
            down[1] = lax.ppermute(high, "rows", backward)
            continue
        kinds = tuple(narrow if arrived is None else wide for arrived in up + down)
        offsets = (level, -level)
        if level == 1:
            offsets, kinds = (1, -1, 0), kinds + (wide, wide)
        mine = spread(offsets, kinds)
        if level == top // 2:
            marker = joined(down[1], mine[3])
            mine = list(mine[:3]) + [marker]
            down[1] = None
        up = [lax.ppermute(joined(up[i], mine[i]), "rows", forward) for i in range(2)]
        down = [lax.ppermute(joined(down[i], mine[2 + i]), "rows", backward) for i in range(2)]
    planes = [[4 * z + i for i in range(4)] for z in range(rows // 4)]
    lines = [[4 * z + i for z in range(rows // 4)] for i in range(4)]
    sums = after(lax.psum(sums, "rows", axis_index_groups=planes), marker)
    sums = lax.psum(sums, "rows", axis_index_groups=lines)
    grad_self, grad_neigh = sums[:hid, :every], sums[:hid, every:]
    grad_bias = lax.dynamic_slice_in_dim(sums[hid, :every], lax.axis_index("feat") * hid, hid)
    (grad_features,) = call(
        finish_kernel, "finish", [((hid, width), narrow)], [VMEM] * 7, [VMEM], [], 8, 0,
        8 * hid * width, self_own, mine[4], mine[5], up[0], down[0], up[1], down[1],
    )
    return (activation, grad_features, grad_self, grad_neigh, grad_bias)


def solution(mesh):
    in_specs = (
        P("feat", "rows"),
        P("rows", None, None, None),
        P("rows", None),
        P("feat", None),
        P("feat", None),
        P("feat"),
        P("feat", "rows"),
    )
    out_specs = (P("feat", "rows"), P("feat", "rows"), P("feat", None), P("feat", None), P("feat"))
    body = functools.partial(shards, mesh.shape["rows"], mesh.shape["feat"])
    return jax.shard_map(body, mesh=mesh, in_specs=in_specs, out_specs=out_specs, check_vma=False)
```

```python
import functools

import jax
import jax.numpy as jnp
from jax import lax
from jax.experimental import pallas as pl
from jax.experimental.pallas import tpu as pltpu
from jax.sharding import PartitionSpec as P

CAP = 12
MIB = 1024 * 1024
HBM = pl.BlockSpec(memory_space=pltpu.HBM)
VMEM = pl.BlockSpec(memory_space=pltpu.VMEM)
SMEM = pl.BlockSpec(memory_space=pltpu.SMEM)
LAST = (((1,), (1,)), ((), ()))


def params(mib):
    return pltpu.CompilerParams(vmem_limit_bytes=mib * MIB)


def cost(flops, moved):
    return pl.CostEstimate(flops=flops, bytes_accessed=moved, transcendentals=0)


def product(left, right, dims=(((1,), (0,)), ((), ()))):
    return lax.dot_general(left, right, dims, preferred_element_type=jnp.float32)


def ring_pairs(rows, step, flip=0):
    levels, chips = rows // 4, rows // 2
    order = [2 * z for z in range(levels)] + [2 * z + 1 for z in reversed(range(levels))]
    return [
        (2 * order[p] + core, 2 * order[(p + step) % chips] + (core ^ flip))
        for p in range(chips)
        for core in range(2)
    ]


def ring_row(row, offset, rows):
    levels, chips = rows // 4, rows // 2
    z, x, core = row // 4, lax.rem(row // 2, 2), lax.rem(row, 2)
    target = lax.rem(jnp.where(x == 0, z, chips - 1 - z) + (offset + chips), chips)
    low = target < levels
    return 2 * jnp.where(low, 2 * target, 2 * (chips - 1 - target) + 1) + core


def swap(value, rows, bit=1):
    return lax.ppermute(value, "rows", [(r, r ^ bit) for r in range(rows)])


def send(value, k, flip, rows, feats):
    pairs = [
        (r * feats + i, (r ^ flip) * feats + (i + k) % feats)
        for r in range(rows)
        for i in range(feats)
    ]
    return lax.ppermute(value, ("rows", "feat"), pairs)


def after(value, *others):
    return lax.optimization_barrier((value, *others))[0]


def behind(k, feats, size):
    return pl.multiple_of(lax.rem(lax.axis_index("feat") - k + feats, feats) * size, size)


def pack_kernel(feature, grad_output, ws, wn, bias, out, parts, sems):
    hid, every = ws.shape
    width = feature.shape[1]
    copies = []
    for source, low, size in (
        (feature, 0, width),
        (grad_output, width, width),
        (ws, 2 * width, every),
        (wn, 2 * width + every, every),
        (parts, 2 * width + 2 * every, 128),
    ):
        place = out.at[:, pl.ds(low, size)]
        copies.append(pltpu.make_async_copy(source, place, sems.at[len(copies)]))
    line = lax.broadcasted_iota(jnp.int32, (hid, hid), 0)
    lane = lax.broadcasted_iota(jnp.int32, (hid, hid), 1)
    column = jnp.sum(jnp.where(line == lane, bias[...], 0.0), axis=1, keepdims=True)
    high = column.astype(jnp.bfloat16).astype(jnp.float32)
    middle = (column - high).astype(jnp.bfloat16).astype(jnp.float32)
    low = column - high - middle
    at = lax.broadcasted_iota(jnp.int32, (hid, 128), 1)
    value = jnp.where(at == 0, high, jnp.where(at == 1, middle, jnp.where(at == 2, low, 0.0)))
    parts[...] = value.astype(jnp.bfloat16)
    for copy in copies:
        copy.start()
    for copy in copies:
        copy.wait()


def prepare_kernel(feats, *refs):
    packs, (turned, cot_all, base), (weights, bias, x_all) = refs[:feats], refs[feats:-3], refs[-3:]
    hid, width = packs[0].shape[0], x_all.shape[1]
    every = feats * hid
    for k in range(feats):
        at = pl.ds(behind(k, feats, hid), hid)
        pack = packs[k]
        x_all[at] = pack[:, :width]
        cot_all[at] = pack[:, width : 2 * width]
        weights[at] = pack[:, 2 * width : 2 * width + 2 * every].astype(jnp.float32)
        parts = pack[:, 2 * width + 2 * every :].astype(jnp.float32)
        bias[at] = jnp.sum(parts, axis=1, keepdims=True)
    own = weights[:, :every].T.astype(jnp.bfloat16)
    turned[...] = weights[:, every:].T.astype(jnp.bfloat16)
    chunk = min(width, 512)
    for c in range(0, width, chunk):
        lane = pl.ds(c, chunk)
        base[:, lane] = product(own, x_all[:, lane]) + bias[...]


def table_kernel(cols, table, counts):
    blocks, per_block = cols.shape
    base = blocks * per_block
    groups = counts.shape[0]

    def clear(i, carry):
        counts[i] = 0
        for s in range(CAP):
            table[base + i * CAP + s] = -1
        return carry

    lax.fori_loop(0, groups, clear, 0)

    def step(block, carry):
        for t in range(per_block):
            col = cols[block, t]
            group = col // blocks
            seen = counts[group]
            counts[group] = seen + 1
            index = block * per_block + t
            table[index] = col
            table[base + group * CAP + seen] = index * 256 + (col - group * blocks)
        return carry

    lax.fori_loop(0, blocks, step, 0)


def load_kernel(source, out, sem):
    copy = pltpu.make_async_copy(source, out, sem)
    copy.start()
    copy.wait()


def aggregate_kernel(wanted, rows, table, tiles, *refs):
    count = len(wanted)
    blocks, per_block, tile, unused = tiles.shape
    half = refs[0].shape[0]
    sources, (out, inverse, held, sems) = refs[:count], refs[count:]
    row = lax.axis_index("rows")
    copies = []
    for n, (offset, side) in enumerate(wanted):
        place = ring_row(row, offset, rows)
        if side:
            place = place + 1 - 2 * lax.rem(place, 2)
        copies.append(pltpu.make_async_copy(sources[n], held.at[place], sems.at[n]))
    for copy in copies:
        copy.start()
    for copy in copies:
        copy.wait()
    ones = jnp.ones((16, 2 * tile), jnp.bfloat16)

    def step(block, carry):
        total = None
        for t in range(0, per_block, 2):
            left, right = [], []
            for u in (t, t + 1):
                col = table[block * per_block + u]
                source = col // blocks
                at = pl.multiple_of((col - source * blocks) * tile, tile)
                left.append(held[source, :, pl.ds(at, tile)])
                right.append(tiles[block, u])
            term = product(
                jnp.concatenate([jnp.concatenate(left, axis=1), ones], axis=0),
                jnp.concatenate(right, axis=1),
                LAST,
            )
            total = term if total is None else total + term
        factor = 1.0 / total[half : half + 1]
        lane = pl.ds(pl.multiple_of(block * tile, tile), tile)
        out[:, lane] = (total[:half] * factor).astype(jnp.bfloat16)
        inverse[:, lane] = factor
        return carry

    lax.fori_loop(0, blocks, step, 0, unroll=4)


def middle_kernel(feats, turned, wn, inverse, base, cot, *refs):
    near, far, refs = refs[:feats], refs[feats : 2 * feats], refs[2 * feats :]
    act, grad, scaled, agg_own, agg, value = refs
    hid, width = act.shape
    half = hid // 2
    core = lax.rem(lax.axis_index("rows"), 2)
    for k in range(feats):
        first = behind(k, feats, hid)
        agg[pl.ds(pl.multiple_of(first + core * half, half), half)] = near[k][...]
        agg[pl.ds(pl.multiple_of(first + (1 - core) * half, half), half)] = far[k][...]
    own = pl.ds(behind(0, feats, hid), hid)
    agg_own[...] = agg[own]
    chunk = min(width, 256)
    for c in range(0, width, chunk):
        lane = pl.ds(c, chunk)
        pre = product(turned[...], agg[:, lane]) + base[:, lane]
        slope = jnp.exp(jnp.minimum(pre, 0.0))
        grad[:, lane] = (cot[:, lane].astype(jnp.float32) * slope).astype(jnp.bfloat16)
        value[...] = jnp.where(pre > 0, pre, slope - 1.0)
        back = product(wn[...], grad[:, lane])
        scaled[:, lane] = (back * inverse[:, lane]).astype(jnp.bfloat16)
        act[:, lane] = value[own].astype(jnp.bfloat16)


def own_quarter():
    row = lax.axis_index("rows")
    return 2 * lax.rem(row, 2) + lax.rem(row // 2, 2)


def turned_quarter(mine, index):
    both = (index // 2, index % 2)
    core = both[0] + mine // 2 - 2 * both[0] * (mine // 2)
    x = both[1] + lax.rem(mine, 2) - 2 * both[1] * lax.rem(mine, 2)
    return 2 * core + x


def weights_kernel(ws, x_own, agg_own, grad, self_own, sums):
    hid, every = ws.shape
    g = grad[...]
    self_own[...] = product(ws[...], g)
    wide = every // 2
    mine = own_quarter()
    values = [product(x_own[...], g, LAST), product(agg_own[...], g, LAST)]
    total = product(jnp.ones((8, g.shape[1]), jnp.bfloat16), g, LAST)
    for quarter in range(4):
        slot = turned_quarter(mine, quarter)
        lane = slice(quarter % 2 * wide, (quarter % 2 + 1) * wide)
        sums[slot, :hid] = values[quarter // 2][:, lane]
        sums[slot, hid:] = total[:, lane]


def collect_kernel(pair, pair_far, grad_self, grad_neigh, sums):
    hid, every = grad_self.shape
    wide = every // 2
    mine = own_quarter()
    for slot in range(4):
        value = (pair, pair_far)[slot // 2][slot % 2]
        quarter = turned_quarter(mine, slot)
        for q, out in enumerate((grad_self, grad_self, grad_neigh, grad_neigh)):

            @pl.when(quarter == q)
            def _():
                lane = slice(q % 2 * wide, (q % 2 + 1) * wide)
                out[:, lane] = value[:hid]
                if q < 2:
                    sums[:, lane] = value[hid:]


def arrange_kernel(own, other, held):
    hid, tile = held.shape[2:]
    blocks = held.shape[1] - 1
    for side, source in enumerate((own, other)):
        held[side, blocks] = jnp.zeros((hid, tile), jnp.bfloat16)
        for block in range(blocks):
            held[side, block] = source[:, block * tile : (block + 1) * tile]


def spread_kernel(plan, table, table_pair, adj, pair, held, *refs):
    rows, offsets, kinds = plan
    results, total = refs[:-1], refs[-1]
    blocks, per_block, tile, unused = adj.shape
    half = total.shape[0] // 2
    row = lax.axis_index("rows")
    firsts = [blocks * per_block + ring_row(row, offset, rows) * CAP for offset in offsets]
    for d in range(len(offsets)):
        total[...] = jnp.zeros_like(total)
        for side, (slots, tiles) in enumerate(((table, adj), (table_pair, pair))):
            for s0 in range(0, CAP, 4):
                terms = []
                for s in range(s0, s0 + 4):
                    entry = slots[firsts[d] + s]
                    index = jnp.maximum(entry, 0) // 256
                    block = index // per_block
                    place = jnp.where(entry < 0, blocks, block)
                    lane = lax.rem(jnp.maximum(entry, 0), 256) * tile
                    term = product(held[side, place], tiles[block, index - block * per_block])
                    terms.append((pl.multiple_of(lane, tile), term))
                for lane, term in terms:
                    total[:, pl.ds(lane, tile)] += term
        for part in range(2):
            value = total[part * half : (part + 1) * half]
            results[2 * d + part][...] = value.astype(kinds[2 * d + part])


def join_kernel(arrived, mine, out):
    out[...] = (arrived[...].astype(jnp.float32) + mine[...]).astype(jnp.bfloat16)


def finish_kernel(own, base_low, base_high, a_low, b_low, a_high, b_high, out):
    half = a_low.shape[0]
    for part, (base, a, b) in enumerate(((base_low, a_low, b_low), (base_high, a_high, b_high))):
        lines = slice(part * half, (part + 1) * half)
        value = own[lines] + base[...] + a[...].astype(jnp.float32)
        out[lines] = (value + b[...].astype(jnp.float32)).astype(jnp.bfloat16)


def call(kernel, name, outs, ins, out_specs, scratch, mib, flops, moved, *args):
    return pl.pallas_call(
        kernel,
        out_shape=[jax.ShapeDtypeStruct(shape, kind) for shape, kind in outs],
        in_specs=ins,
        out_specs=out_specs,
        scratch_shapes=scratch,
        compiler_params=params(mib),
        cost_estimate=cost(flops, moved),
        name=name,
    )(*args)


def shards(rows, feats, features, adjacency, tile_cols, self_weight, neigh_weight, bias_vector, grad_output):
    hid, width = features.shape
    blocks, per_block, tile, unused = adjacency.shape
    half = hid // 2
    every = hid * feats
    top = rows // 4
    narrow, wide = jnp.bfloat16, jnp.float32
    bind = functools.partial

    core = lax.rem(lax.axis_index("rows"), 2)
    mine = lax.dynamic_slice_in_dim(features, core * half, half)
    away = lax.dynamic_slice_in_dim(features, (1 - core) * half, half)
    sources, wanted = [mine], [(0, 0)]
    up, down = [mine, away], [mine, away]
    pair = swap(adjacency, rows)
    (table,) = call(
        table_kernel, "table", [((tile_cols.size + rows * CAP,), jnp.int32)], [SMEM], [SMEM],
        [pltpu.SMEM((rows,), jnp.int32)], 2, 0, 8 * rows * CAP, tile_cols,
    )
    packed = 2 * width + 2 * every + 128
    (pack,) = call(
        pack_kernel, "pack", [((hid, packed), narrow)], [HBM] * 4 + [VMEM], [VMEM],
        [pltpu.VMEM((hid, 128), narrow), pltpu.SemaphoreType.DMA((5,))], 4, 0,
        4 * hid * packed,
        features, grad_output, self_weight, neigh_weight, bias_vector.reshape(1, hid),
    )
    (tiles,) = call(
        load_kernel, "load", [(adjacency.shape, narrow)], [HBM], [VMEM],
        [pltpu.SemaphoreType.DMA], 2, 0, 4 * adjacency.size, adjacency,
    )
    for step in range(1, top + 1):
        if step == 2:
            up[1], down[1], pair, pack, tiles = lax.optimization_barrier(
                (up[1], down[1], pair, pack, tiles)
            )
            packs = [pack] + [send(pack, k, 0, rows, feats) for k in range(1, feats)]
        if step == 3:
            up[1], table = lax.optimization_barrier((up[1], table))
        if step == top:
            table_pair = swap(after(table, up[0], down[0]), rows)
            sources.append(swap(after(away, up[0], down[0]), rows))
            wanted.append((0, 1))
        for side in range(2):
            flip = side if step == 1 else 0
            forward, backward = ring_pairs(rows, 1, flip), ring_pairs(rows, -1, flip)
            if step < top or side == 0:
                up[side] = lax.ppermute(up[side], "rows", forward)
                sources.append(up[side])
                wanted.append((-step, side))
            if step < top or side == 1:
                down[side] = lax.ppermute(down[side], "rows", backward)
                sources.append(down[side])
                wanted.append((step, side))

    def aggregate(columns, values):
        return call(
            bind(aggregate_kernel, tuple(wanted), rows), "aggregate",
            [((half, width), narrow), ((1, width), wide)],
            [SMEM, VMEM] + [HBM] * len(sources), [VMEM] * 2,
            [pltpu.VMEM((rows, half, width), narrow), pltpu.SemaphoreType.DMA((len(sources),))],
            11, hid * adjacency.size, 2 * adjacency.size + rows * hid * width,
            columns, values, *sources,
        )

    value, unused_inverse = aggregate(table_pair, pair)
    far = [send(value, k, 1, rows, feats) for k in reversed(range(feats))][::-1]
    value, inverse = aggregate(table, tiles)
    near = [value] + [send(value, k, 0, rows, feats) for k in range(1, feats)]

    turned, cot_all, base = call(
        bind(prepare_kernel, feats), "prepare",
        [((every, every), narrow), ((every, width), narrow), ((every, width), wide)],
        [VMEM] * feats, [VMEM] * 3,
        [
            pltpu.VMEM((every, 2 * every), wide),
            pltpu.VMEM((every, 1), wide),
            pltpu.VMEM((every, width), narrow),
        ],
        8, 2 * every * every * width, 4 * every * packed, *packs,
    )
    activation, grad, scaled, agg_own = call(
        bind(middle_kernel, feats), "middle",
        [((hid, width), narrow), ((every, width), narrow)] + [((hid, width), narrow)] * 2,
        [VMEM] * (5 + 2 * feats), [VMEM] * 4,
        [pltpu.VMEM((every, width), narrow), pltpu.VMEM((every, min(width, 256)), wide)], 9,
        3 * every * every * width, 14 * every * width,
        turned, neigh_weight, inverse, base, cot_all, *near, *far,
    )
    scaled_pair = swap(scaled, rows)
    self_own, sums = call(
        weights_kernel, "weights", [((hid, width), wide), ((4, hid + 8, every // 2), wide)],
        [VMEM] * 4, [VMEM] * 2, [], 6, 6 * hid * every * width, 10 * every * width,
        self_weight, features, agg_own, grad,
    )
    (held,) = call(
        arrange_kernel, "arrange", [((2, blocks + 1, hid, tile), narrow)],
        [VMEM] * 2, [VMEM], [], 4, 0, 8 * hid * width, scaled, scaled_pair,
    )

    def spread(offsets, kinds):
        n = 2 * CAP * len(offsets)
        return call(
            bind(spread_kernel, (rows, offsets, kinds)), "spread",
            [((half, width), kind) for kind in kinds],
            [SMEM] * 2 + [VMEM] * 3, [VMEM] * len(kinds), [pltpu.VMEM((hid, width), wide)],
            9, 2 * n * hid * tile * tile, 8 * hid * width * len(offsets),
            table, table_pair, tiles, pair, held,
        )

    def joined(arrived, mine):
        if arrived is None:
            return mine
        (out,) = call(
            join_kernel, "join", [((half, width), narrow)], [VMEM] * 2, [VMEM], [], 3,
            0, 4 * hid * width, arrived, mine,
        )
        return out

    near = sums[:2] + swap(sums[2:], rows, 1)
    total = near[0] + swap(near[1], rows, 2)
    bit, sends = 4, 0

    def ring(value, pairs):
        nonlocal total, bit, sends
        sends += 1
        if sends >= 5 and sends % 4 == 1 and bit < 2 * rows:
            value = after(value, total)
            total = after(total, value)
            if bit < rows:
                total = total + swap(total, rows, bit)
            bit *= 2
        return lax.ppermute(value, "rows", pairs)

    up, down = [None, None], [None, None]
    forward, backward = ring_pairs(rows, 1), ring_pairs(rows, -1)
    for level in range(top, 0, -1):
        if level == top:
            low, high = spread((top,), (narrow, narrow))
            up[0] = ring(low, forward)
            down[1] = ring(high, backward)
            continue
        kinds = tuple(narrow if arrived is None else wide for arrived in up + down)
        offsets = (level, -level)
        if level == 1:
            offsets, kinds = (1, -1, 0), kinds + (wide, wide)
        mine = spread(offsets, kinds)
        first = [i for i in range(2) if up[i] is None]
        for i in first + [i for i in range(2) if i not in first]:
            flow = 1 - i
            up[i] = ring(joined(up[i], mine[i]), forward)
            down[flow] = ring(joined(down[flow], mine[2 + flow]), backward)
    near = jnp.stack([total, swap(total, rows, 2)])
    far = swap(near, rows, 1)
    grad_self, grad_neigh, total = call(
        collect_kernel, "collect",
        [((hid, every), wide), ((hid, every), wide), ((8, every), wide)],
        [VMEM] * 2, [VMEM] * 3, [], 4, 0, 16 * hid * every, near, far,
    )
    grad_bias = lax.dynamic_slice_in_dim(total[0], lax.axis_index("feat") * hid, hid)
    (grad_features,) = call(
        finish_kernel, "finish", [((hid, width), narrow)], [VMEM] * 7, [VMEM], [], 6, 0,
        8 * hid * width, self_own, mine[4], mine[5], up[0], down[0], up[1], down[1],
    )
    return (activation, grad_features, grad_self, grad_neigh, grad_bias)


def solution(mesh):
    in_specs = (
        P("feat", "rows"),
        P("rows", None, None, None),
        P("rows", None),
        P("feat", None),
        P("feat", None),
        P("feat"),
        P("feat", "rows"),
    )
    out_specs = (P("feat", "rows"), P("feat", "rows"), P("feat", None), P("feat", None), P("feat"))
    body = functools.partial(shards, mesh.shape["rows"], mesh.shape["feat"])
    return jax.shard_map(body, mesh=mesh, in_specs=in_specs, out_specs=out_specs, check_vma=False)
```

```python
import functools

import jax
import jax.numpy as jnp
from jax import lax
from jax.experimental import pallas as pl
from jax.experimental.pallas import tpu as pltpu
from jax.sharding import PartitionSpec as P

CAP = 12
MIB = 1024 * 1024
HBM = pl.BlockSpec(memory_space=pltpu.HBM)
VMEM = pl.BlockSpec(memory_space=pltpu.VMEM)
SMEM = pl.BlockSpec(memory_space=pltpu.SMEM)
LAST = (((1,), (1,)), ((), ()))


def params(mib):
    return pltpu.CompilerParams(vmem_limit_bytes=mib * MIB)


def cost(flops, moved):
    return pl.CostEstimate(flops=flops, bytes_accessed=moved, transcendentals=0)


def product(left, right, dims=(((1,), (0,)), ((), ()))):
    return lax.dot_general(left, right, dims, preferred_element_type=jnp.float32)


def ring_pairs(rows, step, flip=0):
    levels, chips = rows // 4, rows // 2
    order = [2 * z for z in range(levels)] + [2 * z + 1 for z in reversed(range(levels))]
    return [
        (2 * order[p] + core, 2 * order[(p + step) % chips] + (core ^ flip))
        for p in range(chips)
        for core in range(2)
    ]


def ring_row(row, offset, rows):
    levels, chips = rows // 4, rows // 2
    z, x, core = row // 4, lax.rem(row // 2, 2), lax.rem(row, 2)
    target = lax.rem(jnp.where(x == 0, z, chips - 1 - z) + (offset + chips), chips)
    low = target < levels
    return 2 * jnp.where(low, 2 * target, 2 * (chips - 1 - target) + 1) + core


def swap(value, rows, bit=1):
    return lax.ppermute(value, "rows", [(r, r ^ bit) for r in range(rows)])


def send(value, k, flip, rows, feats):
    pairs = [
        (r * feats + i, (r ^ flip) * feats + (i + k) % feats)
        for r in range(rows)
        for i in range(feats)
    ]
    return lax.ppermute(value, ("rows", "feat"), pairs)


def after(value, *others):
    return lax.optimization_barrier((value, *others))[0]


def behind(k, feats, size):
    return pl.multiple_of(lax.rem(lax.axis_index("feat") - k + feats, feats) * size, size)


def pack_kernel(feature, grad_output, ws, wn, bias, out, parts, sems):
    hid, every = ws.shape
    width = feature.shape[1]
    copies = []
    for source, low, size in (
        (feature, 0, width),
        (grad_output, width, width),
        (ws, 2 * width, every),
        (wn, 2 * width + every, every),
        (parts, 2 * width + 2 * every, 128),
    ):
        place = out.at[:, pl.ds(low, size)]
        copies.append(pltpu.make_async_copy(source, place, sems.at[len(copies)]))
    line = lax.broadcasted_iota(jnp.int32, (hid, hid), 0)
    lane = lax.broadcasted_iota(jnp.int32, (hid, hid), 1)
    column = jnp.sum(jnp.where(line == lane, bias[...], 0.0), axis=1, keepdims=True)
    high = column.astype(jnp.bfloat16).astype(jnp.float32)
    middle = (column - high).astype(jnp.bfloat16).astype(jnp.float32)
    low = column - high - middle
    at = lax.broadcasted_iota(jnp.int32, (hid, 128), 1)
    value = jnp.where(at == 0, high, jnp.where(at == 1, middle, jnp.where(at == 2, low, 0.0)))
    parts[...] = value.astype(jnp.bfloat16)
    for copy in copies:
        copy.start()
    for copy in copies:
        copy.wait()


def prepare_kernel(feats, *refs):
    packs, (turned, cot_all, base), (weights, bias, x_all) = refs[:feats], refs[feats:-3], refs[-3:]
    hid, width = packs[0].shape[0], x_all.shape[1]
    every = feats * hid
    for k in range(feats):
        at = pl.ds(behind(k, feats, hid), hid)
        pack = packs[k]
        x_all[at] = pack[:, :width]
        cot_all[at] = pack[:, width : 2 * width]
        weights[at] = pack[:, 2 * width : 2 * width + 2 * every].astype(jnp.float32)
        parts = pack[:, 2 * width + 2 * every :].astype(jnp.float32)
        bias[at] = jnp.sum(parts, axis=1, keepdims=True)
    own = weights[:, :every].T.astype(jnp.bfloat16)
    turned[...] = weights[:, every:].T.astype(jnp.bfloat16)
    chunk = min(width, 512)
    for c in range(0, width, chunk):
        lane = pl.ds(c, chunk)
        base[:, lane] = product(own, x_all[:, lane]) + bias[...]


def table_kernel(cols, table, counts):
    blocks, per_block = cols.shape
    base = blocks * per_block
    groups = counts.shape[0]

    def clear(i, carry):
        counts[i] = 0
        for s in range(CAP):
            table[base + i * CAP + s] = -1
        return carry

    lax.fori_loop(0, groups, clear, 0)

    def step(block, carry):
        for t in range(per_block):
            col = cols[block, t]
            group = col // blocks
            seen = counts[group]
            counts[group] = seen + 1
            index = block * per_block + t
            table[index] = col
            table[base + group * CAP + seen] = index * 256 + (col - group * blocks)
        return carry

    lax.fori_loop(0, blocks, step, 0)


def load_kernel(source, out, sem):
    copy = pltpu.make_async_copy(source, out, sem)
    copy.start()
    copy.wait()


def aggregate_kernel(wanted, rows, table, tiles, *refs):
    count = len(wanted)
    blocks, per_block, tile, unused = tiles.shape
    half = refs[0].shape[0]
    sources, (out, inverse, held, sems) = refs[:count], refs[count:]
    row = lax.axis_index("rows")
    copies = []
    for n, (offset, side) in enumerate(wanted):
        place = ring_row(row, offset, rows)
        if side:
            place = place + 1 - 2 * lax.rem(place, 2)
        copies.append(pltpu.make_async_copy(sources[n], held.at[place], sems.at[n]))
    for copy in copies:
        copy.start()
    for copy in copies:
        copy.wait()
    ones = jnp.ones((16, 2 * tile), jnp.bfloat16)

    def step(block, carry):
        total = None
        for t in range(0, per_block, 2):
            left, right = [], []
            for u in (t, t + 1):
                col = table[block * per_block + u]
                source = col // blocks
                at = pl.multiple_of((col - source * blocks) * tile, tile)
                left.append(held[source, :, pl.ds(at, tile)])
                right.append(tiles[block, u])
            term = product(
                jnp.concatenate([jnp.concatenate(left, axis=1), ones], axis=0),
                jnp.concatenate(right, axis=1),
                LAST,
            )
            total = term if total is None else total + term
        factor = 1.0 / total[half : half + 1]
        lane = pl.ds(pl.multiple_of(block * tile, tile), tile)
        out[:, lane] = (total[:half] * factor).astype(jnp.bfloat16)
        inverse[:, lane] = factor
        return carry

    lax.fori_loop(0, blocks, step, 0, unroll=4)


def middle_kernel(feats, turned, wn, inverse, base, cot, *refs):
    near, far, refs = refs[:feats], refs[feats : 2 * feats], refs[2 * feats :]
    act, grad, scaled, agg_own, agg, value = refs
    hid, width = act.shape
    half = hid // 2
    core = lax.rem(lax.axis_index("rows"), 2)
    for k in range(feats):
        first = behind(k, feats, hid)
        agg[pl.ds(pl.multiple_of(first + core * half, half), half)] = near[k][...]
        agg[pl.ds(pl.multiple_of(first + (1 - core) * half, half), half)] = far[k][...]
    own = pl.ds(behind(0, feats, hid), hid)
    agg_own[...] = agg[own]
    chunk = min(width, 256)
    for c in range(0, width, chunk):
        lane = pl.ds(c, chunk)
        pre = product(turned[...], agg[:, lane]) + base[:, lane]
        slope = jnp.exp(jnp.minimum(pre, 0.0))
        grad[:, lane] = (cot[:, lane].astype(jnp.float32) * slope).astype(jnp.bfloat16)
        value[...] = jnp.where(pre > 0, pre, slope - 1.0)
        back = product(wn[...], grad[:, lane])
        scaled[:, lane] = (back * inverse[:, lane]).astype(jnp.bfloat16)
        act[:, lane] = value[own].astype(jnp.bfloat16)


def own_quarter():
    row = lax.axis_index("rows")
    return 2 * lax.rem(row, 2) + lax.rem(row // 2, 2)


def turned_quarter(mine, index):
    both = (index // 2, index % 2)
    core = both[0] + mine // 2 - 2 * both[0] * (mine // 2)
    x = both[1] + lax.rem(mine, 2) - 2 * both[1] * lax.rem(mine, 2)
    return 2 * core + x


def weights_kernel(ws, x_own, agg_own, grad, self_own, sums):
    hid, every = ws.shape
    g = grad[...]
    self_own[...] = product(ws[...], g)
    wide = every // 2
    mine = own_quarter()
    values = [product(x_own[...], g, LAST), product(agg_own[...], g, LAST)]
    total = product(jnp.ones((8, g.shape[1]), jnp.bfloat16), g, LAST)
    for quarter in range(4):
        slot = turned_quarter(mine, quarter)
        lane = slice(quarter % 2 * wide, (quarter % 2 + 1) * wide)
        sums[slot, :hid] = values[quarter // 2][:, lane]
        sums[slot, hid:] = total[:, lane]


def collect_kernel(pair, pair_far, grad_self, grad_neigh, sums):
    hid, every = grad_self.shape
    wide = every // 2
    mine = own_quarter()
    for slot in range(4):
        value = (pair, pair_far)[slot // 2][slot % 2]
        quarter = turned_quarter(mine, slot)
        for q, out in enumerate((grad_self, grad_self, grad_neigh, grad_neigh)):

            @pl.when(quarter == q)
            def _():
                lane = slice(q % 2 * wide, (q % 2 + 1) * wide)
                out[:, lane] = value[:hid]
                if q < 2:
                    sums[:, lane] = value[hid:]


def arrange_kernel(own, other, held):
    hid, tile = held.shape[2:]
    blocks = held.shape[1] - 1
    for side, source in enumerate((own, other)):
        held[side, blocks] = jnp.zeros((hid, tile), jnp.bfloat16)
        for block in range(blocks):
            held[side, block] = source[:, block * tile : (block + 1) * tile]


def spread_kernel(plan, table, table_pair, adj, pair, held, *refs):
    rows, offsets, kinds = plan
    results, total = refs[:-1], refs[-1]
    blocks, per_block, tile, unused = adj.shape
    half = total.shape[0] // 2
    row = lax.axis_index("rows")
    firsts = [blocks * per_block + ring_row(row, offset, rows) * CAP for offset in offsets]
    for d in range(len(offsets)):
        total[...] = jnp.zeros_like(total)
        for side, (slots, tiles) in enumerate(((table, adj), (table_pair, pair))):
            for s0 in range(0, CAP, 4):
                terms = []
                for s in range(s0, s0 + 4):
                    entry = slots[firsts[d] + s]
                    index = jnp.maximum(entry, 0) // 256
                    block = index // per_block
                    place = jnp.where(entry < 0, blocks, block)
                    lane = lax.rem(jnp.maximum(entry, 0), 256) * tile
                    term = product(held[side, place], tiles[block, index - block * per_block])
                    terms.append((pl.multiple_of(lane, tile), term))
                for lane, term in terms:
                    total[:, pl.ds(lane, tile)] += term
        for part in range(2):
            value = total[part * half : (part + 1) * half]
            results[2 * d + part][...] = value.astype(kinds[2 * d + part])


def join_kernel(arrived, mine, out):
    out[...] = (arrived[...].astype(jnp.float32) + mine[...]).astype(jnp.bfloat16)


def finish_kernel(own, base_low, base_high, a_low, b_low, a_high, b_high, out):
    half = a_low.shape[0]
    for part, (base, a, b) in enumerate(((base_low, a_low, b_low), (base_high, a_high, b_high))):
        lines = slice(part * half, (part + 1) * half)
        value = own[lines] + base[...] + a[...].astype(jnp.float32)
        out[lines] = (value + b[...].astype(jnp.float32)).astype(jnp.bfloat16)


def call(kernel, name, outs, ins, out_specs, scratch, mib, flops, moved, *args):
    return pl.pallas_call(
        kernel,
        out_shape=[jax.ShapeDtypeStruct(shape, kind) for shape, kind in outs],
        in_specs=ins,
        out_specs=out_specs,
        scratch_shapes=scratch,
        compiler_params=params(mib),
        cost_estimate=cost(flops, moved),
        name=name,
    )(*args)


def shards(rows, feats, features, adjacency, tile_cols, self_weight, neigh_weight, bias_vector, grad_output):
    hid, width = features.shape
    blocks, per_block, tile, unused = adjacency.shape
    half = hid // 2
    every = hid * feats
    top = rows // 4
    narrow, wide = jnp.bfloat16, jnp.float32
    bind = functools.partial

    core = lax.rem(lax.axis_index("rows"), 2)
    mine = lax.dynamic_slice_in_dim(features, core * half, half)
    away = lax.dynamic_slice_in_dim(features, (1 - core) * half, half)
    sources, wanted = [mine], [(0, 0)]
    up, down = [mine, away], [mine, away]
    (table,) = call(
        table_kernel, "table", [((tile_cols.size + rows * CAP,), jnp.int32)], [SMEM], [SMEM],
        [pltpu.SMEM((rows,), jnp.int32)], 2, 0, 8 * rows * CAP, tile_cols,
    )
    packed = 2 * width + 2 * every + 128
    (pack,) = call(
        pack_kernel, "pack", [((hid, packed), narrow)], [HBM] * 4 + [VMEM], [VMEM],
        [pltpu.VMEM((hid, 128), narrow), pltpu.SemaphoreType.DMA((5,))], 4, 0,
        4 * hid * packed,
        features, grad_output, self_weight, neigh_weight, bias_vector.reshape(1, hid),
    )

    def load(value):
        (out,) = call(
            load_kernel, "load", [(adjacency.shape, narrow)], [HBM], [VMEM],
            [pltpu.SemaphoreType.DMA], 2, 0, 4 * adjacency.size, value,
        )
        return out

    pair, tiles = swap(adjacency, rows), load(adjacency)
    for step in range(1, top + 1):
        if step == 2:
            up, down, pair, pack, tiles = lax.optimization_barrier((up, down, pair, pack, tiles))
            packs = [pack] + [send(pack, k, 0, rows, feats) for k in range(1, feats)]
        if step == 3:
            up[1], table = lax.optimization_barrier((up[1], table))
        if step == top:
            table_pair = swap(after(table, up[0], down[0]), rows)
            pair = load(pair)
            sources.append(swap(after(away, up[0], down[0], pair), rows))
            wanted.append((0, 1))
        for side in range(2):
            flip = side if step == 1 else 0
            forward, backward = ring_pairs(rows, 1, flip), ring_pairs(rows, -1, flip)
            if step < top or side == 0:
                up[side] = lax.ppermute(up[side], "rows", forward)
                sources.append(up[side])
                wanted.append((-step, side))
            if step < top or side == 1:
                down[side] = lax.ppermute(down[side], "rows", backward)
                sources.append(down[side])
                wanted.append((step, side))

    def aggregate(columns, values):
        return call(
            bind(aggregate_kernel, tuple(wanted), rows), "aggregate",
            [((half, width), narrow), ((1, width), wide)],
            [SMEM, VMEM] + [HBM] * len(sources), [VMEM] * 2,
            [pltpu.VMEM((rows, half, width), narrow), pltpu.SemaphoreType.DMA((len(sources),))],
            11, hid * adjacency.size, 2 * adjacency.size + rows * hid * width,
            columns, values, *sources,
        )

    value, unused_inverse = aggregate(table_pair, pair)
    far = [send(value, k, 1, rows, feats) for k in reversed(range(feats))][::-1]
    value, inverse = aggregate(table, tiles)
    near = [value] + [send(value, k, 0, rows, feats) for k in range(1, feats)]

    turned, cot_all, base = call(
        bind(prepare_kernel, feats), "prepare",
        [((every, every), narrow), ((every, width), narrow), ((every, width), wide)],
        [VMEM] * feats, [VMEM] * 3,
        [
            pltpu.VMEM((every, 2 * every), wide),
            pltpu.VMEM((every, 1), wide),
            pltpu.VMEM((every, width), narrow),
        ],
        8, 2 * every * every * width, 4 * every * packed, *packs,
    )
    activation, grad, scaled, agg_own = call(
        bind(middle_kernel, feats), "middle",
        [((hid, width), narrow), ((every, width), narrow)] + [((hid, width), narrow)] * 2,
        [VMEM] * (5 + 2 * feats), [VMEM] * 4,
        [pltpu.VMEM((every, width), narrow), pltpu.VMEM((every, min(width, 256)), wide)], 9,
        3 * every * every * width, 14 * every * width,
        turned, neigh_weight, inverse, base, cot_all, *near, *far,
    )
    scaled_pair = swap(scaled, rows)
    self_own, sums = call(
        weights_kernel, "weights", [((hid, width), wide), ((4, hid + 8, every // 2), wide)],
        [VMEM] * 4, [VMEM] * 2, [], 6, 6 * hid * every * width, 10 * every * width,
        self_weight, features, agg_own, grad,
    )
    (held,) = call(
        arrange_kernel, "arrange", [((2, blocks + 1, hid, tile), narrow)],
        [VMEM] * 2, [VMEM], [], 4, 0, 8 * hid * width, scaled, scaled_pair,
    )

    def spread(offsets, kinds):
        n = 2 * CAP * len(offsets)
        return call(
            bind(spread_kernel, (rows, offsets, kinds)), "spread",
            [((half, width), kind) for kind in kinds],
            [SMEM] * 2 + [VMEM] * 3, [VMEM] * len(kinds), [pltpu.VMEM((hid, width), wide)],
            9, 2 * n * hid * tile * tile, 8 * hid * width * len(offsets),
            table, table_pair, tiles, pair, held,
        )

    def joined(arrived, mine):
        if arrived is None:
            return mine
        (out,) = call(
            join_kernel, "join", [((half, width), narrow)], [VMEM] * 2, [VMEM], [], 3,
            0, 4 * hid * width, arrived, mine,
        )
        return out

    near = sums[:2] + swap(after(sums[2:], scaled_pair), rows, 1)
    total = near[0] + swap(near[1], rows, 2)
    bit, sends = 4, 0

    def ring(value, pairs):
        nonlocal total, bit, sends
        sends += 1
        if sends >= 5 and sends % 4 == 1 and bit < 2 * rows:
            value = after(value, total)
            total = after(total, value)
            if bit < rows:
                total = total + swap(total, rows, bit)
            bit *= 2
        return lax.ppermute(value, "rows", pairs)

    up, down = [None, None], [None, None]
    forward, backward = ring_pairs(rows, 1), ring_pairs(rows, -1)
    for level in range(top, 0, -1):
        if level == top:
            low, high = spread((top,), (narrow, narrow))
            up[0] = ring(low, forward)
            down[1] = ring(high, backward)
            continue
        kinds = tuple(narrow if arrived is None else wide for arrived in up + down)
        offsets = (level, -level)
        if level == 1:
            offsets, kinds = (1, -1, 0), kinds + (wide, wide)
        mine = spread(offsets, kinds)
        for i in (1, 0):
            flow = 1 - i
            up[i] = ring(joined(up[i], mine[i]), forward)
            down[flow] = ring(joined(down[flow], mine[2 + flow]), backward)
    near = jnp.stack([total, swap(total, rows, 2)])
    far = swap(near, rows, 1)
    grad_self, grad_neigh, total = call(
        collect_kernel, "collect",
        [((hid, every), wide), ((hid, every), wide), ((8, every), wide)],
        [VMEM] * 2, [VMEM] * 3, [], 4, 0, 16 * hid * every, near, far,
    )
    grad_bias = lax.dynamic_slice_in_dim(total[0], lax.axis_index("feat") * hid, hid)
    (grad_features,) = call(
        finish_kernel, "finish", [((hid, width), narrow)], [VMEM] * 7, [VMEM], [], 6, 0,
        8 * hid * width, self_own, mine[4], mine[5], up[0], down[0], up[1], down[1],
    )
    return (activation, grad_features, grad_self, grad_neigh, grad_bias)


def solution(mesh):
    in_specs = (
        P("feat", "rows"),
        P("rows", None, None, None),
        P("rows", None),
        P("feat", None),
        P("feat", None),
        P("feat"),
        P("feat", "rows"),
    )
    out_specs = (P("feat", "rows"), P("feat", "rows"), P("feat", None), P("feat", None), P("feat"))
    body = functools.partial(shards, mesh.shape["rows"], mesh.shape["feat"])
    return jax.shard_map(body, mesh=mesh, in_specs=in_specs, out_specs=out_specs, check_vma=False)
```

```python
import functools

import jax
import jax.numpy as jnp
from jax import lax
from jax.experimental import pallas as pl
from jax.experimental.pallas import tpu as pltpu
from jax.sharding import PartitionSpec as P

CAP = 12
MIB = 1024 * 1024
HBM = pl.BlockSpec(memory_space=pltpu.HBM)
VMEM = pl.BlockSpec(memory_space=pltpu.VMEM)
SMEM = pl.BlockSpec(memory_space=pltpu.SMEM)
LAST = (((1,), (1,)), ((), ()))


def params(mib):
    return pltpu.CompilerParams(vmem_limit_bytes=mib * MIB)


def cost(flops, moved):
    return pl.CostEstimate(flops=flops, bytes_accessed=moved, transcendentals=0)


def product(left, right, dims=(((1,), (0,)), ((), ()))):
    return lax.dot_general(left, right, dims, preferred_element_type=jnp.float32)


def ring_pairs(rows, step, flip=0):
    levels, chips = rows // 4, rows // 2
    order = [2 * z for z in range(levels)] + [2 * z + 1 for z in reversed(range(levels))]
    return [
        (2 * order[p] + core, 2 * order[(p + step) % chips] + (core ^ flip))
        for p in range(chips)
        for core in range(2)
    ]


def ring_row(row, offset, rows):
    levels, chips = rows // 4, rows // 2
    z, x, core = row // 4, lax.rem(row // 2, 2), lax.rem(row, 2)
    target = lax.rem(jnp.where(x == 0, z, chips - 1 - z) + (offset + chips), chips)
    low = target < levels
    return 2 * jnp.where(low, 2 * target, 2 * (chips - 1 - target) + 1) + core


def swap(value, rows, bit=1):
    return lax.ppermute(value, "rows", [(r, r ^ bit) for r in range(rows)])


def send(value, k, flip, rows, feats):
    pairs = [
        (r * feats + i, (r ^ flip) * feats + (i + k) % feats)
        for r in range(rows)
        for i in range(feats)
    ]
    return lax.ppermute(value, ("rows", "feat"), pairs)


def after(value, *others):
    return lax.optimization_barrier((value, *others))[0]


def behind(k, feats, size):
    return pl.multiple_of(lax.rem(lax.axis_index("feat") - k + feats, feats) * size, size)


def pack_kernel(feature, grad_output, ws, wn, bias, out, parts, sems):
    hid, every = ws.shape
    width = feature.shape[1]
    copies = []
    for source, low, size in (
        (feature, 0, width),
        (grad_output, width, width),
        (ws, 2 * width, every),
        (wn, 2 * width + every, every),
        (parts, 2 * width + 2 * every, 128),
    ):
        place = out.at[:, pl.ds(low, size)]
        copies.append(pltpu.make_async_copy(source, place, sems.at[len(copies)]))
    line = lax.broadcasted_iota(jnp.int32, (hid, hid), 0)
    lane = lax.broadcasted_iota(jnp.int32, (hid, hid), 1)
    column = jnp.sum(jnp.where(line == lane, bias[...], 0.0), axis=1, keepdims=True)
    high = column.astype(jnp.bfloat16).astype(jnp.float32)
    middle = (column - high).astype(jnp.bfloat16).astype(jnp.float32)
    low = column - high - middle
    at = lax.broadcasted_iota(jnp.int32, (hid, 128), 1)
    value = jnp.where(at == 0, high, jnp.where(at == 1, middle, jnp.where(at == 2, low, 0.0)))
    parts[...] = value.astype(jnp.bfloat16)
    for copy in copies:
        copy.start()
    for copy in copies:
        copy.wait()


def prepare_kernel(feats, *refs):
    packs, (turned, cot_all, base), (weights, bias, x_all) = refs[:feats], refs[feats:-3], refs[-3:]
    hid, width = packs[0].shape[0], x_all.shape[1]
    every = feats * hid
    for k in range(feats):
        at = pl.ds(behind(k, feats, hid), hid)
        pack = packs[k]
        x_all[at] = pack[:, :width]
        cot_all[at] = pack[:, width : 2 * width]
        weights[at] = pack[:, 2 * width : 2 * width + 2 * every].astype(jnp.float32)
        parts = pack[:, 2 * width + 2 * every :].astype(jnp.float32)
        bias[at] = jnp.sum(parts, axis=1, keepdims=True)
    own = weights[:, :every].T.astype(jnp.bfloat16)
    turned[...] = weights[:, every:].T.astype(jnp.bfloat16)
    chunk = min(width, 512)
    for c in range(0, width, chunk):
        lane = pl.ds(c, chunk)
        base[:, lane] = product(own, x_all[:, lane]) + bias[...]


def table_kernel(cols, table, counts):
    blocks, per_block = cols.shape
    base = blocks * per_block
    groups = counts.shape[0]

    def clear(i, carry):
        counts[i] = 0
        for s in range(CAP):
            table[base + i * CAP + s] = -1
        return carry

    lax.fori_loop(0, groups, clear, 0)

    def step(block, carry):
        for t in range(per_block):
            col = cols[block, t]
            group = col // blocks
            seen = counts[group]
            counts[group] = seen + 1
            index = block * per_block + t
            table[index] = col
            table[base + group * CAP + seen] = index * 256 + (col - group * blocks)
        return carry

    lax.fori_loop(0, blocks, step, 0)


def load_kernel(source, out, sem):
    copy = pltpu.make_async_copy(source, out, sem)
    copy.start()
    copy.wait()


def aggregate_kernel(wanted, rows, table, tiles, *refs):
    count = len(wanted)
    blocks, per_block, tile, unused = tiles.shape
    half = refs[0].shape[0]
    sources, (out, inverse, held, sems) = refs[:count], refs[count:]
    row = lax.axis_index("rows")
    copies = []
    for n, (offset, side) in enumerate(wanted):
        place = ring_row(row, offset, rows)
        if side:
            place = place + 1 - 2 * lax.rem(place, 2)
        copies.append(pltpu.make_async_copy(sources[n], held.at[place], sems.at[n]))
    for copy in copies:
        copy.start()
    for copy in copies:
        copy.wait()
    ones = jnp.ones((16, 2 * tile), jnp.bfloat16)

    def step(block, carry):
        total = None
        for t in range(0, per_block, 2):
            left, right = [], []
            for u in (t, t + 1):
                col = table[block * per_block + u]
                source = col // blocks
                at = pl.multiple_of((col - source * blocks) * tile, tile)
                left.append(held[source, :, pl.ds(at, tile)])
                right.append(tiles[block, u])
            term = product(
                jnp.concatenate([jnp.concatenate(left, axis=1), ones], axis=0),
                jnp.concatenate(right, axis=1),
                LAST,
            )
            total = term if total is None else total + term
        factor = 1.0 / total[half : half + 1]
        lane = pl.ds(pl.multiple_of(block * tile, tile), tile)
        out[:, lane] = (total[:half] * factor).astype(jnp.bfloat16)
        inverse[:, lane] = factor
        return carry

    lax.fori_loop(0, blocks, step, 0, unroll=4)


def middle_kernel(feats, turned, wn, inverse, base, cot, *refs):
    near, far, refs = refs[:feats], refs[feats : 2 * feats], refs[2 * feats :]
    act, grad, scaled, agg_own, agg, value = refs
    hid, width = act.shape
    half = hid // 2
    core = lax.rem(lax.axis_index("rows"), 2)
    for k in range(feats):
        first = behind(k, feats, hid)
        agg[pl.ds(pl.multiple_of(first + core * half, half), half)] = near[k][...]
        agg[pl.ds(pl.multiple_of(first + (1 - core) * half, half), half)] = far[k][...]
    own = pl.ds(behind(0, feats, hid), hid)
    agg_own[...] = agg[own]
    chunk = min(width, 256)
    for c in range(0, width, chunk):
        lane = pl.ds(c, chunk)
        pre = product(turned[...], agg[:, lane]) + base[:, lane]
        slope = jnp.exp(jnp.minimum(pre, 0.0))
        grad[:, lane] = (cot[:, lane].astype(jnp.float32) * slope).astype(jnp.bfloat16)
        value[...] = jnp.where(pre > 0, pre, slope - 1.0)
        back = product(wn[...], grad[:, lane])
        scaled[:, lane] = (back * inverse[:, lane]).astype(jnp.bfloat16)
        act[:, lane] = value[own].astype(jnp.bfloat16)


def own_quarter():
    return 2 * lax.rem(lax.axis_index("rows"), 2)


def turned_quarter(mine, index):
    turned = index // 2 + mine // 2 - 2 * (index // 2) * (mine // 2)
    return 2 * turned + index % 2


def weights_kernel(ws, x_own, agg_own, grad, self_own, sums):
    hid, every = ws.shape
    g = grad[...]
    self_own[...] = product(ws[...], g)
    wide = every // 2
    mine = own_quarter()
    values = [product(x_own[...], g, LAST), product(agg_own[...], g, LAST)]
    total = product(jnp.ones((8, g.shape[1]), jnp.bfloat16), g, LAST)
    for quarter in range(4):
        slot = turned_quarter(mine, quarter)
        lane = slice(quarter % 2 * wide, (quarter % 2 + 1) * wide)
        sums[slot, :hid] = values[quarter // 2][:, lane]
        sums[slot, hid:] = total[:, lane]


def collect_kernel(pair, pair_far, grad_self, grad_neigh, sums):
    hid, every = grad_self.shape
    wide = every // 2
    mine = own_quarter()
    for slot in range(4):
        value = (pair, pair_far)[slot // 2][slot % 2]
        quarter = turned_quarter(mine, slot)
        for q, out in enumerate((grad_self, grad_self, grad_neigh, grad_neigh)):

            @pl.when(quarter == q)
            def _():
                lane = slice(q % 2 * wide, (q % 2 + 1) * wide)
                out[:, lane] = value[:hid]
                if q < 2:
                    sums[:, lane] = value[hid:]


def arrange_kernel(own, other, held):
    hid, tile = held.shape[2:]
    blocks = held.shape[1] - 1
    for side, source in enumerate((own, other)):
        held[side, blocks] = jnp.zeros((hid, tile), jnp.bfloat16)
        for block in range(blocks):
            held[side, block] = source[:, block * tile : (block + 1) * tile]


def spread_kernel(plan, table, table_pair, adj, pair, held, *refs):
    rows, offsets, kinds = plan
    results, total = refs[:-1], refs[-1]
    blocks, per_block, tile, unused = adj.shape
    half = total.shape[0] // 2
    row = lax.axis_index("rows")
    firsts = [blocks * per_block + ring_row(row, offset, rows) * CAP for offset in offsets]
    for d in range(len(offsets)):
        total[...] = jnp.zeros_like(total)
        for side, (slots, tiles) in enumerate(((table, adj), (table_pair, pair))):
            for s0 in range(0, CAP, 4):
                terms = []
                for s in range(s0, s0 + 4):
                    entry = slots[firsts[d] + s]
                    index = jnp.maximum(entry, 0) // 256
                    block = index // per_block
                    place = jnp.where(entry < 0, blocks, block)
                    lane = lax.rem(jnp.maximum(entry, 0), 256) * tile
                    term = product(held[side, place], tiles[block, index - block * per_block])
                    terms.append((pl.multiple_of(lane, tile), term))
                for lane, term in terms:
                    total[:, pl.ds(lane, tile)] += term
        for part in range(2):
            value = total[part * half : (part + 1) * half]
            results[2 * d + part][...] = value.astype(kinds[2 * d + part])


def join_kernel(arrived, mine, out):
    out[...] = (arrived[...].astype(jnp.float32) + mine[...]).astype(jnp.bfloat16)


def finish_kernel(own, base_low, base_high, a_low, b_low, a_high, b_high, out):
    half = a_low.shape[0]
    for part, (base, a, b) in enumerate(((base_low, a_low, b_low), (base_high, a_high, b_high))):
        lines = slice(part * half, (part + 1) * half)
        value = own[lines] + base[...] + a[...].astype(jnp.float32)
        out[lines] = (value + b[...].astype(jnp.float32)).astype(jnp.bfloat16)


def call(kernel, name, outs, ins, out_specs, scratch, mib, flops, moved, *args):
    return pl.pallas_call(
        kernel,
        out_shape=[jax.ShapeDtypeStruct(shape, kind) for shape, kind in outs],
        in_specs=ins,
        out_specs=out_specs,
        scratch_shapes=scratch,
        compiler_params=params(mib),
        cost_estimate=cost(flops, moved),
        name=name,
    )(*args)


def shards(rows, feats, features, adjacency, tile_cols, self_weight, neigh_weight, bias_vector, grad_output):
    hid, width = features.shape
    blocks, per_block, tile, unused = adjacency.shape
    half = hid // 2
    every = hid * feats
    top = rows // 4
    narrow, wide = jnp.bfloat16, jnp.float32
    bind = functools.partial

    core = lax.rem(lax.axis_index("rows"), 2)
    mine = lax.dynamic_slice_in_dim(features, core * half, half)
    away = lax.dynamic_slice_in_dim(features, (1 - core) * half, half)
    sources, wanted = [mine], [(0, 0)]
    up, down = [mine, away], [mine, away]
    (table,) = call(
        table_kernel, "table", [((tile_cols.size + rows * CAP,), jnp.int32)], [SMEM], [SMEM],
        [pltpu.SMEM((rows,), jnp.int32)], 2, 0, 8 * rows * CAP, tile_cols,
    )
    packed = 2 * width + 2 * every + 128
    (pack,) = call(
        pack_kernel, "pack", [((hid, packed), narrow)], [HBM] * 4 + [VMEM], [VMEM],
        [pltpu.VMEM((hid, 128), narrow), pltpu.SemaphoreType.DMA((5,))], 4, 0,
        4 * hid * packed,
        features, grad_output, self_weight, neigh_weight, bias_vector.reshape(1, hid),
    )

    def load(value):
        (out,) = call(
            load_kernel, "load", [(adjacency.shape, narrow)], [HBM], [VMEM],
            [pltpu.SemaphoreType.DMA], 2, 0, 4 * adjacency.size, value,
        )
        return out

    pair, tiles = swap(adjacency, rows), load(adjacency)
    for step in range(1, top + 1):
        if step == 2:
            up, down, pair, pack, tiles, table = lax.optimization_barrier(
                (up, down, pair, pack, tiles, table)
            )
            packs = [pack] + [send(pack, k, 0, rows, feats) for k in range(1, feats)]
        if step == 3:
            pair = load(pair)
            up = [after(value, pair) for value in up]
            down = [after(value, pair) for value in down]
        if step == top:
            table_pair = swap(after(table, up[0], down[0]), rows)
            sources.append(swap(after(away, up[0], down[0]), rows))
            wanted.append((0, 1))
        for side in range(2):
            flip = side if step == 1 else 0
            forward, backward = ring_pairs(rows, 1, flip), ring_pairs(rows, -1, flip)
            if step < top or side == 0:
                up[side] = lax.ppermute(up[side], "rows", forward)
                sources.append(up[side])
                wanted.append((-step, side))
            if step < top or side == 1:
                down[side] = lax.ppermute(down[side], "rows", backward)
                sources.append(down[side])
                wanted.append((step, side))

    def aggregate(columns, values):
        return call(
            bind(aggregate_kernel, tuple(wanted), rows), "aggregate",
            [((half, width), narrow), ((1, width), wide)],
            [SMEM, VMEM] + [HBM] * len(sources), [VMEM] * 2,
            [pltpu.VMEM((rows, half, width), narrow), pltpu.SemaphoreType.DMA((len(sources),))],
            11, hid * adjacency.size, 2 * adjacency.size + rows * hid * width,
            columns, values, *sources,
        )

    value, unused_inverse = aggregate(table_pair, pair)
    far = [send(value, k, 1, rows, feats) for k in reversed(range(feats))][::-1]
    value, inverse = aggregate(table, tiles)
    near = [value] + [send(value, k, 0, rows, feats) for k in range(1, feats)]

    turned, cot_all, base = call(
        bind(prepare_kernel, feats), "prepare",
        [((every, every), narrow), ((every, width), narrow), ((every, width), wide)],
        [VMEM] * feats, [VMEM] * 3,
        [
            pltpu.VMEM((every, 2 * every), wide),
            pltpu.VMEM((every, 1), wide),
            pltpu.VMEM((every, width), narrow),
        ],
        8, 2 * every * every * width, 4 * every * packed, *packs,
    )
    activation, grad, scaled, agg_own = call(
        bind(middle_kernel, feats), "middle",
        [((hid, width), narrow), ((every, width), narrow)] + [((hid, width), narrow)] * 2,
        [VMEM] * (5 + 2 * feats), [VMEM] * 4,
        [pltpu.VMEM((every, width), narrow), pltpu.VMEM((every, min(width, 256)), wide)], 9,
        3 * every * every * width, 14 * every * width,
        turned, neigh_weight, inverse, base, cot_all, *near, *far,
    )
    scaled_pair = swap(scaled, rows)
    self_own, sums = call(
        weights_kernel, "weights", [((hid, width), wide), ((4, hid + 8, every // 2), wide)],
        [VMEM] * 4, [VMEM] * 2, [], 6, 6 * hid * every * width, 10 * every * width,
        self_weight, features, agg_own, grad,
    )
    (held,) = call(
        arrange_kernel, "arrange", [((2, blocks + 1, hid, tile), narrow)],
        [VMEM] * 2, [VMEM], [], 4, 0, 8 * hid * width, scaled, scaled_pair,
    )

    def spread(offsets, kinds):
        n = 2 * CAP * len(offsets)
        return call(
            bind(spread_kernel, (rows, offsets, kinds)), "spread",
            [((half, width), kind) for kind in kinds],
            [SMEM] * 2 + [VMEM] * 3, [VMEM] * len(kinds), [pltpu.VMEM((hid, width), wide)],
            9, 2 * n * hid * tile * tile, 8 * hid * width * len(offsets),
            table, table_pair, tiles, pair, held,
        )

    def joined(arrived, mine):
        if arrived is None:
            return mine
        (out,) = call(
            join_kernel, "join", [((half, width), narrow)], [VMEM] * 2, [VMEM], [], 3,
            0, 4 * hid * width, arrived, mine,
        )
        return out

    total = sums[:2] + swap(after(sums[2:], scaled_pair), rows, 1)
    total = total + swap(total, rows, 2)
    bit, sends = 4, 0

    def ring(value, pairs):
        nonlocal total, bit, sends
        sends += 1
        if sends >= 6 and sends % 4 == 2 and bit < 2 * rows:
            value = after(value, total)
            total = after(total, value)
            if bit < rows:
                total = total + swap(total, rows, bit)
            bit *= 2
        return lax.ppermute(value, "rows", pairs)

    up, down = [None, None], [None, None]
    forward, backward = ring_pairs(rows, 1), ring_pairs(rows, -1)
    for level in range(top, 0, -1):
        if level == top:
            low, high = spread((top,), (narrow, narrow))
            up[0] = ring(low, forward)
            down[1] = ring(high, backward)
            continue
        kinds = tuple(narrow if arrived is None else wide for arrived in up + down)
        offsets = (level, -level)
        if level == 1:
            offsets, kinds = (1, -1, 0), kinds + (wide, wide)
        mine = spread(offsets, kinds)
        for i in (1, 0):
            flow = 1 - i
            up[i] = ring(joined(up[i], mine[i]), forward)
            down[flow] = ring(joined(down[flow], mine[2 + flow]), backward)
    far = swap(total, rows, 1)
    grad_self, grad_neigh, total = call(
        collect_kernel, "collect",
        [((hid, every), wide), ((hid, every), wide), ((8, every), wide)],
        [VMEM] * 2, [VMEM] * 3, [], 4, 0, 16 * hid * every, total, far,
    )
    grad_bias = lax.dynamic_slice_in_dim(total[0], lax.axis_index("feat") * hid, hid)
    (grad_features,) = call(
        finish_kernel, "finish", [((hid, width), narrow)], [VMEM] * 7, [VMEM], [], 6, 0,
        8 * hid * width, self_own, mine[4], mine[5], up[0], down[0], up[1], down[1],
    )
    return (activation, grad_features, grad_self, grad_neigh, grad_bias)


def solution(mesh):
    in_specs = (
        P("feat", "rows"),
        P("rows", None, None, None),
        P("rows", None),
        P("feat", None),
        P("feat", None),
        P("feat"),
        P("feat", "rows"),
    )
    out_specs = (P("feat", "rows"), P("feat", "rows"), P("feat", None), P("feat", None), P("feat"))
    body = functools.partial(shards, mesh.shape["rows"], mesh.shape["feat"])
    return jax.shard_map(body, mesh=mesh, in_specs=in_specs, out_specs=out_specs, check_vma=False)
```

```python
import functools

import jax
import jax.numpy as jnp
from jax import lax
from jax.experimental import pallas as pl
from jax.experimental.pallas import tpu as pltpu
from jax.sharding import PartitionSpec as P

CAP = 12
MIB = 1024 * 1024
HBM = pl.BlockSpec(memory_space=pltpu.HBM)
VMEM = pl.BlockSpec(memory_space=pltpu.VMEM)
SMEM = pl.BlockSpec(memory_space=pltpu.SMEM)
LAST = (((1,), (1,)), ((), ()))


def params(mib):
    return pltpu.CompilerParams(vmem_limit_bytes=mib * MIB)


def cost(flops, moved):
    return pl.CostEstimate(flops=flops, bytes_accessed=moved, transcendentals=0)


def product(left, right, dims=(((1,), (0,)), ((), ()))):
    return lax.dot_general(left, right, dims, preferred_element_type=jnp.float32)


def ring_pairs(rows, step, flip=0):
    levels, chips = rows // 4, rows // 2
    order = [2 * z for z in range(levels)] + [2 * z + 1 for z in reversed(range(levels))]
    return [
        (2 * order[p] + core, 2 * order[(p + step) % chips] + (core ^ flip))
        for p in range(chips)
        for core in range(2)
    ]


def ring_row(row, offset, rows):
    levels, chips = rows // 4, rows // 2
    z, x, core = row // 4, lax.rem(row // 2, 2), lax.rem(row, 2)
    target = lax.rem(jnp.where(x == 0, z, chips - 1 - z) + (offset + chips), chips)
    low = target < levels
    return 2 * jnp.where(low, 2 * target, 2 * (chips - 1 - target) + 1) + core


def swap(value, rows, bit=1):
    return lax.ppermute(value, "rows", [(r, r ^ bit) for r in range(rows)])


def send(value, k, flip, rows, feats):
    pairs = [
        (r * feats + i, (r ^ flip) * feats + (i + k) % feats)
        for r in range(rows)
        for i in range(feats)
    ]
    return lax.ppermute(value, ("rows", "feat"), pairs)


def after(value, *others):
    return lax.optimization_barrier((value, *others))[0]


def behind(k, feats, size):
    return pl.multiple_of(lax.rem(lax.axis_index("feat") - k + feats, feats) * size, size)


def pack_kernel(feature, grad_output, ws, wn, bias, out, parts, sems):
    hid, every = ws.shape
    width = feature.shape[1]
    copies = []
    for source, low, size in (
        (feature, 0, width),
        (grad_output, width, width),
        (ws, 2 * width, every),
        (wn, 2 * width + every, every),
        (parts, 2 * width + 2 * every, 128),
    ):
        place = out.at[:, pl.ds(low, size)]
        copies.append(pltpu.make_async_copy(source, place, sems.at[len(copies)]))
    line = lax.broadcasted_iota(jnp.int32, (hid, hid), 0)
    lane = lax.broadcasted_iota(jnp.int32, (hid, hid), 1)
    column = jnp.sum(jnp.where(line == lane, bias[...], 0.0), axis=1, keepdims=True)
    high = column.astype(jnp.bfloat16).astype(jnp.float32)
    middle = (column - high).astype(jnp.bfloat16).astype(jnp.float32)
    low = column - high - middle
    at = lax.broadcasted_iota(jnp.int32, (hid, 128), 1)
    value = jnp.where(at == 0, high, jnp.where(at == 1, middle, jnp.where(at == 2, low, 0.0)))
    parts[...] = value.astype(jnp.bfloat16)
    for copy in copies:
        copy.start()
    for copy in copies:
        copy.wait()


def prepare_kernel(feats, *refs):
    packs, (turned, cot_all, base), (weights, bias, x_all) = refs[:feats], refs[feats:-3], refs[-3:]
    hid, width = packs[0].shape[0], x_all.shape[1]
    every = feats * hid
    for k in range(feats):
        at = pl.ds(behind(k, feats, hid), hid)
        pack = packs[k]
        x_all[at] = pack[:, :width]
        cot_all[at] = pack[:, width : 2 * width]
        weights[at] = pack[:, 2 * width : 2 * width + 2 * every].astype(jnp.float32)
        parts = pack[:, 2 * width + 2 * every :].astype(jnp.float32)
        bias[at] = jnp.sum(parts, axis=1, keepdims=True)
    own = weights[:, :every].T.astype(jnp.bfloat16)
    turned[...] = weights[:, every:].T.astype(jnp.bfloat16)
    chunk = min(width, 512)
    for c in range(0, width, chunk):
        lane = pl.ds(c, chunk)
        base[:, lane] = product(own, x_all[:, lane]) + bias[...]


def table_kernel(cols, table, counts):
    blocks, per_block = cols.shape
    base = blocks * per_block
    groups = counts.shape[0]

    def clear(i, carry):
        counts[i] = 0
        for s in range(CAP):
            table[base + i * CAP + s] = -1
        return carry

    lax.fori_loop(0, groups, clear, 0)

    def step(block, carry):
        for t in range(per_block):
            col = cols[block, t]
            group = col // blocks
            seen = counts[group]
            counts[group] = seen + 1
            index = block * per_block + t
            table[index] = col
            table[base + group * CAP + seen] = index * 256 + (col - group * blocks)
        return carry

    lax.fori_loop(0, blocks, step, 0)


def load_kernel(source, out, sem):
    copy = pltpu.make_async_copy(source, out, sem)
    copy.start()
    copy.wait()


def aggregate_kernel(wanted, rows, table, tiles, *refs):
    count = len(wanted)
    blocks, per_block, tile, unused = tiles.shape
    half = refs[0].shape[0]
    sources, (out, inverse, held, sems) = refs[:count], refs[count:]
    row = lax.axis_index("rows")
    copies = []
    for n, (offset, side) in enumerate(wanted):
        place = ring_row(row, offset, rows)
        if side:
            place = place + 1 - 2 * lax.rem(place, 2)
        copies.append(pltpu.make_async_copy(sources[n], held.at[place], sems.at[n]))
    for copy in copies:
        copy.start()
    for copy in copies:
        copy.wait()
    ones = jnp.ones((16, 2 * tile), jnp.bfloat16)

    def step(block, carry):
        total = None
        for t in range(0, per_block, 2):
            left, right = [], []
            for u in (t, t + 1):
                col = table[block * per_block + u]
                source = col // blocks
                at = pl.multiple_of((col - source * blocks) * tile, tile)
                left.append(held[source, :, pl.ds(at, tile)])
                right.append(tiles[block, u])
            term = product(
                jnp.concatenate([jnp.concatenate(left, axis=1), ones], axis=0),
                jnp.concatenate(right, axis=1),
                LAST,
            )
            total = term if total is None else total + term
        factor = 1.0 / total[half : half + 1]
        lane = pl.ds(pl.multiple_of(block * tile, tile), tile)
        out[:, lane] = (total[:half] * factor).astype(jnp.bfloat16)
        inverse[:, lane] = factor
        return carry

    lax.fori_loop(0, blocks, step, 0, unroll=4)


def middle_kernel(feats, turned, wn, inverse, base, cot, *refs):
    near, far, refs = refs[:feats], refs[feats : 2 * feats], refs[2 * feats :]
    act, grad, scaled, agg_own, agg, value = refs
    hid, width = act.shape
    half = hid // 2
    core = lax.rem(lax.axis_index("rows"), 2)
    for k in range(feats):
        first = behind(k, feats, hid)
        agg[pl.ds(pl.multiple_of(first + core * half, half), half)] = near[k][...]
        agg[pl.ds(pl.multiple_of(first + (1 - core) * half, half), half)] = far[k][...]
    own = pl.ds(behind(0, feats, hid), hid)
    agg_own[...] = agg[own]
    chunk = min(width, 256)
    for c in range(0, width, chunk):
        lane = pl.ds(c, chunk)
        pre = product(turned[...], agg[:, lane]) + base[:, lane]
        slope = jnp.exp(jnp.minimum(pre, 0.0))
        grad[:, lane] = (cot[:, lane].astype(jnp.float32) * slope).astype(jnp.bfloat16)
        value[...] = jnp.where(pre > 0, pre, slope - 1.0)
        back = product(wn[...], grad[:, lane])
        scaled[:, lane] = (back * inverse[:, lane]).astype(jnp.bfloat16)
        act[:, lane] = value[own].astype(jnp.bfloat16)


def own_quarter():
    row = lax.axis_index("rows")
    return 2 * lax.rem(row, 2) + lax.rem(row // 2, 2)


def turned_quarter(mine, index):
    core, x = index // 2, index % 2
    core = core + mine // 2 - 2 * core * (mine // 2)
    return 2 * core + x + lax.rem(mine, 2) - 2 * x * lax.rem(mine, 2)


def weights_kernel(ws, x_own, agg_own, grad, self_own, sums):
    hid, every = ws.shape
    g = grad[...]
    self_own[...] = product(ws[...], g)
    wide = every // 2
    mine = own_quarter()
    values = [product(x_own[...], g, LAST), product(agg_own[...], g, LAST)]
    total = product(jnp.ones((8, g.shape[1]), jnp.bfloat16), g, LAST)
    for quarter in range(4):
        slot = turned_quarter(mine, quarter)
        lane = slice(quarter % 2 * wide, (quarter % 2 + 1) * wide)
        sums[slot, :hid] = values[quarter // 2][:, lane]
        sums[slot, hid:] = total[:, lane]


def collect_kernel(pair, pair_far, grad_self, grad_neigh, sums):
    hid, every = grad_self.shape
    wide = every // 2
    mine = own_quarter()
    for slot in range(4):
        value = (pair, pair_far)[slot // 2][slot % 2]
        quarter = turned_quarter(mine, slot)
        for q, out in enumerate((grad_self, grad_self, grad_neigh, grad_neigh)):

            @pl.when(quarter == q)
            def _():
                lane = slice(q % 2 * wide, (q % 2 + 1) * wide)
                out[:, lane] = value[:hid]
                if q < 2:
                    sums[:, lane] = value[hid:]


def arrange_kernel(own, other, held):
    hid, tile = held.shape[2:]
    blocks = held.shape[1] - 1
    for side, source in enumerate((own, other)):
        held[side, blocks] = jnp.zeros((hid, tile), jnp.bfloat16)
        for block in range(blocks):
            held[side, block] = source[:, block * tile : (block + 1) * tile]


def spread_kernel(plan, table, table_pair, adj, pair, held, *refs):
    rows, offsets, kinds = plan
    results, total = refs[:-1], refs[-1]
    blocks, per_block, tile, unused = adj.shape
    half = total.shape[0] // 2
    row = lax.axis_index("rows")
    firsts = [blocks * per_block + ring_row(row, offset, rows) * CAP for offset in offsets]
    for d in range(len(offsets)):
        total[...] = jnp.zeros_like(total)
        for side, (slots, tiles) in enumerate(((table, adj), (table_pair, pair))):
            for s0 in range(0, CAP, 4):
                terms = []
                for s in range(s0, s0 + 4):
                    entry = slots[firsts[d] + s]
                    index = jnp.maximum(entry, 0) // 256
                    block = index // per_block
                    place = jnp.where(entry < 0, blocks, block)
                    lane = lax.rem(jnp.maximum(entry, 0), 256) * tile
                    term = product(held[side, place], tiles[block, index - block * per_block])
                    terms.append((pl.multiple_of(lane, tile), term))
                for lane, term in terms:
                    total[:, pl.ds(lane, tile)] += term
        for part in range(2):
            value = total[part * half : (part + 1) * half]
            results[2 * d + part][...] = value.astype(kinds[2 * d + part])


def join_kernel(arrived, mine, out):
    out[...] = (arrived[...].astype(jnp.float32) + mine[...]).astype(jnp.bfloat16)


def finish_kernel(own, base_low, base_high, a_low, b_low, a_high, b_high, out):
    half = a_low.shape[0]
    for part, (base, a, b) in enumerate(((base_low, a_low, b_low), (base_high, a_high, b_high))):
        lines = slice(part * half, (part + 1) * half)
        value = own[lines] + base[...] + a[...].astype(jnp.float32)
        out[lines] = (value + b[...].astype(jnp.float32)).astype(jnp.bfloat16)


def call(kernel, name, outs, ins, out_specs, scratch, mib, flops, moved, *args):
    return pl.pallas_call(
        kernel,
        out_shape=[jax.ShapeDtypeStruct(shape, kind) for shape, kind in outs],
        in_specs=ins,
        out_specs=out_specs,
        scratch_shapes=scratch,
        compiler_params=params(mib),
        cost_estimate=cost(flops, moved),
        name=name,
    )(*args)


def shards(rows, feats, features, adjacency, tile_cols, self_weight, neigh_weight, bias_vector, grad_output):
    hid, width = features.shape
    blocks, per_block, tile, unused = adjacency.shape
    half = hid // 2
    every = hid * feats
    top = rows // 4
    narrow, wide = jnp.bfloat16, jnp.float32
    bind = functools.partial

    core = lax.rem(lax.axis_index("rows"), 2)
    mine = lax.dynamic_slice_in_dim(features, core * half, half)
    away = lax.dynamic_slice_in_dim(features, (1 - core) * half, half)
    sources, wanted = [mine], [(0, 0)]
    up, down = [mine, away], [mine, away]
    (table,) = call(
        table_kernel, "table", [((tile_cols.size + rows * CAP,), jnp.int32)], [SMEM], [SMEM],
        [pltpu.SMEM((rows,), jnp.int32)], 2, 0, 8 * rows * CAP, tile_cols,
    )
    packed = 2 * width + 2 * every + 128
    (pack,) = call(
        pack_kernel, "pack", [((hid, packed), narrow)], [HBM] * 4 + [VMEM], [VMEM],
        [pltpu.VMEM((hid, 128), narrow), pltpu.SemaphoreType.DMA((5,))], 4, 0,
        4 * hid * packed,
        features, grad_output, self_weight, neigh_weight, bias_vector.reshape(1, hid),
    )

    def load(value):
        (out,) = call(
            load_kernel, "load", [(adjacency.shape, narrow)], [HBM], [VMEM],
            [pltpu.SemaphoreType.DMA], 2, 0, 4 * adjacency.size, value,
        )
        return out

    pair, tiles = swap(adjacency, rows), load(adjacency)
    for step in range(1, top + 1):
        if step == 2:
            up, down, pair, pack, tiles, table = lax.optimization_barrier(
                (up, down, pair, pack, tiles, table)
            )
            packs = [pack] + [send(pack, k, 0, rows, feats) for k in range(1, feats)]
        if step == 3:
            pair = load(pair)
            up = [after(value, pair) for value in up]
            down = [after(value, pair) for value in down]
        if step == top:
            table_pair = swap(after(table, up[0], down[0]), rows)
            sources.append(swap(after(away, up[0], down[0]), rows))
            wanted.append((0, 1))
        for side in range(2):
            flip = side if step == 1 else 0
            forward, backward = ring_pairs(rows, 1, flip), ring_pairs(rows, -1, flip)
            if step < top or side == 0:
                up[side] = lax.ppermute(up[side], "rows", forward)
                sources.append(up[side])
                wanted.append((-step, side))
            if step < top or side == 1:
                down[side] = lax.ppermute(down[side], "rows", backward)
                sources.append(down[side])
                wanted.append((step, side))

    def aggregate(columns, values):
        return call(
            bind(aggregate_kernel, tuple(wanted), rows), "aggregate",
            [((half, width), narrow), ((1, width), wide)],
            [SMEM, VMEM] + [HBM] * len(sources), [VMEM] * 2,
            [pltpu.VMEM((rows, half, width), narrow), pltpu.SemaphoreType.DMA((len(sources),))],
            11, hid * adjacency.size, 2 * adjacency.size + rows * hid * width,
            columns, values, *sources,
        )

    value, unused_inverse = aggregate(table_pair, pair)
    far = [send(value, k, 1, rows, feats) for k in reversed(range(feats))][::-1]
    value, inverse = aggregate(table, tiles)
    near = [value] + [send(value, k, 0, rows, feats) for k in range(1, feats)]

    turned, cot_all, base = call(
        bind(prepare_kernel, feats), "prepare",
        [((every, every), narrow), ((every, width), narrow), ((every, width), wide)],
        [VMEM] * feats, [VMEM] * 3,
        [
            pltpu.VMEM((every, 2 * every), wide),
            pltpu.VMEM((every, 1), wide),
            pltpu.VMEM((every, width), narrow),
        ],
        8, 2 * every * every * width, 4 * every * packed, *packs,
    )
    activation, grad, scaled, agg_own = call(
        bind(middle_kernel, feats), "middle",
        [((hid, width), narrow), ((every, width), narrow)] + [((hid, width), narrow)] * 2,
        [VMEM] * (5 + 2 * feats), [VMEM] * 4,
        [pltpu.VMEM((every, width), narrow), pltpu.VMEM((every, min(width, 256)), wide)], 9,
        3 * every * every * width, 14 * every * width,
        turned, neigh_weight, inverse, base, cot_all, *near, *far,
    )
    scaled_pair = swap(scaled, rows)
    self_own, sums = call(
        weights_kernel, "weights", [((hid, width), wide), ((4, hid + 8, every // 2), wide)],
        [VMEM] * 4, [VMEM] * 2, [], 6, 6 * hid * every * width, 10 * every * width,
        self_weight, features, agg_own, grad,
    )
    (held,) = call(
        arrange_kernel, "arrange", [((2, blocks + 1, hid, tile), narrow)],
        [VMEM] * 2, [VMEM], [], 4, 0, 8 * hid * width, scaled, scaled_pair,
    )

    def spread(offsets, kinds):
        n = 2 * CAP * len(offsets)
        return call(
            bind(spread_kernel, (rows, offsets, kinds)), "spread",
            [((half, width), kind) for kind in kinds],
            [SMEM] * 2 + [VMEM] * 3, [VMEM] * len(kinds), [pltpu.VMEM((hid, width), wide)],
            9, 2 * n * hid * tile * tile, 8 * hid * width * len(offsets),
            table, table_pair, tiles, pair, held,
        )

    def joined(arrived, mine):
        if arrived is None:
            return mine
        (out,) = call(
            join_kernel, "join", [((half, width), narrow)], [VMEM] * 2, [VMEM], [], 3,
            0, 4 * hid * width, arrived, mine,
        )
        return out

    near = sums[:2] + swap(after(sums[2:], scaled_pair), rows, 1)
    total = near[0] + swap(near[1], rows, 2)
    bit, sends = 4, 0

    def ring(value, pairs):
        nonlocal total, bit, sends
        sends += 1
        due = sends in (3, 5) or (sends >= 10 and sends % 4 == 2)
        if due and bit < 2 * rows:
            value = after(value, total)
            total = after(total, value) if sends >= 10 else total
            if bit < rows:
                total = total + swap(total, rows, bit)
            bit *= 2
        return lax.ppermute(value, "rows", pairs)

    up, down = [None, None], [None, None]
    forward, backward = ring_pairs(rows, 1), ring_pairs(rows, -1)
    for level in range(top, 0, -1):
        if level == top:
            low, high = spread((top,), (narrow, narrow))
            up[0] = ring(low, forward)
            down[1] = ring(high, backward)
            continue
        kinds = tuple(narrow if arrived is None else wide for arrived in up + down)
        offsets = (level, -level)
        if level == 1:
            offsets, kinds = (1, -1, 0), kinds + (wide, wide)
        mine = spread(offsets, kinds)
        for i in (1, 0):
            flow = 1 - i
            up[i] = ring(joined(up[i], mine[i]), forward)
            down[flow] = ring(joined(down[flow], mine[2 + flow]), backward)
    near = jnp.stack([total, swap(total, rows, 2)])
    far = swap(near, rows, 1)
    grad_self, grad_neigh, total = call(
        collect_kernel, "collect",
        [((hid, every), wide), ((hid, every), wide), ((8, every), wide)],
        [VMEM] * 2, [VMEM] * 3, [], 4, 0, 16 * hid * every, near, far,
    )
    grad_bias = lax.dynamic_slice_in_dim(total[0], lax.axis_index("feat") * hid, hid)
    (grad_features,) = call(
        finish_kernel, "finish", [((hid, width), narrow)], [VMEM] * 7, [VMEM], [], 6, 0,
        8 * hid * width, self_own, mine[4], mine[5], up[0], down[0], up[1], down[1],
    )
    return (activation, grad_features, grad_self, grad_neigh, grad_bias)


def solution(mesh):
    in_specs = (
        P("feat", "rows"),
        P("rows", None, None, None),
        P("rows", None),
        P("feat", None),
        P("feat", None),
        P("feat"),
        P("feat", "rows"),
    )
    out_specs = (P("feat", "rows"), P("feat", "rows"), P("feat", None), P("feat", None), P("feat"))
    body = functools.partial(shards, mesh.shape["rows"], mesh.shape["feat"])
    return jax.shard_map(body, mesh=mesh, in_specs=in_specs, out_specs=out_specs, check_vma=False)
```

```python
import functools

import jax
import jax.numpy as jnp
from jax import lax
from jax.experimental import pallas as pl
from jax.experimental.pallas import tpu as pltpu
from jax.sharding import PartitionSpec as P

CAP = 12
MIB = 1024 * 1024
HBM = pl.BlockSpec(memory_space=pltpu.HBM)
VMEM = pl.BlockSpec(memory_space=pltpu.VMEM)
SMEM = pl.BlockSpec(memory_space=pltpu.SMEM)
LAST = (((1,), (1,)), ((), ()))


def params(mib):
    return pltpu.CompilerParams(vmem_limit_bytes=mib * MIB)


def cost(flops, moved):
    return pl.CostEstimate(flops=flops, bytes_accessed=moved, transcendentals=0)


def product(left, right, dims=(((1,), (0,)), ((), ()))):
    return lax.dot_general(left, right, dims, preferred_element_type=jnp.float32)


def ring_pairs(rows, step, flip=0):
    levels, chips = rows // 4, rows // 2
    order = [2 * z for z in range(levels)] + [2 * z + 1 for z in reversed(range(levels))]
    return [
        (2 * order[p] + core, 2 * order[(p + step) % chips] + (core ^ flip))
        for p in range(chips)
        for core in range(2)
    ]


def ring_row(row, offset, rows):
    levels, chips = rows // 4, rows // 2
    z, x, core = row // 4, lax.rem(row // 2, 2), lax.rem(row, 2)
    target = lax.rem(jnp.where(x == 0, z, chips - 1 - z) + (offset + chips), chips)
    low = target < levels
    return 2 * jnp.where(low, 2 * target, 2 * (chips - 1 - target) + 1) + core


def swap(value, rows, bit=1):
    return lax.ppermute(value, "rows", [(r, r ^ bit) for r in range(rows)])


def send(value, k, flip, rows, feats):
    pairs = [
        (r * feats + i, (r ^ flip) * feats + (i + k) % feats)
        for r in range(rows)
        for i in range(feats)
    ]
    return lax.ppermute(value, ("rows", "feat"), pairs)


def after(value, *others):
    return lax.optimization_barrier((value, *others))[0]


def behind(k, feats, size):
    return pl.multiple_of(lax.rem(lax.axis_index("feat") - k + feats, feats) * size, size)


def pack_kernel(feature, grad_output, ws, wn, bias, out, parts, sems):
    hid, every = ws.shape
    width = feature.shape[1]
    copies = []
    for source, low, size in (
        (feature, 0, width),
        (grad_output, width, width),
        (ws, 2 * width, every),
        (wn, 2 * width + every, every),
        (parts, 2 * width + 2 * every, 128),
    ):
        place = out.at[:, pl.ds(low, size)]
        copies.append(pltpu.make_async_copy(source, place, sems.at[len(copies)]))
    line = lax.broadcasted_iota(jnp.int32, (hid, hid), 0)
    lane = lax.broadcasted_iota(jnp.int32, (hid, hid), 1)
    column = jnp.sum(jnp.where(line == lane, bias[...], 0.0), axis=1, keepdims=True)
    high = column.astype(jnp.bfloat16).astype(jnp.float32)
    middle = (column - high).astype(jnp.bfloat16).astype(jnp.float32)
    low = column - high - middle
    at = lax.broadcasted_iota(jnp.int32, (hid, 128), 1)
    value = jnp.where(at == 0, high, jnp.where(at == 1, middle, jnp.where(at == 2, low, 0.0)))
    parts[...] = value.astype(jnp.bfloat16)
    for copy in copies:
        copy.start()
    for copy in copies:
        copy.wait()


def prepare_kernel(feats, *refs):
    packs, (turned, cot_all, base), (weights, bias, x_all) = refs[:feats], refs[feats:-3], refs[-3:]
    hid, width = packs[0].shape[0], x_all.shape[1]
    every = feats * hid
    for k in range(feats):
        at = pl.ds(behind(k, feats, hid), hid)
        pack = packs[k]
        x_all[at] = pack[:, :width]
        cot_all[at] = pack[:, width : 2 * width]
        weights[at] = pack[:, 2 * width : 2 * width + 2 * every].astype(jnp.float32)
        parts = pack[:, 2 * width + 2 * every :].astype(jnp.float32)
        bias[at] = jnp.sum(parts, axis=1, keepdims=True)
    own = weights[:, :every].T.astype(jnp.bfloat16)
    turned[...] = weights[:, every:].T.astype(jnp.bfloat16)
    chunk = min(width, 512)
    for c in range(0, width, chunk):
        lane = pl.ds(c, chunk)
        base[:, lane] = product(own, x_all[:, lane]) + bias[...]


def table_kernel(cols, table, counts):
    blocks, per_block = cols.shape
    base = blocks * per_block
    groups = counts.shape[0]

    def clear(i, carry):
        counts[i] = 0
        for s in range(CAP):
            table[base + i * CAP + s] = -1
        return carry

    lax.fori_loop(0, groups, clear, 0)

    def step(block, carry):
        for t in range(per_block):
            col = cols[block, t]
            group = col // blocks
            seen = counts[group]
            counts[group] = seen + 1
            index = block * per_block + t
            table[index] = col
            table[base + group * CAP + seen] = index * 256 + (col - group * blocks)
        return carry

    lax.fori_loop(0, blocks, step, 0)


def load_kernel(source, out, sem):
    copy = pltpu.make_async_copy(source, out, sem)
    copy.start()
    copy.wait()


def aggregate_kernel(wanted, rows, table, tiles, *refs):
    count = len(wanted)
    blocks, per_block, tile, unused = tiles.shape
    half = refs[0].shape[0]
    sources, (out, inverse, held, sems) = refs[:count], refs[count:]
    row = lax.axis_index("rows")
    copies = []
    for n, (offset, side) in enumerate(wanted):
        place = ring_row(row, offset, rows)
        if side:
            place = place + 1 - 2 * lax.rem(place, 2)
        copies.append(pltpu.make_async_copy(sources[n], held.at[place], sems.at[n]))
    for copy in copies:
        copy.start()
    for copy in copies:
        copy.wait()
    ones = jnp.ones((16, 2 * tile), jnp.bfloat16)

    def step(block, carry):
        total = None
        for t in range(0, per_block, 2):
            left, right = [], []
            for u in (t, t + 1):
                col = table[block * per_block + u]
                source = col // blocks
                at = pl.multiple_of((col - source * blocks) * tile, tile)
                left.append(held[source, :, pl.ds(at, tile)])
                right.append(tiles[block, u])
            term = product(
                jnp.concatenate([jnp.concatenate(left, axis=1), ones], axis=0),
                jnp.concatenate(right, axis=1),
                LAST,
            )
            total = term if total is None else total + term
        factor = 1.0 / total[half : half + 1]
        lane = pl.ds(pl.multiple_of(block * tile, tile), tile)
        out[:, lane] = (total[:half] * factor).astype(jnp.bfloat16)
        inverse[:, lane] = factor
        return carry

    lax.fori_loop(0, blocks, step, 0, unroll=4)


def middle_kernel(feats, turned, wn, inverse, base, cot, *refs):
    near, far, refs = refs[:feats], refs[feats : 2 * feats], refs[2 * feats :]
    act, grad, scaled, agg_own, agg, value = refs
    hid, width = act.shape
    half = hid // 2
    core = lax.rem(lax.axis_index("rows"), 2)
    for k in range(feats):
        first = behind(k, feats, hid)
        agg[pl.ds(pl.multiple_of(first + core * half, half), half)] = near[k][...]
        agg[pl.ds(pl.multiple_of(first + (1 - core) * half, half), half)] = far[k][...]
    own = pl.ds(behind(0, feats, hid), hid)
    agg_own[...] = agg[own]
    chunk = min(width, 256)
    for c in range(0, width, chunk):
        lane = pl.ds(c, chunk)
        pre = product(turned[...], agg[:, lane]) + base[:, lane]
        slope = jnp.exp(jnp.minimum(pre, 0.0))
        grad[:, lane] = (cot[:, lane].astype(jnp.float32) * slope).astype(jnp.bfloat16)
        value[...] = jnp.where(pre > 0, pre, slope - 1.0)
        back = product(wn[...], grad[:, lane])
        scaled[:, lane] = (back * inverse[:, lane]).astype(jnp.bfloat16)
        act[:, lane] = value[own].astype(jnp.bfloat16)


def own_quarter():
    row = lax.axis_index("rows")
    return 2 * lax.rem(row, 2) + lax.rem(row // 2, 2)


def turned_quarter(mine, index):
    core, x = index // 2, index % 2
    core = core + mine // 2 - 2 * core * (mine // 2)
    return 2 * core + x + lax.rem(mine, 2) - 2 * x * lax.rem(mine, 2)


def weights_kernel(ws, x_own, agg_own, grad, self_own, sums):
    hid, every = ws.shape
    g = grad[...]
    self_own[...] = product(ws[...], g)
    wide = every // 2
    mine = own_quarter()
    values = [product(x_own[...], g, LAST), product(agg_own[...], g, LAST)]
    total = product(jnp.ones((8, g.shape[1]), jnp.bfloat16), g, LAST)
    for quarter in range(4):
        slot = turned_quarter(mine, quarter)
        lane = slice(quarter % 2 * wide, (quarter % 2 + 1) * wide)
        sums[slot, :hid] = values[quarter // 2][:, lane]
        sums[slot, hid:] = total[:, lane]


def collect_kernel(pair, pair_far, grad_self, grad_neigh, sums):
    hid, every = grad_self.shape
    wide = every // 2
    mine = own_quarter()
    for slot in range(4):
        value = (pair, pair_far)[slot // 2][slot % 2]
        quarter = turned_quarter(mine, slot)
        for q, out in enumerate((grad_self, grad_self, grad_neigh, grad_neigh)):

            @pl.when(quarter == q)
            def _():
                lane = slice(q % 2 * wide, (q % 2 + 1) * wide)
                out[:, lane] = value[:hid]
                if q < 2:
                    sums[:, lane] = value[hid:]


def arrange_kernel(own, other, held):
    hid, tile = held.shape[2:]
    blocks = held.shape[1] - 1
    for side, source in enumerate((own, other)):
        held[side, blocks] = jnp.zeros((hid, tile), jnp.bfloat16)
        for block in range(blocks):
            held[side, block] = source[:, block * tile : (block + 1) * tile]


def spread_kernel(plan, table, table_pair, adj, pair, held, *refs):
    rows, offsets, kinds = plan
    results, total = refs[:-1], refs[-1]
    blocks, per_block, tile, unused = adj.shape
    half = total.shape[0] // 2
    row = lax.axis_index("rows")
    firsts = [blocks * per_block + ring_row(row, offset, rows) * CAP for offset in offsets]
    for d in range(len(offsets)):
        total[...] = jnp.zeros_like(total)
        for side, (slots, tiles) in enumerate(((table, adj), (table_pair, pair))):
            for s0 in range(0, CAP, 4):
                terms = []
                for s in range(s0, s0 + 4):
                    entry = slots[firsts[d] + s]
                    index = jnp.maximum(entry, 0) // 256
                    block = index // per_block
                    place = jnp.where(entry < 0, blocks, block)
                    lane = lax.rem(jnp.maximum(entry, 0), 256) * tile
                    term = product(held[side, place], tiles[block, index - block * per_block])
                    terms.append((pl.multiple_of(lane, tile), term))
                for lane, term in terms:
                    total[:, pl.ds(lane, tile)] += term
        for part in range(2):
            value = total[part * half : (part + 1) * half]
            results[2 * d + part][...] = value.astype(kinds[2 * d + part])


def join_kernel(arrived, mine, out):
    out[...] = (arrived[...].astype(jnp.float32) + mine[...]).astype(jnp.bfloat16)


def finish_kernel(own, base_low, base_high, a_low, b_low, a_high, b_high, out):
    half = a_low.shape[0]
    for part, (base, a, b) in enumerate(((base_low, a_low, b_low), (base_high, a_high, b_high))):
        lines = slice(part * half, (part + 1) * half)
        value = own[lines] + base[...] + a[...].astype(jnp.float32)
        out[lines] = (value + b[...].astype(jnp.float32)).astype(jnp.bfloat16)


def call(kernel, name, outs, ins, out_specs, scratch, mib, flops, moved, *args):
    return pl.pallas_call(
        kernel,
        out_shape=[jax.ShapeDtypeStruct(shape, kind) for shape, kind in outs],
        in_specs=ins,
        out_specs=out_specs,
        scratch_shapes=scratch,
        compiler_params=params(mib),
        cost_estimate=cost(flops, moved),
        name=name,
    )(*args)


def shards(rows, feats, features, adjacency, tile_cols, self_weight, neigh_weight, bias_vector, grad_output):
    hid, width = features.shape
    blocks, per_block, tile, unused = adjacency.shape
    half = hid // 2
    every = hid * feats
    top = rows // 4
    narrow, wide = jnp.bfloat16, jnp.float32
    bind = functools.partial

    core = lax.rem(lax.axis_index("rows"), 2)
    mine = lax.dynamic_slice_in_dim(features, core * half, half)
    away = lax.dynamic_slice_in_dim(features, (1 - core) * half, half)
    sources, wanted = [mine], [(0, 0)]
    up, down = [mine, away], [mine, away]
    (table,) = call(
        table_kernel, "table", [((tile_cols.size + rows * CAP,), jnp.int32)], [SMEM], [SMEM],
        [pltpu.SMEM((rows,), jnp.int32)], 2, 0, 8 * rows * CAP, tile_cols,
    )
    packed = 2 * width + 2 * every + 128
    (pack,) = call(
        pack_kernel, "pack", [((hid, packed), narrow)], [HBM] * 4 + [VMEM], [VMEM],
        [pltpu.VMEM((hid, 128), narrow), pltpu.SemaphoreType.DMA((5,))], 4, 0,
        4 * hid * packed,
        features, grad_output, self_weight, neigh_weight, bias_vector.reshape(1, hid),
    )

    def load(value):
        (out,) = call(
            load_kernel, "load", [(adjacency.shape, narrow)], [HBM], [VMEM],
            [pltpu.SemaphoreType.DMA], 2, 0, 4 * adjacency.size, value,
        )
        return out

    pair, tiles = swap(adjacency, rows), load(adjacency)
    for step in range(1, top + 1):
        if step == 2:
            up, down, pair, pack, tiles, table = lax.optimization_barrier(
                (up, down, pair, pack, tiles, table)
            )
            packs = [pack] + [send(pack, k, 0, rows, feats) for k in range(1, feats)]
        if step == 3:
            pair = load(pair)
            up = [after(value, pair) for value in up]
            down = [after(value, pair) for value in down]
        if step == top:
            table_pair = swap(after(table, up[0], down[0]), rows)
            sources.append(swap(after(away, up[0], down[0]), rows))
            wanted.append((0, 1))
        for side in range(2):
            flip = side if step == 1 else 0
            forward, backward = ring_pairs(rows, 1, flip), ring_pairs(rows, -1, flip)
            if step < top or side == 0:
                up[side] = lax.ppermute(up[side], "rows", forward)
                sources.append(up[side])
                wanted.append((-step, side))
            if step < top or side == 1:
                down[side] = lax.ppermute(down[side], "rows", backward)
                sources.append(down[side])
                wanted.append((step, side))

    def aggregate(columns, values):
        return call(
            bind(aggregate_kernel, tuple(wanted), rows), "aggregate",
            [((half, width), narrow), ((1, width), wide)],
            [SMEM, VMEM] + [HBM] * len(sources), [VMEM] * 2,
            [pltpu.VMEM((rows, half, width), narrow), pltpu.SemaphoreType.DMA((len(sources),))],
            11, hid * adjacency.size, 2 * adjacency.size + rows * hid * width,
            columns, values, *sources,
        )

    value, unused_inverse = aggregate(table_pair, pair)
    far = [send(value, k, 1, rows, feats) for k in reversed(range(feats))][::-1]
    value, inverse = aggregate(table, tiles)
    near = [value] + [send(value, k, 0, rows, feats) for k in range(1, feats)]

    turned, cot_all, base = call(
        bind(prepare_kernel, feats), "prepare",
        [((every, every), narrow), ((every, width), narrow), ((every, width), wide)],
        [VMEM] * feats, [VMEM] * 3,
        [
            pltpu.VMEM((every, 2 * every), wide),
            pltpu.VMEM((every, 1), wide),
            pltpu.VMEM((every, width), narrow),
        ],
        8, 2 * every * every * width, 4 * every * packed, *packs,
    )
    activation, grad, scaled, agg_own = call(
        bind(middle_kernel, feats), "middle",
        [((hid, width), narrow), ((every, width), narrow)] + [((hid, width), narrow)] * 2,
        [VMEM] * (5 + 2 * feats), [VMEM] * 4,
        [pltpu.VMEM((every, width), narrow), pltpu.VMEM((every, min(width, 256)), wide)], 9,
        3 * every * every * width, 14 * every * width,
        turned, neigh_weight, inverse, base, cot_all, *near, *far,
    )
    scaled_pair = swap(scaled, rows)
    self_own, sums = call(
        weights_kernel, "weights", [((hid, width), wide), ((4, hid + 8, every // 2), wide)],
        [VMEM] * 4, [VMEM] * 2, [], 6, 6 * hid * every * width, 10 * every * width,
        self_weight, features, agg_own, grad,
    )
    (held,) = call(
        arrange_kernel, "arrange", [((2, blocks + 1, hid, tile), narrow)],
        [VMEM] * 2, [VMEM], [], 4, 0, 8 * hid * width, scaled, scaled_pair,
    )

    def spread(offsets, kinds, gate=None):
        n = 2 * CAP * len(offsets)
        return call(
            bind(spread_kernel, (rows, offsets, kinds)), "spread",
            [((half, width), kind) for kind in kinds],
            [SMEM] * 2 + [VMEM] * 3, [VMEM] * len(kinds), [pltpu.VMEM((hid, width), wide)],
            9, 2 * n * hid * tile * tile, 8 * hid * width * len(offsets),
            table, table_pair, tiles, pair, held if gate is None else after(held, gate),
        )

    def joined(arrived, mine):
        if arrived is None:
            return mine
        (out,) = call(
            join_kernel, "join", [((half, width), narrow)], [VMEM] * 2, [VMEM], [], 3,
            0, 4 * hid * width, arrived, mine,
        )
        return out

    near = sums[:2] + swap(after(sums[2:], scaled_pair), rows, 1)
    total = near[0] + swap(near[1], rows, 2)
    bit, sends = 4, 0

    def ring(value, pairs):
        nonlocal total, bit, sends
        sends += 1
        if sends % 7 == 5 and bit < rows:
            total = total + after(swap(total, rows, bit), value)
            bit *= 2
        if sends == 9:
            value = after(value, total)
        return lax.ppermute(value, "rows", pairs)

    up, down = [None, None], [None, None]
    forward, backward = ring_pairs(rows, 1), ring_pairs(rows, -1)
    low, high = spread((top,), (narrow, narrow))
    up[0], down[1] = ring(low, forward), ring(high, backward)
    mine = spread((top - 1, 1 - top), (wide, narrow, narrow, wide))
    for level in range(top - 1, 0, -1):
        offsets = (level - 1, 1 - level) if level > 1 else (0,)
        later = spread(offsets, (wide, wide) * len(offsets))
        for i in (1, 0):
            flow = 1 - i
            value = joined(up[i], mine[i])
            if i == 1 and level > 1:
                value = after(value, later[0])
            up[i] = ring(value, forward)
            down[flow] = ring(joined(down[flow], mine[2 + flow]), backward)
        mine = later
    while bit < rows:
        total = total + swap(total, rows, bit)
        bit *= 2
    near = jnp.stack([total, swap(total, rows, 2)])
    far = swap(near, rows, 1)
    grad_self, grad_neigh, total = call(
        collect_kernel, "collect",
        [((hid, every), wide), ((hid, every), wide), ((8, every), wide)],
        [VMEM] * 2, [VMEM] * 3, [], 4, 0, 16 * hid * every, near, far,
    )
    grad_bias = lax.dynamic_slice_in_dim(total[0], lax.axis_index("feat") * hid, hid)
    (grad_features,) = call(
        finish_kernel, "finish", [((hid, width), narrow)], [VMEM] * 7, [VMEM], [], 6, 0,
        8 * hid * width, self_own, *mine, up[0], down[0], up[1], down[1],
    )
    return (activation, grad_features, grad_self, grad_neigh, grad_bias)


def solution(mesh):
    in_specs = (
        P("feat", "rows"),
        P("rows", None, None, None),
        P("rows", None),
        P("feat", None),
        P("feat", None),
        P("feat"),
        P("feat", "rows"),
    )
    out_specs = (P("feat", "rows"), P("feat", "rows"), P("feat", None), P("feat", None), P("feat"))
    body = functools.partial(shards, mesh.shape["rows"], mesh.shape["feat"])
    return jax.shard_map(body, mesh=mesh, in_specs=in_specs, out_specs=out_specs, check_vma=False)
```

```python
import functools

import jax
import jax.numpy as jnp
from jax import lax
from jax.experimental import pallas as pl
from jax.experimental.pallas import tpu as pltpu
from jax.sharding import PartitionSpec as P

CAP = 12
MIB = 1024 * 1024
HBM = pl.BlockSpec(memory_space=pltpu.HBM)
VMEM = pl.BlockSpec(memory_space=pltpu.VMEM)
SMEM = pl.BlockSpec(memory_space=pltpu.SMEM)
LAST = (((1,), (1,)), ((), ()))


def params(mib):
    return pltpu.CompilerParams(vmem_limit_bytes=mib * MIB)


def cost(flops, moved):
    return pl.CostEstimate(flops=flops, bytes_accessed=moved, transcendentals=0)


def product(left, right, dims=(((1,), (0,)), ((), ()))):
    return lax.dot_general(left, right, dims, preferred_element_type=jnp.float32)


def ring_pairs(rows, step, flip=0):
    levels, chips = rows // 4, rows // 2
    order = [2 * z for z in range(levels)] + [2 * z + 1 for z in reversed(range(levels))]
    return [
        (2 * order[p] + core, 2 * order[(p + step) % chips] + (core ^ flip))
        for p in range(chips)
        for core in range(2)
    ]


def ring_row(row, offset, rows):
    levels, chips = rows // 4, rows // 2
    z, x, core = row // 4, lax.rem(row // 2, 2), lax.rem(row, 2)
    target = lax.rem(jnp.where(x == 0, z, chips - 1 - z) + (offset + chips), chips)
    low = target < levels
    return 2 * jnp.where(low, 2 * target, 2 * (chips - 1 - target) + 1) + core


def swap(value, rows, bit=1):
    return lax.ppermute(value, "rows", [(r, r ^ bit) for r in range(rows)])


def send(value, k, flip, rows, feats):
    pairs = [
        (r * feats + i, (r ^ flip) * feats + (i + k) % feats)
        for r in range(rows)
        for i in range(feats)
    ]
    return lax.ppermute(value, ("rows", "feat"), pairs)


def after(value, *others):
    return lax.optimization_barrier((value, *others))[0]


def behind(k, feats, size):
    return pl.multiple_of(lax.rem(lax.axis_index("feat") - k + feats, feats) * size, size)


def pack_kernel(feature, grad_output, ws, wn, bias, out, parts, sems):
    hid, every = ws.shape
    width = feature.shape[1]
    copies = []
    for source, low, size in (
        (feature, 0, width),
        (grad_output, width, width),
        (ws, 2 * width, every),
        (wn, 2 * width + every, every),
        (parts, 2 * width + 2 * every, 128),
    ):
        place = out.at[:, pl.ds(low, size)]
        copies.append(pltpu.make_async_copy(source, place, sems.at[len(copies)]))
    line = lax.broadcasted_iota(jnp.int32, (hid, hid), 0)
    lane = lax.broadcasted_iota(jnp.int32, (hid, hid), 1)
    column = jnp.sum(jnp.where(line == lane, bias[...], 0.0), axis=1, keepdims=True)
    high = column.astype(jnp.bfloat16).astype(jnp.float32)
    middle = (column - high).astype(jnp.bfloat16).astype(jnp.float32)
    low = column - high - middle
    at = lax.broadcasted_iota(jnp.int32, (hid, 128), 1)
    value = jnp.where(at == 0, high, jnp.where(at == 1, middle, jnp.where(at == 2, low, 0.0)))
    parts[...] = value.astype(jnp.bfloat16)
    for copy in copies:
        copy.start()
    for copy in copies:
        copy.wait()


def prepare_kernel(feats, *refs):
    packs, (turned, cot_all, base), (weights, bias, x_all) = refs[:feats], refs[feats:-3], refs[-3:]
    hid, width = packs[0].shape[0], x_all.shape[1]
    every = feats * hid
    for k in range(feats):
        at = pl.ds(behind(k, feats, hid), hid)
        pack = packs[k]
        x_all[at] = pack[:, :width]
        cot_all[at] = pack[:, width : 2 * width]
        weights[at] = pack[:, 2 * width : 2 * width + 2 * every].astype(jnp.float32)
        parts = pack[:, 2 * width + 2 * every :].astype(jnp.float32)
        bias[at] = jnp.sum(parts, axis=1, keepdims=True)
    own = weights[:, :every].T.astype(jnp.bfloat16)
    turned[...] = weights[:, every:].T.astype(jnp.bfloat16)
    chunk = min(width, 512)
    for c in range(0, width, chunk):
        lane = pl.ds(c, chunk)
        base[:, lane] = product(own, x_all[:, lane]) + bias[...]


def table_kernel(cols, table, counts):
    blocks, per_block = cols.shape
    base = blocks * per_block
    groups = counts.shape[0]

    def clear(i, carry):
        counts[i] = 0
        for s in range(CAP):
            table[base + i * CAP + s] = -1
        return carry

    lax.fori_loop(0, groups, clear, 0)

    def step(block, carry):
        for t in range(per_block):
            col = cols[block, t]
            group = col // blocks
            seen = counts[group]
            counts[group] = seen + 1
            index = block * per_block + t
            table[index] = col
            table[base + group * CAP + seen] = index * 256 + (col - group * blocks)
        return carry

    lax.fori_loop(0, blocks, step, 0)


def load_kernel(source, out, sem):
    copy = pltpu.make_async_copy(source, out, sem)
    copy.start()
    copy.wait()


def aggregate_kernel(wanted, rows, table, tiles, *refs):
    count = len(wanted)
    blocks, per_block, tile, unused = tiles.shape
    half = refs[0].shape[0]
    sources, (out, inverse, held, sems) = refs[:count], refs[count:]
    row = lax.axis_index("rows")
    copies = []
    for n, (offset, side) in enumerate(wanted):
        place = ring_row(row, offset, rows)
        if side:
            place = place + 1 - 2 * lax.rem(place, 2)
        copies.append(pltpu.make_async_copy(sources[n], held.at[place], sems.at[n]))
    for copy in copies:
        copy.start()
    for copy in copies:
        copy.wait()
    ones = jnp.ones((16, 2 * tile), jnp.bfloat16)

    def step(block, carry):
        total = None
        for t in range(0, per_block, 2):
            left, right = [], []
            for u in (t, t + 1):
                col = table[block * per_block + u]
                source = col // blocks
                at = pl.multiple_of((col - source * blocks) * tile, tile)
                left.append(held[source, :, pl.ds(at, tile)])
                right.append(tiles[block, u])
            term = product(
                jnp.concatenate([jnp.concatenate(left, axis=1), ones], axis=0),
                jnp.concatenate(right, axis=1),
                LAST,
            )
            total = term if total is None else total + term
        factor = 1.0 / total[half : half + 1]
        lane = pl.ds(pl.multiple_of(block * tile, tile), tile)
        out[:, lane] = (total[:half] * factor).astype(jnp.bfloat16)
        inverse[:, lane] = factor
        return carry

    lax.fori_loop(0, blocks, step, 0, unroll=4)


def middle_kernel(feats, turned, wn, inverse, base, cot, *refs):
    near, far, refs = refs[:feats], refs[feats : 2 * feats], refs[2 * feats :]
    act, grad, scaled, agg_own, agg, value = refs
    hid, width = act.shape
    half = hid // 2
    core = lax.rem(lax.axis_index("rows"), 2)
    for k in range(feats):
        first = behind(k, feats, hid)
        agg[pl.ds(pl.multiple_of(first + core * half, half), half)] = near[k][...]
        agg[pl.ds(pl.multiple_of(first + (1 - core) * half, half), half)] = far[k][...]
    own = pl.ds(behind(0, feats, hid), hid)
    agg_own[...] = agg[own]
    chunk = min(width, 256)
    for c in range(0, width, chunk):
        lane = pl.ds(c, chunk)
        pre = product(turned[...], agg[:, lane]) + base[:, lane]
        slope = jnp.exp(jnp.minimum(pre, 0.0))
        grad[:, lane] = (cot[:, lane].astype(jnp.float32) * slope).astype(jnp.bfloat16)
        value[...] = jnp.where(pre > 0, pre, slope - 1.0)
        back = product(wn[...], grad[:, lane])
        scaled[:, lane] = (back * inverse[:, lane]).astype(jnp.bfloat16)
        act[:, lane] = value[own].astype(jnp.bfloat16)


def own_quarter():
    row = lax.axis_index("rows")
    return 2 * lax.rem(row, 2) + lax.rem(row // 2, 2)


def turned_quarter(mine, index):
    core, x = index // 2, index % 2
    core = core + mine // 2 - 2 * core * (mine // 2)
    return 2 * core + x + lax.rem(mine, 2) - 2 * x * lax.rem(mine, 2)


def weights_kernel(ws, x_own, agg_own, grad, self_own, sums):
    hid, every = ws.shape
    g = grad[...]
    self_own[...] = product(ws[...], g)
    wide = every // 2
    mine = own_quarter()
    values = [product(x_own[...], g, LAST), product(agg_own[...], g, LAST)]
    total = product(jnp.ones((8, g.shape[1]), jnp.bfloat16), g, LAST)
    for quarter in range(4):
        slot = turned_quarter(mine, quarter)
        lane = slice(quarter % 2 * wide, (quarter % 2 + 1) * wide)
        sums[slot, :hid] = values[quarter // 2][:, lane]
        sums[slot, hid:] = total[:, lane]


def collect_kernel(pair, pair_far, grad_self, grad_neigh, sums):
    hid, every = grad_self.shape
    wide = every // 2
    mine = own_quarter()
    for slot in range(4):
        value = (pair, pair_far)[slot // 2][slot % 2]
        quarter = turned_quarter(mine, slot)
        for q, out in enumerate((grad_self, grad_self, grad_neigh, grad_neigh)):

            @pl.when(quarter == q)
            def _():
                lane = slice(q % 2 * wide, (q % 2 + 1) * wide)
                out[:, lane] = value[:hid]
                if q < 2:
                    sums[:, lane] = value[hid:]


def arrange_kernel(own, other, held):
    hid, tile = held.shape[2:]
    blocks = held.shape[1] - 1
    for side, source in enumerate((own, other)):
        held[side, blocks] = jnp.zeros((hid, tile), jnp.bfloat16)
        for block in range(blocks):
            held[side, block] = source[:, block * tile : (block + 1) * tile]


def spread_kernel(plan, table, table_pair, adj, pair, held, *refs):
    rows, offsets, kinds = plan
    results, total = refs[:-1], refs[-1]
    blocks, per_block, tile, unused = adj.shape
    half = total.shape[0] // 2
    row = lax.axis_index("rows")
    firsts = [blocks * per_block + ring_row(row, offset, rows) * CAP for offset in offsets]
    for d in range(len(offsets)):
        total[...] = jnp.zeros_like(total)
        for side, (slots, tiles) in enumerate(((table, adj), (table_pair, pair))):
            for s0 in range(0, CAP, 4):
                terms = []
                for s in range(s0, s0 + 4):
                    entry = slots[firsts[d] + s]
                    index = jnp.maximum(entry, 0) // 256
                    block = index // per_block
                    place = jnp.where(entry < 0, blocks, block)
                    lane = lax.rem(jnp.maximum(entry, 0), 256) * tile
                    term = product(held[side, place], tiles[block, index - block * per_block])
                    terms.append((pl.multiple_of(lane, tile), term))
                for lane, term in terms:
                    total[:, pl.ds(lane, tile)] += term
        for part in range(2):
            value = total[part * half : (part + 1) * half]
            results[2 * d + part][...] = value.astype(kinds[2 * d + part])


def join_kernel(arrived, mine, out):
    out[...] = (arrived[...].astype(jnp.float32) + mine[...]).astype(jnp.bfloat16)


def finish_kernel(own, base_low, base_high, a_low, b_low, a_high, b_high, out):
    half = a_low.shape[0]
    for part, (base, a, b) in enumerate(((base_low, a_low, b_low), (base_high, a_high, b_high))):
        lines = slice(part * half, (part + 1) * half)
        value = own[lines] + base[...] + a[...].astype(jnp.float32)
        out[lines] = (value + b[...].astype(jnp.float32)).astype(jnp.bfloat16)


def call(kernel, name, outs, ins, out_specs, scratch, mib, flops, moved, *args):
    return pl.pallas_call(
        kernel,
        out_shape=[jax.ShapeDtypeStruct(shape, kind) for shape, kind in outs],
        in_specs=ins,
        out_specs=out_specs,
        scratch_shapes=scratch,
        compiler_params=params(mib),
        cost_estimate=cost(flops, moved),
        name=name,
    )(*args)


def shards(rows, feats, features, adjacency, tile_cols, self_weight, neigh_weight, bias_vector, grad_output):
    hid, width = features.shape
    blocks, per_block, tile, unused = adjacency.shape
    half = hid // 2
    every = hid * feats
    top = rows // 4
    narrow, wide = jnp.bfloat16, jnp.float32
    bind = functools.partial

    core = lax.rem(lax.axis_index("rows"), 2)
    mine = lax.dynamic_slice_in_dim(features, core * half, half)
    away = lax.dynamic_slice_in_dim(features, (1 - core) * half, half)
    sources, wanted = [mine], [(0, 0)]
    up, down = [mine, away], [mine, away]
    (table,) = call(
        table_kernel, "table", [((tile_cols.size + rows * CAP,), jnp.int32)], [SMEM], [SMEM],
        [pltpu.SMEM((rows,), jnp.int32)], 2, 0, 8 * rows * CAP, tile_cols,
    )
    packed = 2 * width + 2 * every + 128
    (pack,) = call(
        pack_kernel, "pack", [((hid, packed), narrow)], [HBM] * 4 + [VMEM], [VMEM],
        [pltpu.VMEM((hid, 128), narrow), pltpu.SemaphoreType.DMA((5,))], 4, 0,
        4 * hid * packed,
        features, grad_output, self_weight, neigh_weight, bias_vector.reshape(1, hid),
    )

    def load(value):
        (out,) = call(
            load_kernel, "load", [(adjacency.shape, narrow)], [HBM], [VMEM],
            [pltpu.SemaphoreType.DMA], 2, 0, 4 * adjacency.size, value,
        )
        return out

    pair, tiles = swap(adjacency, rows), load(adjacency)
    for step in range(1, top + 1):
        if step == 2:
            up, down, pair, pack, tiles, table = lax.optimization_barrier(
                (up, down, pair, pack, tiles, table)
            )
            packs = [pack] + [send(pack, k, 0, rows, feats) for k in range(1, feats)]
        if step == 3:
            pair = load(pair)
            up = [after(value, pair) for value in up]
            down = [after(value, pair) for value in down]
        if step == top:
            table_pair = swap(after(table, up[0], down[0]), rows)
            sources.append(swap(after(away, up[0], down[0]), rows))
            wanted.append((0, 1))
        for side in range(2):
            flip = side if step == 1 else 0
            forward, backward = ring_pairs(rows, 1, flip), ring_pairs(rows, -1, flip)
            if step < top or side == 0:
                up[side] = lax.ppermute(up[side], "rows", forward)
                sources.append(up[side])
                wanted.append((-step, side))
            if step < top or side == 1:
                down[side] = lax.ppermute(down[side], "rows", backward)
                sources.append(down[side])
                wanted.append((step, side))

    def aggregate(columns, values):
        return call(
            bind(aggregate_kernel, tuple(wanted), rows), "aggregate",
            [((half, width), narrow), ((1, width), wide)],
            [SMEM, VMEM] + [HBM] * len(sources), [VMEM] * 2,
            [pltpu.VMEM((rows, half, width), narrow), pltpu.SemaphoreType.DMA((len(sources),))],
            11, hid * adjacency.size, 2 * adjacency.size + rows * hid * width,
            columns, values, *sources,
        )

    value, unused_inverse = aggregate(table_pair, pair)
    far = [send(value, k, 1, rows, feats) for k in reversed(range(feats))][::-1]
    value, inverse = aggregate(table, tiles)
    near = [value] + [send(value, k, 0, rows, feats) for k in range(1, feats)]

    turned, cot_all, base = call(
        bind(prepare_kernel, feats), "prepare",
        [((every, every), narrow), ((every, width), narrow), ((every, width), wide)],
        [VMEM] * feats, [VMEM] * 3,
        [
            pltpu.VMEM((every, 2 * every), wide),
            pltpu.VMEM((every, 1), wide),
            pltpu.VMEM((every, width), narrow),
        ],
        8, 2 * every * every * width, 4 * every * packed, *packs,
    )
    activation, grad, scaled, agg_own = call(
        bind(middle_kernel, feats), "middle",
        [((hid, width), narrow), ((every, width), narrow)] + [((hid, width), narrow)] * 2,
        [VMEM] * (5 + 2 * feats), [VMEM] * 4,
        [pltpu.VMEM((every, width), narrow), pltpu.VMEM((every, min(width, 256)), wide)], 9,
        3 * every * every * width, 14 * every * width,
        turned, neigh_weight, inverse, base, cot_all, *near, *far,
    )
    scaled_pair = swap(scaled, rows)
    self_own, sums = call(
        weights_kernel, "weights", [((hid, width), wide), ((4, hid + 8, every // 2), wide)],
        [VMEM] * 4, [VMEM] * 2, [], 6, 6 * hid * every * width, 10 * every * width,
        self_weight, features, agg_own, grad,
    )
    (held,) = call(
        arrange_kernel, "arrange", [((2, blocks + 1, hid, tile), narrow)],
        [VMEM] * 2, [VMEM], [], 4, 0, 8 * hid * width, scaled, scaled_pair,
    )

    def spread(offsets, kinds, gate=None):
        n = 2 * CAP * len(offsets)
        return call(
            bind(spread_kernel, (rows, offsets, kinds)), "spread",
            [((half, width), kind) for kind in kinds],
            [SMEM] * 2 + [VMEM] * 3, [VMEM] * len(kinds), [pltpu.VMEM((hid, width), wide)],
            9, 2 * n * hid * tile * tile, 8 * hid * width * len(offsets),
            table, table_pair, tiles, pair, held if gate is None else after(held, gate),
        )

    def joined(arrived, mine):
        if arrived is None:
            return mine
        (out,) = call(
            join_kernel, "join", [((half, width), narrow)], [VMEM] * 2, [VMEM], [], 3,
            0, 4 * hid * width, arrived, mine,
        )
        return out

    near = sums[:2] + swap(after(sums[2:], scaled_pair), rows, 1)
    total = near[0] + swap(near[1], rows, 2)
    bit, sends = 4, 0

    def ring(value, pairs):
        nonlocal total, bit, sends
        sends += 1
        if sends % 7 == 5 and bit < rows:
            total = total + after(swap(total, rows, bit), value)
            bit *= 2
        if sends == 9:
            value = after(value, total)
        return lax.ppermute(value, "rows", pairs)

    up, down = [None, None], [None, None]
    forward, backward = ring_pairs(rows, 1), ring_pairs(rows, -1)
    low, high = spread((top,), (narrow, narrow))
    up[0], down[1] = ring(low, forward), ring(high, backward)
    mine = spread((top - 1, 1 - top), (wide, narrow, narrow, wide))
    for level in range(top - 1, 0, -1):
        offsets = (level - 1, 1 - level) if level > 1 else (0,)
        later = spread(offsets, (wide, wide) * len(offsets))
        for i in (1, 0):
            flow = 1 - i
            value = joined(up[i], mine[i])
            if i == (1 if level > 1 else 0):
                value = after(value, later[0])
            up[i] = ring(value, forward)
            down[flow] = ring(joined(down[flow], mine[2 + flow]), backward)
        mine = later
    while bit < rows:
        total = total + swap(total, rows, bit)
        bit *= 2
    near = jnp.stack([total, swap(total, rows, 2)])
    far = swap(near, rows, 1)
    grad_self, grad_neigh, total = call(
        collect_kernel, "collect",
        [((hid, every), wide), ((hid, every), wide), ((8, every), wide)],
        [VMEM] * 2, [VMEM] * 3, [], 4, 0, 16 * hid * every, near, far,
    )
    grad_bias = lax.dynamic_slice_in_dim(total[0], lax.axis_index("feat") * hid, hid)
    (grad_features,) = call(
        finish_kernel, "finish", [((hid, width), narrow)], [VMEM] * 7, [VMEM], [], 6, 0,
        8 * hid * width, self_own, *mine, up[0], down[0], up[1], down[1],
    )
    return (activation, grad_features, grad_self, grad_neigh, grad_bias)


def solution(mesh):
    in_specs = (
        P("feat", "rows"),
        P("rows", None, None, None),
        P("rows", None),
        P("feat", None),
        P("feat", None),
        P("feat"),
        P("feat", "rows"),
    )
    out_specs = (P("feat", "rows"), P("feat", "rows"), P("feat", None), P("feat", None), P("feat"))
    body = functools.partial(shards, mesh.shape["rows"], mesh.shape["feat"])
    return jax.shard_map(body, mesh=mesh, in_specs=in_specs, out_specs=out_specs, check_vma=False)
```

```python
import functools

import jax
import jax.numpy as jnp
from jax import lax
from jax.experimental import pallas as pl
from jax.experimental.pallas import tpu as pltpu
from jax.sharding import PartitionSpec as P

CAP = 12
MIB = 1024 * 1024
HBM = pl.BlockSpec(memory_space=pltpu.HBM)
VMEM = pl.BlockSpec(memory_space=pltpu.VMEM)
SMEM = pl.BlockSpec(memory_space=pltpu.SMEM)
LAST = (((1,), (1,)), ((), ()))


def params(mib):
    return pltpu.CompilerParams(vmem_limit_bytes=mib * MIB)


def cost(flops, moved):
    return pl.CostEstimate(flops=flops, bytes_accessed=moved, transcendentals=0)


def product(left, right, dims=(((1,), (0,)), ((), ()))):
    return lax.dot_general(left, right, dims, preferred_element_type=jnp.float32)


def ring_pairs(rows, step, flip=0):
    levels, chips = rows // 4, rows // 2
    order = [2 * z for z in range(levels)] + [2 * z + 1 for z in reversed(range(levels))]
    return [
        (2 * order[p] + core, 2 * order[(p + step) % chips] + (core ^ flip))
        for p in range(chips)
        for core in range(2)
    ]


def ring_row(row, offset, rows):
    levels, chips = rows // 4, rows // 2
    z, x, core = row // 4, lax.rem(row // 2, 2), lax.rem(row, 2)
    target = lax.rem(jnp.where(x == 0, z, chips - 1 - z) + (offset + chips), chips)
    low = target < levels
    return 2 * jnp.where(low, 2 * target, 2 * (chips - 1 - target) + 1) + core


def swap(value, rows, bit=1):
    return lax.ppermute(value, "rows", [(r, r ^ bit) for r in range(rows)])


def send(value, k, flip, rows, feats):
    pairs = [
        (r * feats + i, (r ^ flip) * feats + (i + k) % feats)
        for r in range(rows)
        for i in range(feats)
    ]
    return lax.ppermute(value, ("rows", "feat"), pairs)


def after(value, *others):
    return lax.optimization_barrier((value, *others))[0]


def behind(k, feats, size):
    return pl.multiple_of(lax.rem(lax.axis_index("feat") - k + feats, feats) * size, size)


def pack_kernel(feature, grad_output, ws, wn, bias, out, parts, sems):
    hid, every = ws.shape
    width = feature.shape[1]
    copies = []
    for source, low, size in (
        (feature, 0, width),
        (grad_output, width, width),
        (ws, 2 * width, every),
        (wn, 2 * width + every, every),
        (parts, 2 * width + 2 * every, 128),
    ):
        place = out.at[:, pl.ds(low, size)]
        copies.append(pltpu.make_async_copy(source, place, sems.at[len(copies)]))
    line = lax.broadcasted_iota(jnp.int32, (hid, hid), 0)
    lane = lax.broadcasted_iota(jnp.int32, (hid, hid), 1)
    column = jnp.sum(jnp.where(line == lane, bias[...], 0.0), axis=1, keepdims=True)
    high = column.astype(jnp.bfloat16).astype(jnp.float32)
    middle = (column - high).astype(jnp.bfloat16).astype(jnp.float32)
    low = column - high - middle
    at = lax.broadcasted_iota(jnp.int32, (hid, 128), 1)
    value = jnp.where(at == 0, high, jnp.where(at == 1, middle, jnp.where(at == 2, low, 0.0)))
    parts[...] = value.astype(jnp.bfloat16)
    for copy in copies:
        copy.start()
    for copy in copies:
        copy.wait()


def prepare_kernel(feats, *refs):
    packs, (turned, cot_all, base), (weights, bias, x_all) = refs[:feats], refs[feats:-3], refs[-3:]
    hid, width = packs[0].shape[0], x_all.shape[1]
    every = feats * hid
    for k in range(feats):
        at = pl.ds(behind(k, feats, hid), hid)
        pack = packs[k]
        x_all[at] = pack[:, :width]
        cot_all[at] = pack[:, width : 2 * width]
        weights[at] = pack[:, 2 * width : 2 * width + 2 * every].astype(jnp.float32)
        parts = pack[:, 2 * width + 2 * every :].astype(jnp.float32)
        bias[at] = jnp.sum(parts, axis=1, keepdims=True)
    own = weights[:, :every].T.astype(jnp.bfloat16)
    turned[...] = weights[:, every:].T.astype(jnp.bfloat16)
    chunk = min(width, 512)
    for c in range(0, width, chunk):
        lane = pl.ds(c, chunk)
        base[:, lane] = product(own, x_all[:, lane]) + bias[...]


def table_kernel(cols, table, counts):
    blocks, per_block = cols.shape
    base = blocks * per_block
    groups = counts.shape[0]

    def clear(i, carry):
        counts[i] = 0
        for s in range(CAP):
            table[base + i * CAP + s] = -1
        return carry

    lax.fori_loop(0, groups, clear, 0)

    def step(block, carry):
        for t in range(per_block):
            col = cols[block, t]
            group = col // blocks
            seen = counts[group]
            counts[group] = seen + 1
            index = block * per_block + t
            table[index] = col
            table[base + group * CAP + seen] = index * 256 + (col - group * blocks)
        return carry

    lax.fori_loop(0, blocks, step, 0)


def load_kernel(source, out, sem):
    copy = pltpu.make_async_copy(source, out, sem)
    copy.start()
    copy.wait()


def aggregate_kernel(wanted, rows, table, tiles, *refs):
    count = len(wanted)
    blocks, per_block, tile, unused = tiles.shape
    half = refs[0].shape[0]
    sources, (out, inverse, held, sems) = refs[:count], refs[count:]
    row = lax.axis_index("rows")
    copies = []
    for n, (offset, side) in enumerate(wanted):
        place = ring_row(row, offset, rows)
        if side:
            place = place + 1 - 2 * lax.rem(place, 2)
        copies.append(pltpu.make_async_copy(sources[n], held.at[place], sems.at[n]))
    for copy in copies:
        copy.start()
    for copy in copies:
        copy.wait()
    ones = jnp.ones((16, 2 * tile), jnp.bfloat16)

    def step(block, carry):
        total = None
        for t in range(0, per_block, 2):
            left, right = [], []
            for u in (t, t + 1):
                col = table[block * per_block + u]
                source = col // blocks
                at = pl.multiple_of((col - source * blocks) * tile, tile)
                left.append(held[source, :, pl.ds(at, tile)])
                right.append(tiles[block, u])
            term = product(
                jnp.concatenate([jnp.concatenate(left, axis=1), ones], axis=0),
                jnp.concatenate(right, axis=1),
                LAST,
            )
            total = term if total is None else total + term
        factor = 1.0 / total[half : half + 1]
        lane = pl.ds(pl.multiple_of(block * tile, tile), tile)
        out[:, lane] = (total[:half] * factor).astype(jnp.bfloat16)
        inverse[:, lane] = factor
        return carry

    lax.fori_loop(0, blocks, step, 0, unroll=4)


def middle_kernel(feats, turned, wn, inverse, base, cot, *refs):
    near, far, refs = refs[:feats], refs[feats : 2 * feats], refs[2 * feats :]
    act, grad, scaled, agg_own, agg, value = refs
    hid, width = act.shape
    half = hid // 2
    core = lax.rem(lax.axis_index("rows"), 2)
    for k in range(feats):
        first = behind(k, feats, hid)
        agg[pl.ds(pl.multiple_of(first + core * half, half), half)] = near[k][...]
        agg[pl.ds(pl.multiple_of(first + (1 - core) * half, half), half)] = far[k][...]
    own = pl.ds(behind(0, feats, hid), hid)
    agg_own[...] = agg[own]
    chunk = min(width, 256)
    for c in range(0, width, chunk):
        lane = pl.ds(c, chunk)
        pre = product(turned[...], agg[:, lane]) + base[:, lane]
        slope = jnp.exp(jnp.minimum(pre, 0.0))
        grad[:, lane] = (cot[:, lane].astype(jnp.float32) * slope).astype(jnp.bfloat16)
        value[...] = jnp.where(pre > 0, pre, slope - 1.0)
        back = product(wn[...], grad[:, lane])
        scaled[:, lane] = (back * inverse[:, lane]).astype(jnp.bfloat16)
        act[:, lane] = value[own].astype(jnp.bfloat16)


def own_quarter():
    return 2 * lax.rem(lax.axis_index("rows"), 2)


def turned_quarter(mine, index):
    turned = index // 2 + mine // 2 - 2 * (index // 2) * (mine // 2)
    return 2 * turned + index % 2


def weights_kernel(ws, x_own, agg_own, grad, self_own, sums):
    hid, every = ws.shape
    g = grad[...]
    self_own[...] = product(ws[...], g)
    wide = every // 2
    mine = own_quarter()
    values = [product(x_own[...], g, LAST), product(agg_own[...], g, LAST)]
    total = product(jnp.ones((8, g.shape[1]), jnp.bfloat16), g, LAST)
    for quarter in range(4):
        slot = turned_quarter(mine, quarter)
        lane = slice(quarter % 2 * wide, (quarter % 2 + 1) * wide)
        sums[slot, :hid] = values[quarter // 2][:, lane]
        sums[slot, hid:] = total[:, lane]


def collect_kernel(pair, pair_far, grad_self, grad_neigh, sums):
    hid, every = grad_self.shape
    wide = every // 2
    mine = own_quarter()
    for slot in range(4):
        value = (pair, pair_far)[slot // 2][slot % 2]
        quarter = turned_quarter(mine, slot)
        for q, out in enumerate((grad_self, grad_self, grad_neigh, grad_neigh)):

            @pl.when(quarter == q)
            def _():
                lane = slice(q % 2 * wide, (q % 2 + 1) * wide)
                out[:, lane] = value[:hid]
                if q < 2:
                    sums[:, lane] = value[hid:]


def arrange_kernel(own, other, held):
    hid, tile = held.shape[2:]
    blocks = held.shape[1] - 1
    for side, source in enumerate((own, other)):
        held[side, blocks] = jnp.zeros((hid, tile), jnp.bfloat16)
        for block in range(blocks):
            held[side, block] = source[:, block * tile : (block + 1) * tile]


def spread_kernel(plan, table, table_pair, adj, pair, held, *refs):
    rows, offsets, kinds = plan
    results, total = refs[:-1], refs[-1]
    blocks, per_block, tile, unused = adj.shape
    half = total.shape[0] // 2
    row = lax.axis_index("rows")
    firsts = [blocks * per_block + ring_row(row, offset, rows) * CAP for offset in offsets]
    for d in range(len(offsets)):
        total[...] = jnp.zeros_like(total)
        for side, (slots, tiles) in enumerate(((table, adj), (table_pair, pair))):
            for s0 in range(0, CAP, 4):
                terms = []
                for s in range(s0, s0 + 4):
                    entry = slots[firsts[d] + s]
                    index = jnp.maximum(entry, 0) // 256
                    block = index // per_block
                    place = jnp.where(entry < 0, blocks, block)
                    lane = lax.rem(jnp.maximum(entry, 0), 256) * tile
                    term = product(held[side, place], tiles[block, index - block * per_block])
                    terms.append((pl.multiple_of(lane, tile), term))
                for lane, term in terms:
                    total[:, pl.ds(lane, tile)] += term
        for part in range(2):
            value = total[part * half : (part + 1) * half]
            results[2 * d + part][...] = value.astype(kinds[2 * d + part])


def join_kernel(arrived, mine, out):
    out[...] = (arrived[...].astype(jnp.float32) + mine[...]).astype(jnp.bfloat16)


def finish_kernel(own, base_low, base_high, a_low, b_low, a_high, b_high, out):
    half = a_low.shape[0]
    for part, (base, a, b) in enumerate(((base_low, a_low, b_low), (base_high, a_high, b_high))):
        lines = slice(part * half, (part + 1) * half)
        value = own[lines] + base[...] + a[...].astype(jnp.float32)
        out[lines] = (value + b[...].astype(jnp.float32)).astype(jnp.bfloat16)


def call(kernel, name, outs, ins, out_specs, scratch, mib, flops, moved, *args):
    return pl.pallas_call(
        kernel,
        out_shape=[jax.ShapeDtypeStruct(shape, kind) for shape, kind in outs],
        in_specs=ins,
        out_specs=out_specs,
        scratch_shapes=scratch,
        compiler_params=params(mib),
        cost_estimate=cost(flops, moved),
        name=name,
    )(*args)


def shards(rows, feats, features, adjacency, tile_cols, self_weight, neigh_weight, bias_vector, grad_output):
    hid, width = features.shape
    blocks, per_block, tile, unused = adjacency.shape
    half = hid // 2
    every = hid * feats
    top = rows // 4
    narrow, wide = jnp.bfloat16, jnp.float32
    bind = functools.partial

    core = lax.rem(lax.axis_index("rows"), 2)
    mine = lax.dynamic_slice_in_dim(features, core * half, half)
    away = lax.dynamic_slice_in_dim(features, (1 - core) * half, half)
    sources, wanted = [mine], [(0, 0)]
    up, down = [mine, away], [mine, away]
    (table,) = call(
        table_kernel, "table", [((tile_cols.size + rows * CAP,), jnp.int32)], [SMEM], [SMEM],
        [pltpu.SMEM((rows,), jnp.int32)], 2, 0, 8 * rows * CAP, tile_cols,
    )
    packed = 2 * width + 2 * every + 128
    (pack,) = call(
        pack_kernel, "pack", [((hid, packed), narrow)], [HBM] * 4 + [VMEM], [VMEM],
        [pltpu.VMEM((hid, 128), narrow), pltpu.SemaphoreType.DMA((5,))], 4, 0,
        4 * hid * packed,
        features, grad_output, self_weight, neigh_weight, bias_vector.reshape(1, hid),
    )

    def load(value):
        (out,) = call(
            load_kernel, "load", [(adjacency.shape, narrow)], [HBM], [VMEM],
            [pltpu.SemaphoreType.DMA], 2, 0, 4 * adjacency.size, value,
        )
        return out

    pair, tiles = swap(adjacency, rows), load(adjacency)
    for step in range(1, top + 1):
        if step == 2:
            up[1], down[1], pair, pack, tiles, table = lax.optimization_barrier(
                (up[1], down[1], pair, pack, tiles, table)
            )
            packs = [pack] + [send(pack, k, 0, rows, feats) for k in range(1, feats)]
        if step == 3:
            pair = load(pair)
            up = [after(value, pair) for value in up]
            down = [after(value, pair) for value in down]
        if step == top:
            table_pair = swap(after(table, up[0], down[0]), rows)
            sources.append(swap(after(away, up[0], down[0]), rows))
            wanted.append((0, 1))
        for side in range(2):
            flip = side if step == 1 else 0
            forward, backward = ring_pairs(rows, 1, flip), ring_pairs(rows, -1, flip)
            if step < top or side == 0:
                up[side] = lax.ppermute(up[side], "rows", forward)
                sources.append(up[side])
                wanted.append((-step, side))
            if step < top or side == 1:
                down[side] = lax.ppermute(down[side], "rows", backward)
                sources.append(down[side])
                wanted.append((step, side))

    def aggregate(columns, values):
        return call(
            bind(aggregate_kernel, tuple(wanted), rows), "aggregate",
            [((half, width), narrow), ((1, width), wide)],
            [SMEM, VMEM] + [HBM] * len(sources), [VMEM] * 2,
            [pltpu.VMEM((rows, half, width), narrow), pltpu.SemaphoreType.DMA((len(sources),))],
            11, hid * adjacency.size, 2 * adjacency.size + rows * hid * width,
            columns, values, *sources,
        )

    value, unused_inverse = aggregate(table_pair, pair)
    far = [send(value, k, 1, rows, feats) for k in reversed(range(feats))][::-1]
    value, inverse = aggregate(table, tiles)
    near = [value] + [send(value, k, 0, rows, feats) for k in range(1, feats)]

    turned, cot_all, base = call(
        bind(prepare_kernel, feats), "prepare",
        [((every, every), narrow), ((every, width), narrow), ((every, width), wide)],
        [VMEM] * feats, [VMEM] * 3,
        [
            pltpu.VMEM((every, 2 * every), wide),
            pltpu.VMEM((every, 1), wide),
            pltpu.VMEM((every, width), narrow),
        ],
        8, 2 * every * every * width, 4 * every * packed, *packs,
    )
    activation, grad, scaled, agg_own = call(
        bind(middle_kernel, feats), "middle",
        [((hid, width), narrow), ((every, width), narrow)] + [((hid, width), narrow)] * 2,
        [VMEM] * (5 + 2 * feats), [VMEM] * 4,
        [pltpu.VMEM((every, width), narrow), pltpu.VMEM((every, min(width, 256)), wide)], 9,
        3 * every * every * width, 14 * every * width,
        turned, neigh_weight, inverse, base, cot_all, *near, *far,
    )
    scaled_pair = swap(scaled, rows)
    self_own, sums = call(
        weights_kernel, "weights", [((hid, width), wide), ((4, hid + 8, every // 2), wide)],
        [VMEM] * 4, [VMEM] * 2, [], 6, 6 * hid * every * width, 10 * every * width,
        self_weight, features, agg_own, grad,
    )
    (held,) = call(
        arrange_kernel, "arrange", [((2, blocks + 1, hid, tile), narrow)],
        [VMEM] * 2, [VMEM], [], 4, 0, 8 * hid * width, scaled, scaled_pair,
    )

    def spread(offsets, kinds):
        n = 2 * CAP * len(offsets)
        return call(
            bind(spread_kernel, (rows, offsets, kinds)), "spread",
            [((half, width), kind) for kind in kinds],
            [SMEM] * 2 + [VMEM] * 3, [VMEM] * len(kinds), [pltpu.VMEM((hid, width), wide)],
            9, 2 * n * hid * tile * tile, 8 * hid * width * len(offsets),
            table, table_pair, tiles, pair, held,
        )

    def joined(arrived, mine):
        if arrived is None:
            return mine
        (out,) = call(
            join_kernel, "join", [((half, width), narrow)], [VMEM] * 2, [VMEM], [], 3,
            0, 4 * hid * width, arrived, mine,
        )
        return out

    total = sums[:2] + swap(after(sums[2:], scaled_pair), rows, 1)
    total = total + swap(total, rows, 2)
    bit, sends = 4, 0

    def ring(value, pairs):
        nonlocal total, bit, sends
        sends += 1
        if sends >= 6 and sends % 4 == 2 and bit < 2 * rows:
            value = after(value, total)
            total = after(total, value)
            if bit < rows:
                total = total + swap(total, rows, bit)
            bit *= 2
        return lax.ppermute(value, "rows", pairs)

    up, down = [None, None], [None, None]
    forward, backward = ring_pairs(rows, 1), ring_pairs(rows, -1)
    for level in range(top, 0, -1):
        if level == top:
            low, high = spread((top,), (narrow, narrow))
            up[0] = ring(low, forward)
            down[1] = ring(high, backward)
            continue
        kinds = tuple(narrow if arrived is None else wide for arrived in up + down)
        offsets = (level, -level)
        if level == 1:
            offsets, kinds = (1, -1, 0), kinds + (wide, wide)
        mine = spread(offsets, kinds)
        for i in (1, 0):
            flow = 1 - i
            up[i] = ring(joined(up[i], mine[i]), forward)
            down[flow] = ring(joined(down[flow], mine[2 + flow]), backward)
    far = swap(total, rows, 1)
    grad_self, grad_neigh, total = call(
        collect_kernel, "collect",
        [((hid, every), wide), ((hid, every), wide), ((8, every), wide)],
        [VMEM] * 2, [VMEM] * 3, [], 4, 0, 16 * hid * every, total, far,
    )
    grad_bias = lax.dynamic_slice_in_dim(total[0], lax.axis_index("feat") * hid, hid)
    (grad_features,) = call(
        finish_kernel, "finish", [((hid, width), narrow)], [VMEM] * 7, [VMEM], [], 6, 0,
        8 * hid * width, self_own, mine[4], mine[5], up[0], down[0], up[1], down[1],
    )
    return (activation, grad_features, grad_self, grad_neigh, grad_bias)


def solution(mesh):
    in_specs = (
        P("feat", "rows"),
        P("rows", None, None, None),
        P("rows", None),
        P("feat", None),
        P("feat", None),
        P("feat"),
        P("feat", "rows"),
    )
    out_specs = (P("feat", "rows"), P("feat", "rows"), P("feat", None), P("feat", None), P("feat"))
    body = functools.partial(shards, mesh.shape["rows"], mesh.shape["feat"])
    return jax.shard_map(body, mesh=mesh, in_specs=in_specs, out_specs=out_specs, check_vma=False)
```

```python
import functools

import jax
import jax.numpy as jnp
from jax import lax
from jax.experimental import pallas as pl
from jax.experimental.pallas import tpu as pltpu
from jax.sharding import PartitionSpec as P

CAP = 12
MIB = 1024 * 1024
HBM = pl.BlockSpec(memory_space=pltpu.HBM)
VMEM = pl.BlockSpec(memory_space=pltpu.VMEM)
SMEM = pl.BlockSpec(memory_space=pltpu.SMEM)
LAST = (((1,), (1,)), ((), ()))


def params(mib):
    return pltpu.CompilerParams(vmem_limit_bytes=mib * MIB)


def cost(flops, moved):
    return pl.CostEstimate(flops=flops, bytes_accessed=moved, transcendentals=0)


def product(left, right, dims=(((1,), (0,)), ((), ()))):
    return lax.dot_general(left, right, dims, preferred_element_type=jnp.float32)


def ring_pairs(rows, step, flip=0):
    levels, chips = rows // 4, rows // 2
    order = [2 * z for z in range(levels)] + [2 * z + 1 for z in reversed(range(levels))]
    return [
        (2 * order[p] + core, 2 * order[(p + step) % chips] + (core ^ flip))
        for p in range(chips)
        for core in range(2)
    ]


def ring_row(row, offset, rows):
    levels, chips = rows // 4, rows // 2
    z, x, core = row // 4, lax.rem(row // 2, 2), lax.rem(row, 2)
    target = lax.rem(jnp.where(x == 0, z, chips - 1 - z) + (offset + chips), chips)
    low = target < levels
    return 2 * jnp.where(low, 2 * target, 2 * (chips - 1 - target) + 1) + core


def swap(value, rows, bit=1):
    return lax.ppermute(value, "rows", [(r, r ^ bit) for r in range(rows)])


def send(value, k, flip, rows, feats):
    pairs = [
        (r * feats + i, (r ^ flip) * feats + (i + k) % feats)
        for r in range(rows)
        for i in range(feats)
    ]
    return lax.ppermute(value, ("rows", "feat"), pairs)


def after(value, *others):
    return lax.optimization_barrier((value, *others))[0]


def behind(k, feats, size):
    return pl.multiple_of(lax.rem(lax.axis_index("feat") - k + feats, feats) * size, size)


def pack_kernel(feature, grad_output, ws, wn, bias, out, parts, sems):
    hid, every = ws.shape
    width = feature.shape[1]
    copies = []
    for source, low, size in (
        (feature, 0, width),
        (grad_output, width, width),
        (ws, 2 * width, every),
        (wn, 2 * width + every, every),
        (parts, 2 * width + 2 * every, 128),
    ):
        place = out.at[:, pl.ds(low, size)]
        copies.append(pltpu.make_async_copy(source, place, sems.at[len(copies)]))
    line = lax.broadcasted_iota(jnp.int32, (hid, hid), 0)
    lane = lax.broadcasted_iota(jnp.int32, (hid, hid), 1)
    column = jnp.sum(jnp.where(line == lane, bias[...], 0.0), axis=1, keepdims=True)
    high = column.astype(jnp.bfloat16).astype(jnp.float32)
    middle = (column - high).astype(jnp.bfloat16).astype(jnp.float32)
    low = column - high - middle
    at = lax.broadcasted_iota(jnp.int32, (hid, 128), 1)
    value = jnp.where(at == 0, high, jnp.where(at == 1, middle, jnp.where(at == 2, low, 0.0)))
    parts[...] = value.astype(jnp.bfloat16)
    for copy in copies:
        copy.start()
    for copy in copies:
        copy.wait()


def prepare_kernel(feats, *refs):
    packs, (turned, cot_all, base), (weights, bias, x_all) = refs[:feats], refs[feats:-3], refs[-3:]
    hid, width = packs[0].shape[0], x_all.shape[1]
    every = feats * hid
    for k in range(feats):
        at = pl.ds(behind(k, feats, hid), hid)
        pack = packs[k]
        x_all[at] = pack[:, :width]
        cot_all[at] = pack[:, width : 2 * width]
        weights[at] = pack[:, 2 * width : 2 * width + 2 * every].astype(jnp.float32)
        parts = pack[:, 2 * width + 2 * every :].astype(jnp.float32)
        bias[at] = jnp.sum(parts, axis=1, keepdims=True)
    own = weights[:, :every].T.astype(jnp.bfloat16)
    turned[...] = weights[:, every:].T.astype(jnp.bfloat16)
    chunk = min(width, 512)
    for c in range(0, width, chunk):
        lane = pl.ds(c, chunk)
        base[:, lane] = product(own, x_all[:, lane]) + bias[...]


def table_kernel(cols, table, counts):
    blocks, per_block = cols.shape
    base = blocks * per_block
    groups = counts.shape[0]

    def clear(i, carry):
        counts[i] = 0
        for s in range(CAP):
            table[base + i * CAP + s] = -1
        return carry

    lax.fori_loop(0, groups, clear, 0)

    def step(block, carry):
        for t in range(per_block):
            col = cols[block, t]
            group = col // blocks
            seen = counts[group]
            counts[group] = seen + 1
            index = block * per_block + t
            table[index] = col
            table[base + group * CAP + seen] = index * 256 + (col - group * blocks)
        return carry

    lax.fori_loop(0, blocks, step, 0)


def load_kernel(source, out, sem):
    copy = pltpu.make_async_copy(source, out, sem)
    copy.start()
    copy.wait()


def aggregate_kernel(wanted, rows, table, tiles, *refs):
    count = len(wanted)
    blocks, per_block, tile, unused = tiles.shape
    half = refs[0].shape[0]
    sources, (out, inverse, held, sems) = refs[:count], refs[count:]
    row = lax.axis_index("rows")
    copies = []
    for n, (offset, side) in enumerate(wanted):
        place = ring_row(row, offset, rows)
        if side:
            place = place + 1 - 2 * lax.rem(place, 2)
        copies.append(pltpu.make_async_copy(sources[n], held.at[place], sems.at[n]))
    for copy in copies:
        copy.start()
    for copy in copies:
        copy.wait()
    ones = jnp.ones((16, 2 * tile), jnp.bfloat16)

    def step(block, carry):
        total = None
        for t in range(0, per_block, 2):
            left, right = [], []
            for u in (t, t + 1):
                col = table[block * per_block + u]
                source = col // blocks
                at = pl.multiple_of((col - source * blocks) * tile, tile)
                left.append(held[source, :, pl.ds(at, tile)])
                right.append(tiles[block, u])
            term = product(
                jnp.concatenate([jnp.concatenate(left, axis=1), ones], axis=0),
                jnp.concatenate(right, axis=1),
                LAST,
            )
            total = term if total is None else total + term
        factor = 1.0 / total[half : half + 1]
        lane = pl.ds(pl.multiple_of(block * tile, tile), tile)
        out[:, lane] = (total[:half] * factor).astype(jnp.bfloat16)
        inverse[:, lane] = factor
        return carry

    lax.fori_loop(0, blocks, step, 0, unroll=4)


def middle_kernel(feats, turned, wn, inverse, base, cot, *refs):
    near, far, refs = refs[:feats], refs[feats : 2 * feats], refs[2 * feats :]
    act, grad, scaled, agg_own, agg, value = refs
    hid, width = act.shape
    half = hid // 2
    core = lax.rem(lax.axis_index("rows"), 2)
    for k in range(feats):
        first = behind(k, feats, hid)
        agg[pl.ds(pl.multiple_of(first + core * half, half), half)] = near[k][...]
        agg[pl.ds(pl.multiple_of(first + (1 - core) * half, half), half)] = far[k][...]
    own = pl.ds(behind(0, feats, hid), hid)
    agg_own[...] = agg[own]
    chunk = min(width, 256)
    for c in range(0, width, chunk):
        lane = pl.ds(c, chunk)
        pre = product(turned[...], agg[:, lane]) + base[:, lane]
        slope = jnp.exp(jnp.minimum(pre, 0.0))
        grad[:, lane] = (cot[:, lane].astype(jnp.float32) * slope).astype(jnp.bfloat16)
        value[...] = jnp.where(pre > 0, pre, slope - 1.0)
        back = product(wn[...], grad[:, lane])
        scaled[:, lane] = (back * inverse[:, lane]).astype(jnp.bfloat16)
        act[:, lane] = value[own].astype(jnp.bfloat16)


def own_quarter():
    return 2 * lax.rem(lax.axis_index("rows"), 2)


def turned_quarter(mine, index):
    turned = index // 2 + mine // 2 - 2 * (index // 2) * (mine // 2)
    return 2 * turned + index % 2


def weights_kernel(ws, x_own, agg_own, grad, self_own, sums):
    hid, every = ws.shape
    g = grad[...]
    self_own[...] = product(ws[...], g)
    wide = every // 2
    mine = own_quarter()
    values = [product(x_own[...], g, LAST), product(agg_own[...], g, LAST)]
    total = product(jnp.ones((8, g.shape[1]), jnp.bfloat16), g, LAST)
    for quarter in range(4):
        slot = turned_quarter(mine, quarter)
        lane = slice(quarter % 2 * wide, (quarter % 2 + 1) * wide)
        sums[slot, :hid] = values[quarter // 2][:, lane]
        sums[slot, hid:] = total[:, lane]


def collect_kernel(pair, pair_far, grad_self, grad_neigh, sums):
    hid, every = grad_self.shape
    wide = every // 2
    mine = own_quarter()
    for slot in range(4):
        value = (pair, pair_far)[slot // 2][slot % 2]
        quarter = turned_quarter(mine, slot)
        for q, out in enumerate((grad_self, grad_self, grad_neigh, grad_neigh)):

            @pl.when(quarter == q)
            def _():
                lane = slice(q % 2 * wide, (q % 2 + 1) * wide)
                out[:, lane] = value[:hid]
                if q < 2:
                    sums[:, lane] = value[hid:]


def arrange_kernel(own, other, held):
    hid, tile = held.shape[2:]
    blocks = held.shape[1] - 1
    for side, source in enumerate((own, other)):
        held[side, blocks] = jnp.zeros((hid, tile), jnp.bfloat16)
        for block in range(blocks):
            held[side, block] = source[:, block * tile : (block + 1) * tile]


def spread_kernel(plan, table, table_pair, adj, pair, held, *refs):
    rows, offsets, kinds = plan
    results, total = refs[:-1], refs[-1]
    blocks, per_block, tile, unused = adj.shape
    half = total.shape[0] // 2
    row = lax.axis_index("rows")
    firsts = [blocks * per_block + ring_row(row, offset, rows) * CAP for offset in offsets]
    for d in range(len(offsets)):
        total[...] = jnp.zeros_like(total)
        for side, (slots, tiles) in enumerate(((table, adj), (table_pair, pair))):
            for s0 in range(0, CAP, 4):
                terms = []
                for s in range(s0, s0 + 4):
                    entry = slots[firsts[d] + s]
                    index = jnp.maximum(entry, 0) // 256
                    block = index // per_block
                    place = jnp.where(entry < 0, blocks, block)
                    lane = lax.rem(jnp.maximum(entry, 0), 256) * tile
                    term = product(held[side, place], tiles[block, index - block * per_block])
                    terms.append((pl.multiple_of(lane, tile), term))
                for lane, term in terms:
                    total[:, pl.ds(lane, tile)] += term
        for part in range(2):
            value = total[part * half : (part + 1) * half]
            results[2 * d + part][...] = value.astype(kinds[2 * d + part])


def join_kernel(arrived, mine, out):
    out[...] = (arrived[...].astype(jnp.float32) + mine[...]).astype(jnp.bfloat16)


def finish_kernel(own, base_low, base_high, a_low, b_low, a_high, b_high, out):
    half = a_low.shape[0]
    for part, (base, a, b) in enumerate(((base_low, a_low, b_low), (base_high, a_high, b_high))):
        lines = slice(part * half, (part + 1) * half)
        value = own[lines] + base[...] + a[...].astype(jnp.float32)
        out[lines] = (value + b[...].astype(jnp.float32)).astype(jnp.bfloat16)


def call(kernel, name, outs, ins, out_specs, scratch, mib, flops, moved, *args):
    return pl.pallas_call(
        kernel,
        out_shape=[jax.ShapeDtypeStruct(shape, kind) for shape, kind in outs],
        in_specs=ins,
        out_specs=out_specs,
        scratch_shapes=scratch,
        compiler_params=params(mib),
        cost_estimate=cost(flops, moved),
        name=name,
    )(*args)


def shards(rows, feats, features, adjacency, tile_cols, self_weight, neigh_weight, bias_vector, grad_output):
    hid, width = features.shape
    blocks, per_block, tile, unused = adjacency.shape
    half = hid // 2
    every = hid * feats
    top = rows // 4
    narrow, wide = jnp.bfloat16, jnp.float32
    bind = functools.partial

    core = lax.rem(lax.axis_index("rows"), 2)
    mine = lax.dynamic_slice_in_dim(features, core * half, half)
    away = lax.dynamic_slice_in_dim(features, (1 - core) * half, half)
    sources, wanted = [mine], [(0, 0)]
    up, down = [mine, away], [mine, away]
    (table,) = call(
        table_kernel, "table", [((tile_cols.size + rows * CAP,), jnp.int32)], [SMEM], [SMEM],
        [pltpu.SMEM((rows,), jnp.int32)], 2, 0, 8 * rows * CAP, tile_cols,
    )
    packed = 2 * width + 2 * every + 128
    (pack,) = call(
        pack_kernel, "pack", [((hid, packed), narrow)], [HBM] * 4 + [VMEM], [VMEM],
        [pltpu.VMEM((hid, 128), narrow), pltpu.SemaphoreType.DMA((5,))], 4, 0,
        4 * hid * packed,
        features, grad_output, self_weight, neigh_weight, bias_vector.reshape(1, hid),
    )

    def load(value):
        (out,) = call(
            load_kernel, "load", [(adjacency.shape, narrow)], [HBM], [VMEM],
            [pltpu.SemaphoreType.DMA], 2, 0, 4 * adjacency.size, value,
        )
        return out

    pair, tiles = swap(adjacency, rows), load(adjacency)
    for step in range(1, top + 1):
        if step == 2:
            up, down, pair, pack, tiles, table = lax.optimization_barrier(
                (up, down, pair, pack, tiles, table)
            )
            packs = [pack] + [send(pack, k, 0, rows, feats) for k in range(1, feats)]
        if step == 3:
            pair = load(pair)
            up = [after(value, pair) for value in up]
            down = [after(value, pair) for value in down]
        if step == top:
            table_pair = swap(after(table, up[0], down[0]), rows)
            sources.append(swap(after(away, up[0], down[0]), rows))
            wanted.append((0, 1))
        for side in range(2):
            flip = side if step == 1 else 0
            forward, backward = ring_pairs(rows, 1, flip), ring_pairs(rows, -1, flip)
            if step < top or side == 0:
                up[side] = lax.ppermute(up[side], "rows", forward)
                sources.append(up[side])
                wanted.append((-step, side))
            if step < top or side == 1:
                down[side] = lax.ppermute(down[side], "rows", backward)
                sources.append(down[side])
                wanted.append((step, side))

    def aggregate(columns, values):
        return call(
            bind(aggregate_kernel, tuple(wanted), rows), "aggregate",
            [((half, width), narrow), ((1, width), wide)],
            [SMEM, VMEM] + [HBM] * len(sources), [VMEM] * 2,
            [pltpu.VMEM((rows, half, width), narrow), pltpu.SemaphoreType.DMA((len(sources),))],
            11, hid * adjacency.size, 2 * adjacency.size + rows * hid * width,
            columns, values, *sources,
        )

    value, unused_inverse = aggregate(table_pair, pair)
    far = [send(value, k, 1, rows, feats) for k in reversed(range(feats))][::-1]
    value, inverse = aggregate(table, tiles)
    near = [value] + [send(value, k, 0, rows, feats) for k in range(1, feats)]

    turned, cot_all, base = call(
        bind(prepare_kernel, feats), "prepare",
        [((every, every), narrow), ((every, width), narrow), ((every, width), wide)],
        [VMEM] * feats, [VMEM] * 3,
        [
            pltpu.VMEM((every, 2 * every), wide),
            pltpu.VMEM((every, 1), wide),
            pltpu.VMEM((every, width), narrow),
        ],
        8, 2 * every * every * width, 4 * every * packed, *packs,
    )
    activation, grad, scaled, agg_own = call(
        bind(middle_kernel, feats), "middle",
        [((hid, width), narrow), ((every, width), narrow)] + [((hid, width), narrow)] * 2,
        [VMEM] * (5 + 2 * feats), [VMEM] * 4,
        [pltpu.VMEM((every, width), narrow), pltpu.VMEM((every, min(width, 256)), wide)], 9,
        3 * every * every * width, 14 * every * width,
        turned, neigh_weight, inverse, base, cot_all, *near, *far,
    )
    scaled_pair = swap(scaled, rows)
    self_own, sums = call(
        weights_kernel, "weights", [((hid, width), wide), ((4, hid + 8, every // 2), wide)],
        [VMEM] * 4, [VMEM] * 2, [], 6, 6 * hid * every * width, 10 * every * width,
        self_weight, features, agg_own, grad,
    )
    (held,) = call(
        arrange_kernel, "arrange", [((2, blocks + 1, hid, tile), narrow)],
        [VMEM] * 2, [VMEM], [], 4, 0, 8 * hid * width, scaled, scaled_pair,
    )

    def spread(offsets, kinds):
        n = 2 * CAP * len(offsets)
        return call(
            bind(spread_kernel, (rows, offsets, kinds)), "spread",
            [((half, width), kind) for kind in kinds],
            [SMEM] * 2 + [VMEM] * 3, [VMEM] * len(kinds), [pltpu.VMEM((hid, width), wide)],
            9, 2 * n * hid * tile * tile, 8 * hid * width * len(offsets),
            table, table_pair, tiles, pair, held,
        )

    def joined(arrived, mine):
        if arrived is None:
            return mine
        (out,) = call(
            join_kernel, "join", [((half, width), narrow)], [VMEM] * 2, [VMEM], [], 3,
            0, 4 * hid * width, arrived, mine,
        )
        return out

    total = sums[:2] + swap(after(sums[2:], scaled_pair), rows, 1)
    arriving, bit, sends = swap(total, rows, 2), 4, 0

    def ring(value, pairs):
        nonlocal total, arriving, bit, sends
        sends += 1
        if sends >= 6 and sends % 4 == 2 and arriving is not None:
            if sends == 6:
                total = total + arriving
                value = after(value, total)
            else:
                total = total + after(arriving, value)
            arriving = None
            if bit < rows:
                arriving = swap(total, rows, bit)
            bit *= 2
        return lax.ppermute(value, "rows", pairs)

    up, down = [None, None], [None, None]
    forward, backward = ring_pairs(rows, 1), ring_pairs(rows, -1)
    for level in range(top, 0, -1):
        if level == top:
            low, high = spread((top,), (narrow, narrow))
            up[0] = ring(low, forward)
            down[1] = ring(high, backward)
            continue
        kinds = tuple(narrow if arrived is None else wide for arrived in up + down)
        offsets = (level, -level)
        if level == 1:
            offsets, kinds = (1, -1, 0), kinds + (wide, wide)
        mine = spread(offsets, kinds)
        for i in (1, 0):
            flow = 1 - i
            up[i] = ring(joined(up[i], mine[i]), forward)
            down[flow] = ring(joined(down[flow], mine[2 + flow]), backward)
    far = swap(total, rows, 1)
    grad_self, grad_neigh, total = call(
        collect_kernel, "collect",
        [((hid, every), wide), ((hid, every), wide), ((8, every), wide)],
        [VMEM] * 2, [VMEM] * 3, [], 4, 0, 16 * hid * every, total, far,
    )
    grad_bias = lax.dynamic_slice_in_dim(total[0], lax.axis_index("feat") * hid, hid)
    (grad_features,) = call(
        finish_kernel, "finish", [((hid, width), narrow)], [VMEM] * 7, [VMEM], [], 6, 0,
        8 * hid * width, self_own, mine[4], mine[5], up[0], down[0], up[1], down[1],
    )
    return (activation, grad_features, grad_self, grad_neigh, grad_bias)


def solution(mesh):
    in_specs = (
        P("feat", "rows"),
        P("rows", None, None, None),
        P("rows", None),
        P("feat", None),
        P("feat", None),
        P("feat"),
        P("feat", "rows"),
    )
    out_specs = (P("feat", "rows"), P("feat", "rows"), P("feat", None), P("feat", None), P("feat"))
    body = functools.partial(shards, mesh.shape["rows"], mesh.shape["feat"])
    return jax.shard_map(body, mesh=mesh, in_specs=in_specs, out_specs=out_specs, check_vma=False)
```

```python
import functools

import jax
import jax.numpy as jnp
from jax import lax
from jax.experimental import pallas as pl
from jax.experimental.pallas import tpu as pltpu
from jax.sharding import PartitionSpec as P

CAP = 12
MIB = 1024 * 1024
HBM = pl.BlockSpec(memory_space=pltpu.HBM)
VMEM = pl.BlockSpec(memory_space=pltpu.VMEM)
SMEM = pl.BlockSpec(memory_space=pltpu.SMEM)
LAST = (((1,), (1,)), ((), ()))


def params(mib):
    return pltpu.CompilerParams(vmem_limit_bytes=mib * MIB)


def cost(flops, moved):
    return pl.CostEstimate(flops=flops, bytes_accessed=moved, transcendentals=0)


def product(left, right, dims=(((1,), (0,)), ((), ()))):
    return lax.dot_general(left, right, dims, preferred_element_type=jnp.float32)


def ring_pairs(rows, step, flip=0):
    levels, chips = rows // 4, rows // 2
    order = [2 * z for z in range(levels)] + [2 * z + 1 for z in reversed(range(levels))]
    return [
        (2 * order[p] + core, 2 * order[(p + step) % chips] + (core ^ flip))
        for p in range(chips)
        for core in range(2)
    ]


def ring_row(row, offset, rows):
    levels, chips = rows // 4, rows // 2
    z, x, core = row // 4, lax.rem(row // 2, 2), lax.rem(row, 2)
    target = lax.rem(jnp.where(x == 0, z, chips - 1 - z) + (offset + chips), chips)
    low = target < levels
    return 2 * jnp.where(low, 2 * target, 2 * (chips - 1 - target) + 1) + core


def swap(value, rows, bit=1):
    return lax.ppermute(value, "rows", [(r, r ^ bit) for r in range(rows)])


def send(value, k, flip, rows, feats):
    pairs = [
        (r * feats + i, (r ^ flip) * feats + (i + k) % feats)
        for r in range(rows)
        for i in range(feats)
    ]
    return lax.ppermute(value, ("rows", "feat"), pairs)


def after(value, *others):
    return lax.optimization_barrier((value, *others))[0]


def behind(k, feats, size):
    return pl.multiple_of(lax.rem(lax.axis_index("feat") - k + feats, feats) * size, size)


def pack_kernel(feature, grad_output, ws, wn, bias, out, parts, sems):
    hid, every = ws.shape
    width = feature.shape[1]
    copies = []
    for source, low, size in (
        (feature, 0, width),
        (grad_output, width, width),
        (ws, 2 * width, every),
        (wn, 2 * width + every, every),
        (parts, 2 * width + 2 * every, 128),
    ):
        place = out.at[:, pl.ds(low, size)]
        copies.append(pltpu.make_async_copy(source, place, sems.at[len(copies)]))
    line = lax.broadcasted_iota(jnp.int32, (hid, hid), 0)
    lane = lax.broadcasted_iota(jnp.int32, (hid, hid), 1)
    column = jnp.sum(jnp.where(line == lane, bias[...], 0.0), axis=1, keepdims=True)
    high = column.astype(jnp.bfloat16).astype(jnp.float32)
    middle = (column - high).astype(jnp.bfloat16).astype(jnp.float32)
    low = column - high - middle
    at = lax.broadcasted_iota(jnp.int32, (hid, 128), 1)
    value = jnp.where(at == 0, high, jnp.where(at == 1, middle, jnp.where(at == 2, low, 0.0)))
    parts[...] = value.astype(jnp.bfloat16)
    for copy in copies:
        copy.start()
    for copy in copies:
        copy.wait()


def prepare_kernel(feats, *refs):
    packs, (turned, cot_all, base), (weights, bias, x_all) = refs[:feats], refs[feats:-3], refs[-3:]
    hid, width = packs[0].shape[0], x_all.shape[1]
    every = feats * hid
    for k in range(feats):
        at = pl.ds(behind(k, feats, hid), hid)
        pack = packs[k]
        x_all[at] = pack[:, :width]
        cot_all[at] = pack[:, width : 2 * width]
        weights[at] = pack[:, 2 * width : 2 * width + 2 * every].astype(jnp.float32)
        parts = pack[:, 2 * width + 2 * every :].astype(jnp.float32)
        bias[at] = jnp.sum(parts, axis=1, keepdims=True)
    own = weights[:, :every].T.astype(jnp.bfloat16)
    turned[...] = weights[:, every:].T.astype(jnp.bfloat16)
    chunk = min(width, 512)
    for c in range(0, width, chunk):
        lane = pl.ds(c, chunk)
        base[:, lane] = product(own, x_all[:, lane]) + bias[...]


def table_kernel(cols, table, counts):
    blocks, per_block = cols.shape
    base = blocks * per_block
    groups = counts.shape[0]

    def clear(i, carry):
        counts[i] = 0
        for s in range(CAP):
            table[base + i * CAP + s] = -1
        return carry

    lax.fori_loop(0, groups, clear, 0)

    def step(block, carry):
        for t in range(per_block):
            col = cols[block, t]
            group = col // blocks
            seen = counts[group]
            counts[group] = seen + 1
            index = block * per_block + t
            table[index] = col
            table[base + group * CAP + seen] = index * 256 + (col - group * blocks)
        return carry

    lax.fori_loop(0, blocks, step, 0)


def load_kernel(source, out, sem):
    copy = pltpu.make_async_copy(source, out, sem)
    copy.start()
    copy.wait()


def aggregate_kernel(wanted, rows, table, tiles, *refs):
    count = len(wanted)
    blocks, per_block, tile, unused = tiles.shape
    half = refs[0].shape[0]
    sources, (out, inverse, held, sems) = refs[:count], refs[count:]
    row = lax.axis_index("rows")
    copies = []
    for n, (offset, side) in enumerate(wanted):
        place = ring_row(row, offset, rows)
        if side:
            place = place + 1 - 2 * lax.rem(place, 2)
        copies.append(pltpu.make_async_copy(sources[n], held.at[place], sems.at[n]))
    for copy in copies:
        copy.start()
    for copy in copies:
        copy.wait()
    ones = jnp.ones((16, 2 * tile), jnp.bfloat16)

    def step(block, carry):
        total = None
        for t in range(0, per_block, 2):
            left, right = [], []
            for u in (t, t + 1):
                col = table[block * per_block + u]
                source = col // blocks
                at = pl.multiple_of((col - source * blocks) * tile, tile)
                left.append(held[source, :, pl.ds(at, tile)])
                right.append(tiles[block, u])
            term = product(
                jnp.concatenate([jnp.concatenate(left, axis=1), ones], axis=0),
                jnp.concatenate(right, axis=1),
                LAST,
            )
            total = term if total is None else total + term
        factor = 1.0 / total[half : half + 1]
        lane = pl.ds(pl.multiple_of(block * tile, tile), tile)
        out[:, lane] = (total[:half] * factor).astype(jnp.bfloat16)
        inverse[:, lane] = factor
        return carry

    lax.fori_loop(0, blocks, step, 0, unroll=8)


def middle_kernel(feats, turned, wn, inverse, base, cot, *refs):
    near, far, refs = refs[:feats], refs[feats : 2 * feats], refs[2 * feats :]
    act, grad, scaled, agg_own, agg, value = refs
    hid, width = act.shape
    half = hid // 2
    core = lax.rem(lax.axis_index("rows"), 2)
    for k in range(feats):
        first = behind(k, feats, hid)
        agg[pl.ds(pl.multiple_of(first + core * half, half), half)] = near[k][...]
        agg[pl.ds(pl.multiple_of(first + (1 - core) * half, half), half)] = far[k][...]
    own = pl.ds(behind(0, feats, hid), hid)
    agg_own[...] = agg[own]
    chunk = min(width, 256)
    for c in range(0, width, chunk):
        lane = pl.ds(c, chunk)
        pre = product(turned[...], agg[:, lane]) + base[:, lane]
        slope = jnp.exp(jnp.minimum(pre, 0.0))
        grad[:, lane] = (cot[:, lane].astype(jnp.float32) * slope).astype(jnp.bfloat16)
        value[...] = jnp.where(pre > 0, pre, slope - 1.0)
        back = product(wn[...], grad[:, lane])
        scaled[:, lane] = (back * inverse[:, lane]).astype(jnp.bfloat16)
        act[:, lane] = value[own].astype(jnp.bfloat16)


def own_quarter():
    return 2 * lax.rem(lax.axis_index("rows"), 2)


def turned_quarter(mine, index):
    turned = index // 2 + mine // 2 - 2 * (index // 2) * (mine // 2)
    return 2 * turned + index % 2


def weights_kernel(ws, x_own, agg_own, grad, self_own, sums):
    hid, every = ws.shape
    g = grad[...]
    self_own[...] = product(ws[...], g)
    wide = every // 2
    mine = own_quarter()
    values = [product(x_own[...], g, LAST), product(agg_own[...], g, LAST)]
    total = product(jnp.ones((8, g.shape[1]), jnp.bfloat16), g, LAST)
    for quarter in range(4):
        slot = turned_quarter(mine, quarter)
        lane = slice(quarter % 2 * wide, (quarter % 2 + 1) * wide)
        sums[slot, :hid] = values[quarter // 2][:, lane]
        sums[slot, hid:] = total[:, lane]


def collect_kernel(pair, pair_far, grad_self, grad_neigh, sums):
    hid, every = grad_self.shape
    wide = every // 2
    mine = own_quarter()
    for slot in range(4):
        value = (pair, pair_far)[slot // 2][slot % 2]
        quarter = turned_quarter(mine, slot)
        for q, out in enumerate((grad_self, grad_self, grad_neigh, grad_neigh)):

            @pl.when(quarter == q)
            def _():
                lane = slice(q % 2 * wide, (q % 2 + 1) * wide)
                out[:, lane] = value[:hid]
                if q < 2:
                    sums[:, lane] = value[hid:]


def arrange_kernel(own, other, held):
    hid, tile = held.shape[2:]
    blocks = held.shape[1] - 1
    for side, source in enumerate((own, other)):
        held[side, blocks] = jnp.zeros((hid, tile), jnp.bfloat16)
        for block in range(blocks):
            held[side, block] = source[:, block * tile : (block + 1) * tile]


def spread_kernel(plan, table, table_pair, adj, pair, held, *refs):
    rows, offsets, kinds = plan
    results, total = refs[:-1], refs[-1]
    blocks, per_block, tile, unused = adj.shape
    half = total.shape[0] // 2
    row = lax.axis_index("rows")
    firsts = [blocks * per_block + ring_row(row, offset, rows) * CAP for offset in offsets]
    for d in range(len(offsets)):
        total[...] = jnp.zeros_like(total)
        for side, (slots, tiles) in enumerate(((table, adj), (table_pair, pair))):
            for s0 in range(0, CAP, 4):
                terms = []
                for s in range(s0, s0 + 4):
                    entry = slots[firsts[d] + s]
                    index = jnp.maximum(entry, 0) // 256
                    block = index // per_block
                    place = jnp.where(entry < 0, blocks, block)
                    lane = lax.rem(jnp.maximum(entry, 0), 256) * tile
                    term = product(held[side, place], tiles[block, index - block * per_block])
                    terms.append((pl.multiple_of(lane, tile), term))
                for lane, term in terms:
                    total[:, pl.ds(lane, tile)] += term
        for part in range(2):
            value = total[part * half : (part + 1) * half]
            results[2 * d + part][...] = value.astype(kinds[2 * d + part])


def join_kernel(arrived, mine, out):
    out[...] = (arrived[...].astype(jnp.float32) + mine[...]).astype(jnp.bfloat16)


def finish_kernel(own, base_low, base_high, a_low, b_low, a_high, b_high, out):
    half = a_low.shape[0]
    for part, (base, a, b) in enumerate(((base_low, a_low, b_low), (base_high, a_high, b_high))):
        lines = slice(part * half, (part + 1) * half)
        value = own[lines] + base[...] + a[...].astype(jnp.float32)
        out[lines] = (value + b[...].astype(jnp.float32)).astype(jnp.bfloat16)


def call(kernel, name, outs, ins, out_specs, scratch, mib, flops, moved, *args):
    return pl.pallas_call(
        kernel,
        out_shape=[jax.ShapeDtypeStruct(shape, kind) for shape, kind in outs],
        in_specs=ins,
        out_specs=out_specs,
        scratch_shapes=scratch,
        compiler_params=params(mib),
        cost_estimate=cost(flops, moved),
        name=name,
    )(*args)


def shards(rows, feats, features, adjacency, tile_cols, self_weight, neigh_weight, bias_vector, grad_output):
    hid, width = features.shape
    blocks, per_block, tile, unused = adjacency.shape
    half = hid // 2
    every = hid * feats
    top = rows // 4
    narrow, wide = jnp.bfloat16, jnp.float32
    bind = functools.partial

    core = lax.rem(lax.axis_index("rows"), 2)
    mine = lax.dynamic_slice_in_dim(features, core * half, half)
    away = lax.dynamic_slice_in_dim(features, (1 - core) * half, half)
    sources, wanted = [mine], [(0, 0)]
    up, down = [mine, away], [mine, away]
    (table,) = call(
        table_kernel, "table", [((tile_cols.size + rows * CAP,), jnp.int32)], [SMEM], [SMEM],
        [pltpu.SMEM((rows,), jnp.int32)], 2, 0, 8 * rows * CAP, tile_cols,
    )
    packed = 2 * width + 2 * every + 128
    (pack,) = call(
        pack_kernel, "pack", [((hid, packed), narrow)], [HBM] * 4 + [VMEM], [VMEM],
        [pltpu.VMEM((hid, 128), narrow), pltpu.SemaphoreType.DMA((5,))], 4, 0,
        4 * hid * packed,
        features, grad_output, self_weight, neigh_weight, bias_vector.reshape(1, hid),
    )

    def load(value):
        (out,) = call(
            load_kernel, "load", [(adjacency.shape, narrow)], [HBM], [VMEM],
            [pltpu.SemaphoreType.DMA], 2, 0, 4 * adjacency.size, value,
        )
        return out

    pair, tiles = swap(adjacency, rows), load(adjacency)
    for step in range(1, top + 1):
        if step == 2:
            up, down, pair, pack, tiles, table = lax.optimization_barrier(
                (up, down, pair, pack, tiles, table)
            )
            packs = [pack] + [send(pack, k, 0, rows, feats) for k in range(1, feats)]
        if step == 3:
            pair = load(pair)
            up = [after(value, pair) for value in up]
            down = [after(value, pair) for value in down]
        if step == top:
            table_pair = swap(after(table, up[0], down[0]), rows)
            sources.append(swap(after(away, up[0], down[0]), rows))
            wanted.append((0, 1))
        for side in range(2):
            flip = side if step == 1 else 0
            forward, backward = ring_pairs(rows, 1, flip), ring_pairs(rows, -1, flip)
            if step < top or side == 0:
                up[side] = lax.ppermute(up[side], "rows", forward)
                sources.append(up[side])
                wanted.append((-step, side))
            if step < top or side == 1:
                down[side] = lax.ppermute(down[side], "rows", backward)
                sources.append(down[side])
                wanted.append((step, side))

    def aggregate(columns, values):
        return call(
            bind(aggregate_kernel, tuple(wanted), rows), "aggregate",
            [((half, width), narrow), ((1, width), wide)],
            [SMEM, VMEM] + [HBM] * len(sources), [VMEM] * 2,
            [pltpu.VMEM((rows, half, width), narrow), pltpu.SemaphoreType.DMA((len(sources),))],
            11, hid * adjacency.size, 2 * adjacency.size + rows * hid * width,
            columns, values, *sources,
        )

    value, unused_inverse = aggregate(table_pair, pair)
    far = [send(value, k, 1, rows, feats) for k in reversed(range(feats))][::-1]
    value, inverse = aggregate(table, tiles)
    near = [value] + [send(value, k, 0, rows, feats) for k in range(1, feats)]

    turned, cot_all, base = call(
        bind(prepare_kernel, feats), "prepare",
        [((every, every), narrow), ((every, width), narrow), ((every, width), wide)],
        [VMEM] * feats, [VMEM] * 3,
        [
            pltpu.VMEM((every, 2 * every), wide),
            pltpu.VMEM((every, 1), wide),
            pltpu.VMEM((every, width), narrow),
        ],
        8, 2 * every * every * width, 4 * every * packed, *packs,
    )
    activation, grad, scaled, agg_own = call(
        bind(middle_kernel, feats), "middle",
        [((hid, width), narrow), ((every, width), narrow)] + [((hid, width), narrow)] * 2,
        [VMEM] * (5 + 2 * feats), [VMEM] * 4,
        [pltpu.VMEM((every, width), narrow), pltpu.VMEM((every, min(width, 256)), wide)], 9,
        3 * every * every * width, 14 * every * width,
        turned, neigh_weight, inverse, base, cot_all, *near, *far,
    )
    scaled_pair = swap(scaled, rows)
    self_own, sums = call(
        weights_kernel, "weights", [((hid, width), wide), ((4, hid + 8, every // 2), wide)],
        [VMEM] * 4, [VMEM] * 2, [], 6, 6 * hid * every * width, 10 * every * width,
        self_weight, features, agg_own, grad,
    )
    (held,) = call(
        arrange_kernel, "arrange", [((2, blocks + 1, hid, tile), narrow)],
        [VMEM] * 2, [VMEM], [], 4, 0, 8 * hid * width, scaled, scaled_pair,
    )

    def spread(offsets, kinds):
        n = 2 * CAP * len(offsets)
        return call(
            bind(spread_kernel, (rows, offsets, kinds)), "spread",
            [((half, width), kind) for kind in kinds],
            [SMEM] * 2 + [VMEM] * 3, [VMEM] * len(kinds), [pltpu.VMEM((hid, width), wide)],
            9, 2 * n * hid * tile * tile, 8 * hid * width * len(offsets),
            table, table_pair, tiles, pair, held,
        )

    def joined(arrived, mine):
        if arrived is None:
            return mine
        (out,) = call(
            join_kernel, "join", [((half, width), narrow)], [VMEM] * 2, [VMEM], [], 2,
            0, 4 * hid * width, arrived, mine,
        )
        return out

    total = sums[:2] + swap(after(sums[2:], scaled_pair), rows, 1)
    arriving, bit, sends = swap(total, rows, 2), 4, 0

    def ring(value, pairs):
        nonlocal total, arriving, bit, sends
        sends += 1
        if sends >= 6 and sends % 4 == 2 and arriving is not None:
            if sends == 6:
                total = total + arriving
                value = after(value, total)
            else:
                total = total + after(arriving, value)
            arriving = None
            if bit < rows:
                arriving = swap(total, rows, bit)
            bit *= 2
        return lax.ppermute(value, "rows", pairs)

    up, down = [None, None], [None, None]
    forward, backward = ring_pairs(rows, 1), ring_pairs(rows, -1)
    for level in range(top, 0, -1):
        if level == top:
            low, high = spread((top,), (narrow, narrow))
            up[0] = ring(low, forward)
            down[1] = ring(high, backward)
            continue
        kinds = tuple(narrow if arrived is None else wide for arrived in up + down)
        offsets = (level, -level)
        if level == 1:
            offsets, kinds = (1, -1, 0), kinds + (wide, wide)
        mine = spread(offsets, kinds)
        for i in (1, 0):
            flow = 1 - i
            up[i] = ring(joined(up[i], mine[i]), forward)
            down[flow] = ring(joined(down[flow], mine[2 + flow]), backward)
    far = swap(total, rows, 1)
    grad_self, grad_neigh, total = call(
        collect_kernel, "collect",
        [((hid, every), wide), ((hid, every), wide), ((8, every), wide)],
        [VMEM] * 2, [VMEM] * 3, [], 4, 0, 16 * hid * every, total, far,
    )
    grad_bias = lax.dynamic_slice_in_dim(total[0], lax.axis_index("feat") * hid, hid)
    (grad_features,) = call(
        finish_kernel, "finish", [((hid, width), narrow)], [VMEM] * 7, [VMEM], [], 6, 0,
        8 * hid * width, self_own, mine[4], mine[5], up[0], down[0], up[1], down[1],
    )
    return (activation, grad_features, grad_self, grad_neigh, grad_bias)


def solution(mesh):
    in_specs = (
        P("feat", "rows"),
        P("rows", None, None, None),
        P("rows", None),
        P("feat", None),
        P("feat", None),
        P("feat"),
        P("feat", "rows"),
    )
    out_specs = (P("feat", "rows"), P("feat", "rows"), P("feat", None), P("feat", None), P("feat"))
    body = functools.partial(shards, mesh.shape["rows"], mesh.shape["feat"])
    return jax.shard_map(body, mesh=mesh, in_specs=in_specs, out_specs=out_specs, check_vma=False)
```

```python
import functools

import jax
import jax.numpy as jnp
from jax import lax
from jax.experimental import pallas as pl
from jax.experimental.pallas import tpu as pltpu
from jax.sharding import PartitionSpec as P

CAP = 12
MIB = 1024 * 1024
HBM = pl.BlockSpec(memory_space=pltpu.HBM)
VMEM = pl.BlockSpec(memory_space=pltpu.VMEM)
SMEM = pl.BlockSpec(memory_space=pltpu.SMEM)
LAST = (((1,), (1,)), ((), ()))


def params(mib):
    return pltpu.CompilerParams(vmem_limit_bytes=mib * MIB)


def cost(flops, moved):
    return pl.CostEstimate(flops=flops, bytes_accessed=moved, transcendentals=0)


def product(left, right, dims=(((1,), (0,)), ((), ()))):
    return lax.dot_general(left, right, dims, preferred_element_type=jnp.float32)


def ring_pairs(rows, step, flip=0):
    levels, chips = rows // 4, rows // 2
    order = [2 * z for z in range(levels)] + [2 * z + 1 for z in reversed(range(levels))]
    return [
        (2 * order[p] + core, 2 * order[(p + step) % chips] + (core ^ flip))
        for p in range(chips)
        for core in range(2)
    ]


def ring_row(row, offset, rows):
    levels, chips = rows // 4, rows // 2
    z, x, core = row // 4, lax.rem(row // 2, 2), lax.rem(row, 2)
    target = lax.rem(jnp.where(x == 0, z, chips - 1 - z) + (offset + chips), chips)
    low = target < levels
    return 2 * jnp.where(low, 2 * target, 2 * (chips - 1 - target) + 1) + core


def swap(value, rows, bit=1):
    return lax.ppermute(value, "rows", [(r, r ^ bit) for r in range(rows)])


def send(value, k, flip, rows, feats):
    pairs = [
        (r * feats + i, (r ^ flip) * feats + (i + k) % feats)
        for r in range(rows)
        for i in range(feats)
    ]
    return lax.ppermute(value, ("rows", "feat"), pairs)


def after(value, *others):
    return lax.optimization_barrier((value, *others))[0]


def behind(k, feats, size):
    return pl.multiple_of(lax.rem(lax.axis_index("feat") - k + feats, feats) * size, size)


def pack_kernel(feature, grad_output, ws, wn, bias, out, parts, sems):
    hid, every = ws.shape
    width = feature.shape[1]
    copies = []
    for source, low, size in (
        (feature, 0, width),
        (grad_output, width, width),
        (ws, 2 * width, every),
        (wn, 2 * width + every, every),
        (parts, 2 * width + 2 * every, 128),
    ):
        place = out.at[:, pl.ds(low, size)]
        copies.append(pltpu.make_async_copy(source, place, sems.at[len(copies)]))
    line = lax.broadcasted_iota(jnp.int32, (hid, hid), 0)
    lane = lax.broadcasted_iota(jnp.int32, (hid, hid), 1)
    column = jnp.sum(jnp.where(line == lane, bias[...], 0.0), axis=1, keepdims=True)
    high = column.astype(jnp.bfloat16).astype(jnp.float32)
    middle = (column - high).astype(jnp.bfloat16).astype(jnp.float32)
    low = column - high - middle
    at = lax.broadcasted_iota(jnp.int32, (hid, 128), 1)
    value = jnp.where(at == 0, high, jnp.where(at == 1, middle, jnp.where(at == 2, low, 0.0)))
    parts[...] = value.astype(jnp.bfloat16)
    for copy in copies:
        copy.start()
    for copy in copies:
        copy.wait()


def prepare_kernel(feats, *refs):
    packs, (turned, cot_all, base), (weights, bias, x_all) = refs[:feats], refs[feats:-3], refs[-3:]
    hid, width = packs[0].shape[0], x_all.shape[1]
    every = feats * hid
    for k in range(feats):
        at = pl.ds(behind(k, feats, hid), hid)
        pack = packs[k]
        x_all[at] = pack[:, :width]
        cot_all[at] = pack[:, width : 2 * width]
        weights[at] = pack[:, 2 * width : 2 * width + 2 * every].astype(jnp.float32)
        parts = pack[:, 2 * width + 2 * every :].astype(jnp.float32)
        bias[at] = jnp.sum(parts, axis=1, keepdims=True)
    own = weights[:, :every].T.astype(jnp.bfloat16)
    turned[...] = weights[:, every:].T.astype(jnp.bfloat16)
    chunk = min(width, 512)
    for c in range(0, width, chunk):
        lane = pl.ds(c, chunk)
        base[:, lane] = product(own, x_all[:, lane]) + bias[...]


def table_kernel(cols, table, counts):
    blocks, per_block = cols.shape
    base = blocks * per_block
    groups = counts.shape[0]

    def clear(i, carry):
        counts[i] = 0
        for s in range(CAP):
            table[base + i * CAP + s] = -1
        return carry

    lax.fori_loop(0, groups, clear, 0)

    def step(block, carry):
        for t in range(per_block):
            col = cols[block, t]
            group = col // blocks
            seen = counts[group]
            counts[group] = seen + 1
            index = block * per_block + t
            table[index] = col
            table[base + group * CAP + seen] = index * 256 + (col - group * blocks)
        return carry

    lax.fori_loop(0, blocks, step, 0)


def load_kernel(source, out, sem):
    copy = pltpu.make_async_copy(source, out, sem)
    copy.start()
    copy.wait()


def aggregate_kernel(wanted, rows, table, tiles, *refs):
    count = len(wanted)
    blocks, per_block, tile, unused = tiles.shape
    half = refs[0].shape[0]
    sources, (out, inverse, held, sems) = refs[:count], refs[count:]
    row = lax.axis_index("rows")
    copies = []
    for n, (offset, side) in enumerate(wanted):
        place = ring_row(row, offset, rows)
        if side:
            place = place + 1 - 2 * lax.rem(place, 2)
        copies.append(pltpu.make_async_copy(sources[n], held.at[place], sems.at[n]))
    for copy in copies:
        copy.start()
    for copy in copies:
        copy.wait()
    ones = jnp.ones((16, 2 * tile), jnp.bfloat16)

    def step(block, carry):
        total = None
        for t in range(0, per_block, 2):
            left, right = [], []
            for u in (t, t + 1):
                col = table[block * per_block + u]
                source = col // blocks
                at = pl.multiple_of((col - source * blocks) * tile, tile)
                left.append(held[source, :, pl.ds(at, tile)])
                right.append(tiles[block, u])
            term = product(
                jnp.concatenate([jnp.concatenate(left, axis=1), ones], axis=0),
                jnp.concatenate(right, axis=1),
                LAST,
            )
            total = term if total is None else total + term
        factor = 1.0 / total[half : half + 1]
        lane = pl.ds(pl.multiple_of(block * tile, tile), tile)
        out[:, lane] = (total[:half] * factor).astype(jnp.bfloat16)
        inverse[:, lane] = factor
        return carry

    lax.fori_loop(0, blocks, step, 0, unroll=4)


def middle_kernel(feats, turned, wn, inverse, base, cot, *refs):
    near, far, refs = refs[:feats], refs[feats : 2 * feats], refs[2 * feats :]
    act, grad, scaled, agg_own, agg = refs
    hid, width = act.shape
    half = hid // 2
    core = lax.rem(lax.axis_index("rows"), 2)
    for k in range(feats):
        first = behind(k, feats, hid)
        agg[pl.ds(pl.multiple_of(first + core * half, half), half)] = near[k][...]
        agg[pl.ds(pl.multiple_of(first + (1 - core) * half, half), half)] = far[k][...]
    own = pl.ds(behind(0, feats, hid), hid)
    agg_own[...] = agg[own]
    chunk = min(width, 256)
    for c in range(0, width, chunk):
        lane = pl.ds(c, chunk)
        pre = product(turned[...], agg[:, lane]) + base[:, lane]
        slope = jnp.exp(jnp.minimum(pre, 0.0))
        g = (cot[:, lane].astype(jnp.float32) * slope).astype(jnp.bfloat16)
        grad[:, lane] = g
        back = product(wn[...], g)
        scaled[:, lane] = (back * inverse[:, lane]).astype(jnp.bfloat16)
        mine, mine_slope = pre[:hid], slope[:hid]
        for k in range(1, feats):
            here = lax.axis_index("feat") == k
            mine = jnp.where(here, pre[k * hid : (k + 1) * hid], mine)
            mine_slope = jnp.where(here, slope[k * hid : (k + 1) * hid], mine_slope)
        act[:, lane] = jnp.where(mine > 0, mine, mine_slope - 1.0).astype(jnp.bfloat16)


def own_quarter():
    return 2 * lax.rem(lax.axis_index("rows"), 2)


def turned_quarter(mine, index):
    turned = index // 2 + mine // 2 - 2 * (index // 2) * (mine // 2)
    return 2 * turned + index % 2


def weights_kernel(ws, x_own, agg_own, grad, self_own, sums):
    hid, every = ws.shape
    g = grad[...]
    self_own[...] = product(ws[...], g)
    wide = every // 2
    mine = own_quarter()
    values = [product(x_own[...], g, LAST), product(agg_own[...], g, LAST)]
    total = product(jnp.ones((8, g.shape[1]), jnp.bfloat16), g, LAST)
    for quarter in range(4):
        slot = turned_quarter(mine, quarter)
        lane = slice(quarter % 2 * wide, (quarter % 2 + 1) * wide)
        sums[slot, :hid] = values[quarter // 2][:, lane]
        sums[slot, hid:] = total[:, lane]


def collect_kernel(pair, pair_far, grad_self, grad_neigh, sums):
    hid, every = grad_self.shape
    wide = every // 2
    mine = own_quarter()
    for slot in range(4):
        value = (pair, pair_far)[slot // 2][slot % 2]
        quarter = turned_quarter(mine, slot)
        for q, out in enumerate((grad_self, grad_self, grad_neigh, grad_neigh)):

            @pl.when(quarter == q)
            def _():
                lane = slice(q % 2 * wide, (q % 2 + 1) * wide)
                out[:, lane] = value[:hid]
                if q < 2:
                    sums[:, lane] = value[hid:]


def arrange_kernel(own, other, held):
    hid, tile = held.shape[2:]
    blocks = held.shape[1] - 1
    for side, source in enumerate((own, other)):
        held[side, blocks] = jnp.zeros((hid, tile), jnp.bfloat16)
        for block in range(blocks):
            held[side, block] = source[:, block * tile : (block + 1) * tile]


def spread_kernel(plan, table, table_pair, adj, pair, held, *refs):
    rows, offsets, kinds = plan
    results, total = refs[:-1], refs[-1]
    blocks, per_block, tile, unused = adj.shape
    half = total.shape[0] // 2
    row = lax.axis_index("rows")
    firsts = [blocks * per_block + ring_row(row, offset, rows) * CAP for offset in offsets]
    for d in range(len(offsets)):
        total[...] = jnp.zeros_like(total)
        for side, (slots, tiles) in enumerate(((table, adj), (table_pair, pair))):
            for s0 in range(0, CAP, 4):
                terms = []
                for s in range(s0, s0 + 4):
                    entry = slots[firsts[d] + s]
                    index = jnp.maximum(entry, 0) // 256
                    block = index // per_block
                    place = jnp.where(entry < 0, blocks, block)
                    lane = lax.rem(jnp.maximum(entry, 0), 256) * tile
                    term = product(held[side, place], tiles[block, index - block * per_block])
                    terms.append((pl.multiple_of(lane, tile), term))
                for lane, term in terms:
                    total[:, pl.ds(lane, tile)] += term
        for part in range(2):
            value = total[part * half : (part + 1) * half]
            results[2 * d + part][...] = value.astype(kinds[2 * d + part])


def join_kernel(arrived, mine, out):
    out[...] = (arrived[...].astype(jnp.float32) + mine[...]).astype(jnp.bfloat16)


def finish_kernel(own, base_low, base_high, a_low, b_low, a_high, b_high, out):
    half = a_low.shape[0]
    for part, (base, a, b) in enumerate(((base_low, a_low, b_low), (base_high, a_high, b_high))):
        lines = slice(part * half, (part + 1) * half)
        value = own[lines] + base[...] + a[...].astype(jnp.float32)
        out[lines] = (value + b[...].astype(jnp.float32)).astype(jnp.bfloat16)


def call(kernel, name, outs, ins, out_specs, scratch, mib, flops, moved, *args):
    return pl.pallas_call(
        kernel,
        out_shape=[jax.ShapeDtypeStruct(shape, kind) for shape, kind in outs],
        in_specs=ins,
        out_specs=out_specs,
        scratch_shapes=scratch,
        compiler_params=params(mib),
        cost_estimate=cost(flops, moved),
        name=name,
    )(*args)


def shards(rows, feats, features, adjacency, tile_cols, self_weight, neigh_weight, bias_vector, grad_output):
    hid, width = features.shape
    blocks, per_block, tile, unused = adjacency.shape
    half = hid // 2
    every = hid * feats
    top = rows // 4
    narrow, wide = jnp.bfloat16, jnp.float32
    bind = functools.partial

    core = lax.rem(lax.axis_index("rows"), 2)
    mine = lax.dynamic_slice_in_dim(features, core * half, half)
    away = lax.dynamic_slice_in_dim(features, (1 - core) * half, half)
    sources, wanted = [mine], [(0, 0)]
    up, down = [mine, away], [mine, away]
    (table,) = call(
        table_kernel, "table", [((tile_cols.size + rows * CAP,), jnp.int32)], [SMEM], [SMEM],
        [pltpu.SMEM((rows,), jnp.int32)], 2, 0, 8 * rows * CAP, tile_cols,
    )
    packed = 2 * width + 2 * every + 128
    (pack,) = call(
        pack_kernel, "pack", [((hid, packed), narrow)], [HBM] * 4 + [VMEM], [VMEM],
        [pltpu.VMEM((hid, 128), narrow), pltpu.SemaphoreType.DMA((5,))], 4, 0,
        4 * hid * packed,
        features, grad_output, self_weight, neigh_weight, bias_vector.reshape(1, hid),
    )

    def load(value):
        (out,) = call(
            load_kernel, "load", [(adjacency.shape, narrow)], [HBM], [VMEM],
            [pltpu.SemaphoreType.DMA], 2, 0, 4 * adjacency.size, value,
        )
        return out

    pair, tiles = swap(adjacency, rows), load(adjacency)
    for step in range(1, top + 1):
        if step == 2:
            up, down, pair, pack, tiles, table = lax.optimization_barrier(
                (up, down, pair, pack, tiles, table)
            )
            packs = [pack] + [send(pack, k, 0, rows, feats) for k in range(1, feats)]
        if step == 3:
            pair = load(pair)
            up = [after(value, pair) for value in up]
            down = [after(value, pair) for value in down]
        if step == top:
            table_pair = swap(after(table, up[0], down[0]), rows)
            sources.append(swap(after(away, up[0], down[0]), rows))
            wanted.append((0, 1))
        for side in range(2):
            flip = side if step == 1 else 0
            forward, backward = ring_pairs(rows, 1, flip), ring_pairs(rows, -1, flip)
            if step < top or side == 0:
                up[side] = lax.ppermute(up[side], "rows", forward)
                sources.append(up[side])
                wanted.append((-step, side))
            if step < top or side == 1:
                down[side] = lax.ppermute(down[side], "rows", backward)
                sources.append(down[side])
                wanted.append((step, side))

    def aggregate(columns, values):
        return call(
            bind(aggregate_kernel, tuple(wanted), rows), "aggregate",
            [((half, width), narrow), ((1, width), wide)],
            [SMEM, VMEM] + [HBM] * len(sources), [VMEM] * 2,
            [pltpu.VMEM((rows, half, width), narrow), pltpu.SemaphoreType.DMA((len(sources),))],
            11, hid * adjacency.size, 2 * adjacency.size + rows * hid * width,
            columns, values, *sources,
        )

    value, unused_inverse = aggregate(table_pair, pair)
    far = [send(value, k, 1, rows, feats) for k in reversed(range(feats))][::-1]
    value, inverse = aggregate(table, tiles)
    near = [value] + [send(value, k, 0, rows, feats) for k in range(1, feats)]

    turned, cot_all, base = call(
        bind(prepare_kernel, feats), "prepare",
        [((every, every), narrow), ((every, width), narrow), ((every, width), wide)],
        [VMEM] * feats, [VMEM] * 3,
        [
            pltpu.VMEM((every, 2 * every), wide),
            pltpu.VMEM((every, 1), wide),
            pltpu.VMEM((every, width), narrow),
        ],
        8, 2 * every * every * width, 4 * every * packed, *packs,
    )
    activation, grad, scaled, agg_own = call(
        bind(middle_kernel, feats), "middle",
        [((hid, width), narrow), ((every, width), narrow)] + [((hid, width), narrow)] * 2,
        [VMEM] * (5 + 2 * feats), [VMEM] * 4,
        [pltpu.VMEM((every, width), narrow)], 9,
        3 * every * every * width, 14 * every * width,
        turned, neigh_weight, inverse, base, cot_all, *near, *far,
    )
    scaled_pair = swap(scaled, rows)
    self_own, sums = call(
        weights_kernel, "weights", [((hid, width), wide), ((4, hid + 8, every // 2), wide)],
        [VMEM] * 4, [VMEM] * 2, [], 6, 6 * hid * every * width, 10 * every * width,
        self_weight, features, agg_own, grad,
    )
    (held,) = call(
        arrange_kernel, "arrange", [((2, blocks + 1, hid, tile), narrow)],
        [VMEM] * 2, [VMEM], [], 4, 0, 8 * hid * width, scaled, scaled_pair,
    )

    def spread(offsets, kinds):
        n = 2 * CAP * len(offsets)
        return call(
            bind(spread_kernel, (rows, offsets, kinds)), "spread",
            [((half, width), kind) for kind in kinds],
            [SMEM] * 2 + [VMEM] * 3, [VMEM] * len(kinds), [pltpu.VMEM((hid, width), wide)],
            9, 2 * n * hid * tile * tile, 8 * hid * width * len(offsets),
            table, table_pair, tiles, pair, held,
        )

    def joined(arrived, mine):
        if arrived is None:
            return mine
        (out,) = call(
            join_kernel, "join", [((half, width), narrow)], [VMEM] * 2, [VMEM], [], 3,
            0, 4 * hid * width, arrived, mine,
        )
        return out

    total = sums[:2] + swap(after(sums[2:], scaled_pair), rows, 1)
    arriving, bit, sends = swap(total, rows, 2), 4, 0

    def ring(value, pairs):
        nonlocal total, arriving, bit, sends
        sends += 1
        if sends >= 6 and sends % 4 == 2 and arriving is not None:
            if sends == 6:
                total = total + arriving
                value = after(value, total)
            else:
                total = total + after(arriving, value)
            arriving = None
            if bit < rows:
                arriving = swap(total, rows, bit)
            bit *= 2
        return lax.ppermute(value, "rows", pairs)

    up, down = [None, None], [None, None]
    forward, backward = ring_pairs(rows, 1), ring_pairs(rows, -1)
    for level in range(top, 0, -1):
        if level == top:
            low, high = spread((top,), (narrow, narrow))
            up[0] = ring(low, forward)
            down[1] = ring(high, backward)
            continue
        kinds = tuple(narrow if arrived is None else wide for arrived in up + down)
        offsets = (level, -level)
        if level == 1:
            offsets, kinds = (1, -1, 0), kinds + (wide, wide)
        mine = spread(offsets, kinds)
        for i in (1, 0):
            flow = 1 - i
            up[i] = ring(joined(up[i], mine[i]), forward)
            down[flow] = ring(joined(down[flow], mine[2 + flow]), backward)
    far = swap(total, rows, 1)
    grad_self, grad_neigh, total = call(
        collect_kernel, "collect",
        [((hid, every), wide), ((hid, every), wide), ((8, every), wide)],
        [VMEM] * 2, [VMEM] * 3, [], 4, 0, 16 * hid * every, total, far,
    )
    grad_bias = lax.dynamic_slice_in_dim(total[0], lax.axis_index("feat") * hid, hid)
    (grad_features,) = call(
        finish_kernel, "finish", [((hid, width), narrow)], [VMEM] * 7, [VMEM], [], 6, 0,
        8 * hid * width, self_own, mine[4], mine[5], up[0], down[0], up[1], down[1],
    )
    return (activation, grad_features, grad_self, grad_neigh, grad_bias)


def solution(mesh):
    in_specs = (
        P("feat", "rows"),
        P("rows", None, None, None),
        P("rows", None),
        P("feat", None),
        P("feat", None),
        P("feat"),
        P("feat", "rows"),
    )
    out_specs = (P("feat", "rows"), P("feat", "rows"), P("feat", None), P("feat", None), P("feat"))
    body = functools.partial(shards, mesh.shape["rows"], mesh.shape["feat"])
    return jax.shard_map(body, mesh=mesh, in_specs=in_specs, out_specs=out_specs, check_vma=False)
```

```python
import functools

import jax
import jax.numpy as jnp
from jax import lax
from jax.experimental import pallas as pl
from jax.experimental.pallas import tpu as pltpu
from jax.sharding import PartitionSpec as P

CAP = 12
MIB = 1024 * 1024
HBM = pl.BlockSpec(memory_space=pltpu.HBM)
VMEM = pl.BlockSpec(memory_space=pltpu.VMEM)
SMEM = pl.BlockSpec(memory_space=pltpu.SMEM)
LAST = (((1,), (1,)), ((), ()))


def params(mib):
    return pltpu.CompilerParams(vmem_limit_bytes=mib * MIB)


def cost(flops, moved):
    return pl.CostEstimate(flops=flops, bytes_accessed=moved, transcendentals=0)


def product(left, right, dims=(((1,), (0,)), ((), ()))):
    return lax.dot_general(left, right, dims, preferred_element_type=jnp.float32)


def ring_pairs(rows, step, flip=0):
    levels, chips = rows // 4, rows // 2
    order = [2 * z for z in range(levels)] + [2 * z + 1 for z in reversed(range(levels))]
    return [
        (2 * order[p] + core, 2 * order[(p + step) % chips] + (core ^ flip))
        for p in range(chips)
        for core in range(2)
    ]


def ring_row(row, offset, rows):
    levels, chips = rows // 4, rows // 2
    z, x, core = row // 4, lax.rem(row // 2, 2), lax.rem(row, 2)
    target = lax.rem(jnp.where(x == 0, z, chips - 1 - z) + (offset + chips), chips)
    low = target < levels
    return 2 * jnp.where(low, 2 * target, 2 * (chips - 1 - target) + 1) + core


def swap(value, rows, bit=1):
    return lax.ppermute(value, "rows", [(r, r ^ bit) for r in range(rows)])


def send(value, k, flip, rows, feats):
    pairs = [
        (r * feats + i, (r ^ flip) * feats + (i + k) % feats)
        for r in range(rows)
        for i in range(feats)
    ]
    return lax.ppermute(value, ("rows", "feat"), pairs)


def after(value, *others):
    return lax.optimization_barrier((value, *others))[0]


def behind(k, feats, size):
    return pl.multiple_of(lax.rem(lax.axis_index("feat") - k + feats, feats) * size, size)


def pack_kernel(feature, grad_output, ws, wn, bias, out, parts, sems):
    hid, every = ws.shape
    width = feature.shape[1]
    copies = []
    for source, low, size in (
        (feature, 0, width),
        (grad_output, width, width),
        (ws, 2 * width, every),
        (wn, 2 * width + every, every),
        (parts, 2 * width + 2 * every, 128),
    ):
        place = out.at[:, pl.ds(low, size)]
        copies.append(pltpu.make_async_copy(source, place, sems.at[len(copies)]))
    line = lax.broadcasted_iota(jnp.int32, (hid, hid), 0)
    lane = lax.broadcasted_iota(jnp.int32, (hid, hid), 1)
    column = jnp.sum(jnp.where(line == lane, bias[...], 0.0), axis=1, keepdims=True)
    high = column.astype(jnp.bfloat16).astype(jnp.float32)
    middle = (column - high).astype(jnp.bfloat16).astype(jnp.float32)
    low = column - high - middle
    at = lax.broadcasted_iota(jnp.int32, (hid, 128), 1)
    value = jnp.where(at == 0, high, jnp.where(at == 1, middle, jnp.where(at == 2, low, 0.0)))
    parts[...] = value.astype(jnp.bfloat16)
    for copy in copies:
        copy.start()
    for copy in copies:
        copy.wait()


def prepare_kernel(feats, *refs):
    packs, (turned, cot_all, base), (weights, bias, x_all) = refs[:feats], refs[feats:-3], refs[-3:]
    hid, width = packs[0].shape[0], x_all.shape[1]
    every = feats * hid
    for k in range(feats):
        at = pl.ds(behind(k, feats, hid), hid)
        pack = packs[k]
        x_all[at] = pack[:, :width]
        cot_all[at] = pack[:, width : 2 * width]
        weights[at] = pack[:, 2 * width : 2 * width + 2 * every].astype(jnp.float32)
        parts = pack[:, 2 * width + 2 * every :].astype(jnp.float32)
        bias[at] = jnp.sum(parts, axis=1, keepdims=True)
    own = weights[:, :every].T.astype(jnp.bfloat16)
    turned[...] = weights[:, every:].T.astype(jnp.bfloat16)
    chunk = min(width, 512)
    for c in range(0, width, chunk):
        lane = pl.ds(c, chunk)
        base[:, lane] = product(own, x_all[:, lane]) + bias[...]


def table_kernel(cols, table, counts):
    blocks, per_block = cols.shape
    base = blocks * per_block
    groups = counts.shape[0]

    def clear(i, carry):
        counts[i] = 0
        for s in range(CAP):
            table[base + i * CAP + s] = -1
        return carry

    lax.fori_loop(0, groups, clear, 0)

    def step(block, carry):
        for t in range(per_block):
            col = cols[block, t]
            group = col // blocks
            seen = counts[group]
            counts[group] = seen + 1
            index = block * per_block + t
            table[index] = col
            table[base + group * CAP + seen] = index * 256 + (col - group * blocks)
        return carry

    lax.fori_loop(0, blocks, step, 0)


def load_kernel(source, out, sem):
    copy = pltpu.make_async_copy(source, out, sem)
    copy.start()
    copy.wait()


def aggregate_kernel(wanted, rows, table, tiles, *refs):
    count = len(wanted)
    blocks, per_block, tile, unused = tiles.shape
    half = refs[0].shape[0]
    sources, (out, inverse, held, sems) = refs[:count], refs[count:]
    row = lax.axis_index("rows")
    copies = []
    for n, (offset, side) in enumerate(wanted):
        place = ring_row(row, offset, rows)
        if side:
            place = place + 1 - 2 * lax.rem(place, 2)
        copies.append(pltpu.make_async_copy(sources[n], held.at[place], sems.at[n]))
    for copy in copies:
        copy.start()
    for copy in copies:
        copy.wait()
    ones = jnp.ones((16, 2 * tile), jnp.bfloat16)

    def step(block, carry):
        total = None
        for t in range(0, per_block, 2):
            left, right = [], []
            for u in (t, t + 1):
                col = table[block * per_block + u]
                source = col // blocks
                at = pl.multiple_of((col - source * blocks) * tile, tile)
                left.append(held[source, :, pl.ds(at, tile)])
                right.append(tiles[block, u])
            term = product(
                jnp.concatenate([jnp.concatenate(left, axis=1), ones], axis=0),
                jnp.concatenate(right, axis=1),
                LAST,
            )
            total = term if total is None else total + term
        factor = 1.0 / total[half : half + 1]
        lane = pl.ds(pl.multiple_of(block * tile, tile), tile)
        out[:, lane] = (total[:half] * factor).astype(jnp.bfloat16)
        inverse[:, lane] = factor
        return carry

    lax.fori_loop(0, blocks, step, 0, unroll=4)


def middle_kernel(feats, turned, wn, inverse, base, cot, *refs):
    near, far, refs = refs[:feats], refs[feats : 2 * feats], refs[2 * feats :]
    act, grad, scaled, agg_own, agg, value = refs
    hid, width = act.shape
    half = hid // 2
    core = lax.rem(lax.axis_index("rows"), 2)
    for k in range(feats):
        first = behind(k, feats, hid)
        agg[pl.ds(pl.multiple_of(first + core * half, half), half)] = near[k][...]
        agg[pl.ds(pl.multiple_of(first + (1 - core) * half, half), half)] = far[k][...]
    own = pl.ds(behind(0, feats, hid), hid)
    agg_own[...] = agg[own]
    chunk = min(width, 256)
    for c in range(0, width, chunk):
        lane = pl.ds(c, chunk)
        pre = product(turned[...], agg[:, lane]) + base[:, lane]
        slope = jnp.exp(jnp.minimum(pre, 0.0))
        grad[:, lane] = (cot[:, lane].astype(jnp.float32) * slope).astype(jnp.bfloat16)
        value[...] = jnp.where(pre > 0, pre, slope - 1.0)
        back = product(wn[...], grad[:, lane])
        scaled[:, lane] = (back * inverse[:, lane]).astype(jnp.bfloat16)
        act[:, lane] = value[own].astype(jnp.bfloat16)


def own_quarter():
    return 2 * lax.rem(lax.axis_index("rows"), 2)


def turned_quarter(mine, index):
    turned = index // 2 + mine // 2 - 2 * (index // 2) * (mine // 2)
    return 2 * turned + index % 2


def weights_kernel(ws, x_own, agg_own, grad, act, self_own, sums, act_out):
    act_out[...] = act[...]
    hid, every = ws.shape
    g = grad[...]
    self_own[...] = product(ws[...], g)
    wide = every // 2
    mine = own_quarter()
    values = [product(x_own[...], g, LAST), product(agg_own[...], g, LAST)]
    total = product(jnp.ones((8, g.shape[1]), jnp.bfloat16), g, LAST)
    for quarter in range(4):
        slot = turned_quarter(mine, quarter)
        lane = slice(quarter % 2 * wide, (quarter % 2 + 1) * wide)
        sums[slot, :hid] = values[quarter // 2][:, lane]
        sums[slot, hid:] = total[:, lane]


def collect_kernel(pair, pair_far, grad_self, grad_neigh, sums):
    hid, every = grad_self.shape
    wide = every // 2
    mine = own_quarter()
    for slot in range(4):
        value = (pair, pair_far)[slot // 2][slot % 2]
        quarter = turned_quarter(mine, slot)
        for q, out in enumerate((grad_self, grad_self, grad_neigh, grad_neigh)):

            @pl.when(quarter == q)
            def _():
                lane = slice(q % 2 * wide, (q % 2 + 1) * wide)
                out[:, lane] = value[:hid]
                if q < 2:
                    sums[:, lane] = value[hid:]


def arrange_kernel(own, other, held):
    hid, tile = held.shape[2:]
    blocks = held.shape[1] - 1
    for side, source in enumerate((own, other)):
        held[side, blocks] = jnp.zeros((hid, tile), jnp.bfloat16)
        for block in range(blocks):
            held[side, block] = source[:, block * tile : (block + 1) * tile]


def spread_kernel(plan, table, table_pair, adj, pair, held, *refs):
    rows, offsets, kinds = plan
    results, total = refs[:-1], refs[-1]
    blocks, per_block, tile, unused = adj.shape
    half = total.shape[0] // 2
    row = lax.axis_index("rows")
    firsts = [blocks * per_block + ring_row(row, offset, rows) * CAP for offset in offsets]
    for d in range(len(offsets)):
        total[...] = jnp.zeros_like(total)
        for side, (slots, tiles) in enumerate(((table, adj), (table_pair, pair))):
            for s0 in range(0, CAP, 4):
                terms = []
                for s in range(s0, s0 + 4):
                    entry = slots[firsts[d] + s]
                    index = jnp.maximum(entry, 0) // 256
                    block = index // per_block
                    place = jnp.where(entry < 0, blocks, block)
                    lane = lax.rem(jnp.maximum(entry, 0), 256) * tile
                    term = product(held[side, place], tiles[block, index - block * per_block])
                    terms.append((pl.multiple_of(lane, tile), term))
                for lane, term in terms:
                    total[:, pl.ds(lane, tile)] += term
        for part in range(2):
            value = total[part * half : (part + 1) * half]
            results[2 * d + part][...] = value.astype(kinds[2 * d + part])


def join_kernel(arrived, mine, out):
    out[...] = (arrived[...].astype(jnp.float32) + mine[...]).astype(jnp.bfloat16)


def finish_kernel(own, base_low, base_high, a_low, b_low, a_high, b_high, out):
    half = a_low.shape[0]
    for part, (base, a, b) in enumerate(((base_low, a_low, b_low), (base_high, a_high, b_high))):
        lines = slice(part * half, (part + 1) * half)
        value = own[lines] + base[...] + a[...].astype(jnp.float32)
        out[lines] = (value + b[...].astype(jnp.float32)).astype(jnp.bfloat16)


def call(kernel, name, outs, ins, out_specs, scratch, mib, flops, moved, *args):
    return pl.pallas_call(
        kernel,
        out_shape=[jax.ShapeDtypeStruct(shape, kind) for shape, kind in outs],
        in_specs=ins,
        out_specs=out_specs,
        scratch_shapes=scratch,
        compiler_params=params(mib),
        cost_estimate=cost(flops, moved),
        name=name,
    )(*args)


def shards(rows, feats, features, adjacency, tile_cols, self_weight, neigh_weight, bias_vector, grad_output):
    hid, width = features.shape
    blocks, per_block, tile, unused = adjacency.shape
    half = hid // 2
    every = hid * feats
    top = rows // 4
    narrow, wide = jnp.bfloat16, jnp.float32
    bind = functools.partial

    core = lax.rem(lax.axis_index("rows"), 2)
    mine = lax.dynamic_slice_in_dim(features, core * half, half)
    away = lax.dynamic_slice_in_dim(features, (1 - core) * half, half)
    sources, wanted = [mine], [(0, 0)]
    up, down = [mine, away], [mine, away]
    (table,) = call(
        table_kernel, "table", [((tile_cols.size + rows * CAP,), jnp.int32)], [SMEM], [SMEM],
        [pltpu.SMEM((rows,), jnp.int32)], 2, 0, 8 * rows * CAP, tile_cols,
    )
    packed = 2 * width + 2 * every + 128
    (pack,) = call(
        pack_kernel, "pack", [((hid, packed), narrow)], [HBM] * 4 + [VMEM], [VMEM],
        [pltpu.VMEM((hid, 128), narrow), pltpu.SemaphoreType.DMA((5,))], 4, 0,
        4 * hid * packed,
        features, grad_output, self_weight, neigh_weight, bias_vector.reshape(1, hid),
    )

    def load(value):
        (out,) = call(
            load_kernel, "load", [(adjacency.shape, narrow)], [HBM], [VMEM],
            [pltpu.SemaphoreType.DMA], 2, 0, 4 * adjacency.size, value,
        )
        return out

    pair, tiles = swap(adjacency, rows), load(adjacency)
    for step in range(1, top + 1):
        if step == 2:
            up, down, pair, pack, tiles, table = lax.optimization_barrier(
                (up, down, pair, pack, tiles, table)
            )
            packs = [pack] + [send(pack, k, 0, rows, feats) for k in range(1, feats)]
        if step == 3:
            pair = load(pair)
            up = [after(value, pair) for value in up]
            down = [after(value, pair) for value in down]
        if step == top:
            table_pair = swap(after(table, up[0], down[0]), rows)
            sources.append(swap(after(away, up[0], down[0]), rows))
            wanted.append((0, 1))
        for side in range(2):
            flip = side if step == 1 else 0
            forward, backward = ring_pairs(rows, 1, flip), ring_pairs(rows, -1, flip)
            if step < top or side == 0:
                up[side] = lax.ppermute(up[side], "rows", forward)
                sources.append(up[side])
                wanted.append((-step, side))
            if step < top or side == 1:
                down[side] = lax.ppermute(down[side], "rows", backward)
                sources.append(down[side])
                wanted.append((step, side))

    def aggregate(columns, values):
        return call(
            bind(aggregate_kernel, tuple(wanted), rows), "aggregate",
            [((half, width), narrow), ((1, width), wide)],
            [SMEM, VMEM] + [HBM] * len(sources), [VMEM] * 2,
            [pltpu.VMEM((rows, half, width), narrow), pltpu.SemaphoreType.DMA((len(sources),))],
            11, hid * adjacency.size, 2 * adjacency.size + rows * hid * width,
            columns, values, *sources,
        )

    value, unused_inverse = aggregate(table_pair, pair)
    far = [send(value, k, 1, rows, feats) for k in reversed(range(feats))][::-1]
    value, inverse = aggregate(table, tiles)
    near = [value] + [send(value, k, 0, rows, feats) for k in range(1, feats)]

    turned, cot_all, base = call(
        bind(prepare_kernel, feats), "prepare",
        [((every, every), narrow), ((every, width), narrow), ((every, width), wide)],
        [VMEM] * feats, [VMEM] * 3,
        [
            pltpu.VMEM((every, 2 * every), wide),
            pltpu.VMEM((every, 1), wide),
            pltpu.VMEM((every, width), narrow),
        ],
        8, 2 * every * every * width, 4 * every * packed, *packs,
    )
    act, grad, scaled, agg_own = call(
        bind(middle_kernel, feats), "middle",
        [((hid, width), narrow), ((every, width), narrow)] + [((hid, width), narrow)] * 2,
        [VMEM] * (5 + 2 * feats), [VMEM] * 4,
        [pltpu.VMEM((every, width), narrow), pltpu.VMEM((every, min(width, 256)), wide)], 9,
        3 * every * every * width, 14 * every * width,
        turned, neigh_weight, inverse, base, cot_all, *near, *far,
    )
    scaled_pair = swap(scaled, rows)
    self_own, sums, activation = call(
        weights_kernel, "weights", [((hid, width), wide), ((4, hid + 8, every // 2), wide), ((hid, width), narrow)],
        [VMEM] * 5, [VMEM] * 3, [], 7, 6 * hid * every * width, 10 * every * width,
        self_weight, features, agg_own, grad, act,
    )
    (held,) = call(
        arrange_kernel, "arrange", [((2, blocks + 1, hid, tile), narrow)],
        [VMEM] * 2, [VMEM], [], 4, 0, 8 * hid * width, scaled, scaled_pair,
    )

    def spread(offsets, kinds):
        n = 2 * CAP * len(offsets)
        return call(
            bind(spread_kernel, (rows, offsets, kinds)), "spread",
            [((half, width), kind) for kind in kinds],
            [SMEM] * 2 + [VMEM] * 3, [VMEM] * len(kinds), [pltpu.VMEM((hid, width), wide)],
            9, 2 * n * hid * tile * tile, 8 * hid * width * len(offsets),
            table, table_pair, tiles, pair, held,
        )

    def joined(arrived, mine):
        if arrived is None:
            return mine
        (out,) = call(
            join_kernel, "join", [((half, width), narrow)], [VMEM] * 2, [VMEM], [], 3,
            0, 4 * hid * width, arrived, mine,
        )
        return out

    total = sums[:2] + swap(after(sums[2:], scaled_pair), rows, 1)
    arriving, bit, sends = swap(total, rows, 2), 4, 0

    def ring(value, pairs):
        nonlocal total, arriving, bit, sends
        sends += 1
        if sends >= 6 and sends % 4 == 2 and arriving is not None:
            if sends == 6:
                total = total + arriving
                value = after(value, total)
            else:
                total = total + after(arriving, value)
            arriving = None
            if bit < rows:
                arriving = swap(total, rows, bit)
            bit *= 2
        return lax.ppermute(value, "rows", pairs)

    up, down = [None, None], [None, None]
    forward, backward = ring_pairs(rows, 1), ring_pairs(rows, -1)
    for level in range(top, 0, -1):
        if level == top:
            low, high = spread((top,), (narrow, narrow))
            up[0] = ring(low, forward)
            down[1] = ring(high, backward)
            continue
        kinds = tuple(narrow if arrived is None else wide for arrived in up + down)
        offsets = (level, -level)
        if level == 1:
            offsets, kinds = (1, -1, 0), kinds + (wide, wide)
        mine = spread(offsets, kinds)
        for i in (1, 0):
            flow = 1 - i
            up[i] = ring(joined(up[i], mine[i]), forward)
            down[flow] = ring(joined(down[flow], mine[2 + flow]), backward)
    far = swap(total, rows, 1)
    grad_self, grad_neigh, total = call(
        collect_kernel, "collect",
        [((hid, every), wide), ((hid, every), wide), ((8, every), wide)],
        [VMEM] * 2, [VMEM] * 3, [], 4, 0, 16 * hid * every, total, far,
    )
    grad_bias = lax.dynamic_slice_in_dim(total[0], lax.axis_index("feat") * hid, hid)
    (grad_features,) = call(
        finish_kernel, "finish", [((hid, width), narrow)], [VMEM] * 7, [VMEM], [], 6, 0,
        8 * hid * width, self_own, mine[4], mine[5], up[0], down[0], up[1], down[1],
    )
    return (activation, grad_features, grad_self, grad_neigh, grad_bias)


def solution(mesh):
    in_specs = (
        P("feat", "rows"),
        P("rows", None, None, None),
        P("rows", None),
        P("feat", None),
        P("feat", None),
        P("feat"),
        P("feat", "rows"),
    )
    out_specs = (P("feat", "rows"), P("feat", "rows"), P("feat", None), P("feat", None), P("feat"))
    body = functools.partial(shards, mesh.shape["rows"], mesh.shape["feat"])
    return jax.shard_map(body, mesh=mesh, in_specs=in_specs, out_specs=out_specs, check_vma=False)
```
